32 devices in a mesh: ens: 8 (over z, core), tile: 4 (over y, x).
Axes of the slice: x: 2, y: 2, z: 4, core: 2. Of those that a mesh axis runs over, the one named last changes fastest.
Arguments:
- coords: float32 [64, 3, 3200], P('ens', None, 'tile'), may hold values from -6 to 6
- counts: int32 [3200, 3200], P('tile'), may hold values from 0 to 63, as said below
- segments: int32 [3200], replicated, may hold values from 0 to 7, never falling along the last dimension, each value on 1 to 800 neighbouring positions
Outputs:
- gradient: float32 [64, 3, 3200], P('ens', None, 'tile')
The draws below stay inside these ranges and needn't reach their ends.
Inputs may be any that keep to these rules, and one draw needn't show every extreme that they name: counts is symmetric: counts[i, j] == counts[j, i].
All inputs are finite; a program needn't handle non-finite values.
Results may differ from the reference program's by a relative error of at most 0.00011.
Values sent between devices are 32-bit elements; how exact they have to be, the bound alone decides.
No kernel may reach another device: no remote copies, remote signals or barrier semaphores. Data moves between devices by JAX's collectives and lax.ppermute only.
A program may use at most 64 MiB of HBM per device.

```python
import math
import jax
import jax.numpy as jnp
import numpy as np
from jax import lax

BEADS = 3200
SEGS = 8
STRUCTS = 64


def draw_counts(key, part):
    raw = jax.random.randint(key, (BEADS, BEADS), 0, 64, dtype=jnp.int32)
    rows = lax.broadcasted_iota(jnp.int32, (BEADS, BEADS), 0)
    cols = lax.broadcasted_iota(jnp.int32, (BEADS, BEADS), 1)
    raw = jnp.where((rows == 0) & (cols == 1), 63, raw)
    raw = jnp.where((rows == 0) & (cols == 2), 0, raw)
    return jnp.where(rows <= cols, raw, raw.T)


def shard_levels(stream_key, dims, shards, low, high):
    gain, own = 1.0, jax.random.fold_in(stream_key, 6)
    for dim, blocks in shards:
        steps = jnp.exp(jax.random.uniform(jax.random.fold_in(own, dim), (blocks,), jnp.float32, low / len(shards), high / len(shards)))
        gain = gain * jnp.repeat(steps, dims[dim] // blocks).reshape([-1 if axis == dim else 1 for axis in range(len(dims))])
    return gain


def profile(number_of, total, reach, lean):
    weights = [(1 << 20) // math.isqrt(grade ** lean) + 1 for grade in range(2, number_of + 1)]
    surplus, given = total - reach - (number_of - 1), [1] * (number_of - 1)
    while surplus > 0:
        free = [i for i in range(number_of - 1) if given[i] < reach]
        pool, remaining = sum([weights[i] for i in free]), surplus
        for i in free:
            more = min(reach - given[i], max(1, remaining * weights[i] // pool), surplus)
            given[i] = given[i] + more
            surplus = surplus - more
    return np.array([reach] + given)


def ragged(own_key, count, total, bound, lean):
    if count == 2:
        one = jax.random.randint(own_key, (), max(1, total - bound), min(bound, total - 1) + 1)
        return jnp.stack([one, total - one])
    lengths = jnp.asarray(profile(count, total, bound, lean), jnp.int32)
    pairs = (count - 1) // 2
    source_of, taker = lengths[1:1 + 2 * pairs:2], lengths[2:2 + 2 * pairs:2]
    slack = jnp.minimum(source_of - 1, bound - taker)
    passed = jax.random.randint(jax.random.fold_in(own_key, 1), (pairs,), 0, 1 << 20) % (slack + 1)
    lengths = lengths.at[1:1 + 2 * pairs:2].set(source_of - passed).at[2:2 + 2 * pairs:2].set(taker + passed)
    return lengths[jax.random.permutation(jax.random.fold_in(own_key, 2), count)]


def scatter_about(stream_key, dims, width, limit, shards=(), kind=jnp.bfloat16):
    array = width * jax.random.normal(stream_key, dims, jnp.float32)
    if shards:
        array = array * shard_levels(stream_key, dims, shards, -0.22, 0.18)
    return jnp.clip(array, -limit, limit).astype(kind)


def setup_inputs(seed: int = 0) -> dict:
    splits = jax.random.split(jax.random.key(seed), 4)
    return {
        "coords": scatter_about(splits[0], (STRUCTS, 3, BEADS), 1.0, 6.0, ((0, 8), (2, 4)), jnp.float32),
        "counts": draw_counts(jax.random.fold_in(splits[3], 71), 0),
        "segments": jnp.searchsorted(jnp.cumsum(ragged(splits[2], SEGS, BEADS, BEADS // 4, 1)), jnp.arange(BEADS), side="right").astype(jnp.int32),
    }


def pair_sigmoid(rows_xyz, all_xyz):
    gap = rows_xyz[:, :, None] - all_xyz[:, None, :]
    dist = jnp.sum(gap * gap, axis=0)
    return jax.nn.sigmoid(1.0 * (6.0 - dist))


def reference(coords, counts, segments):
    beads = coords.shape[2]
    index = jnp.arange(beads, dtype=jnp.int32)
    same = segments[:, None] == segments[None, :]
    weight = jnp.where(index[:, None] == index[None, :], 0.0, jnp.where(same, 1.0, 0.3)).astype(jnp.float32)
    count_f = counts.astype(jnp.float32)
    target = count_f / (count_f + 8.0)

    def accumulate(total, xyz):
        return total + pair_sigmoid(xyz, xyz), None

    total, unused = lax.scan(accumulate, jnp.zeros((beads, beads), jnp.float32), coords)
    pbar = total / coords.shape[0]
    weighted = weight * (pbar - target)

    def grad_one(xyz):
        sig = pair_sigmoid(xyz, xyz)
        term = weighted * sig * (1.0 - sig)
        rowsum = jnp.sum(term, axis=1)
        mixed = jnp.dot(xyz, term.T, precision=lax.Precision.HIGHEST, preferred_element_type=jnp.float32)
        return -(1.0 / 16) * (rowsum[None, :] * xyz - mixed)

    return lax.map(grad_one, coords)
```

```python
import functools

import jax
import jax.numpy as jnp
from jax import lax
from jax.experimental import pallas as pl
from jax.experimental.pallas import tpu as pltpu
from jax.sharding import PartitionSpec as P

LANES = 128
WIDE = 256


def split3(v):
    hi = v.astype(jnp.bfloat16).astype(jnp.float32)
    rest = v - hi
    mid = rest.astype(jnp.bfloat16).astype(jnp.float32)
    return hi, mid, rest - mid


def augment(v, norm_row, one_row):
    n = v.shape[1]
    norm = 1.5 - 0.5 * jnp.sum(v * v, axis=0, keepdims=True)
    v8 = jnp.concatenate([v, jnp.zeros((5, n), jnp.float32)], axis=0)
    row = lax.broadcasted_iota(jnp.int32, (8, n), 0)
    return jnp.where(row == norm_row, norm, jnp.where(row == one_row, 1.0, v8))


def pair_kernel(structs, tiles, row_base_ref, rows_ref, seg_rows_ref, seg_cols_ref, col_ids_ref, counts_ref, *rest):
    cols_refs = rest[:tiles]
    out_ref, lhs_ref, rhs_ref, weight_ref = rest[tiles:]
    n_rows = rows_ref.shape[2]
    n_cols = counts_ref.shape[1]
    wide = weight_ref.shape[1]
    starts = [(a, min(WIDE, wide - a)) for a in range(0, wide, WIDE)]

    def features(s, carry):
        rows = augment(rows_ref[s], 3, 4)
        hi, mid, lo = split3(rows)
        left = jnp.concatenate([hi, hi, mid, mid, hi, lo], axis=0)
        lhs_ref[s] = left.T.astype(jnp.bfloat16)
        cols = [ref[s] for ref in cols_refs]
        if wide > n_cols:
            cols.append(jnp.zeros((3, wide - n_cols), jnp.float32))
        hi, mid, lo = split3(augment(jnp.concatenate(cols, axis=1), 4, 3))
        rhs_ref[s] = jnp.concatenate([hi, mid, hi, mid, lo, hi], axis=0).astype(jnp.bfloat16)
        return carry

    lax.fori_loop(0, structs, features, 0)
    weight_ref[...] = jnp.zeros_like(weight_ref)

    def tanh_block(s, start, size):
        half = jnp.dot(lhs_ref[s], rhs_ref[s, :, pl.ds(start, size)], preferred_element_type=jnp.float32)
        return jnp.tanh(half)

    def add_one(s, carry):
        for start, size in starts:
            weight_ref[:, pl.ds(start, size)] += tanh_block(s, start, size)
        return carry

    lax.fori_loop(0, structs, add_one, 0)

    count = counts_ref[...].astype(jnp.float32)
    target = count / (count + 8.0)
    pbar = 0.5 + (0.5 / structs) * weight_ref[:, pl.ds(0, n_cols)]
    row_ids = row_base_ref[0] + lax.broadcasted_iota(jnp.int32, (n_rows, n_cols), 0)
    weight = jnp.where(seg_rows_ref[...] == seg_cols_ref[...], 1.0, 0.3)
    weight = jnp.where(row_ids == col_ids_ref[...], 0.0, weight)
    weight_ref[:, pl.ds(0, n_cols)] = weight * (pbar - target)
    if wide > n_cols:
        weight_ref[:, pl.ds(n_cols, wide - n_cols)] = jnp.zeros((n_rows, wide - n_cols), jnp.float32)

    def grad_one(s, carry):
        total = jnp.zeros((16, n_rows), jnp.float32)
        for start, size in starts:
            t = tanh_block(s, start, size)
            g = weight_ref[:, pl.ds(start, size)] * (1.0 - t * t)
            hi = g.astype(jnp.bfloat16)
            lo = (g - hi.astype(jnp.float32)).astype(jnp.bfloat16)
            part = rhs_ref[s, pl.ds(0, 16), pl.ds(start, size)]
            dims = (((1,), (1,)), ((), ()))
            total += lax.dot_general(part, hi, dims, preferred_element_type=jnp.float32)
            total += lax.dot_general(part, lo, dims, preferred_element_type=jnp.float32)
        mixed = total[0:3] + total[8:11]
        out_ref[s] = (0.25 / 16) * (mixed - total[3:4] * rows_ref[s])
        return carry

    lax.fori_loop(0, structs, grad_one, 0)


def split_ens(n_ens, beads, tiles):
    best = None
    for parts in range(1, n_ens + 1):
        if n_ens % parts or beads % parts or beads % (n_ens // parts):
            continue
        cost = 2 * (beads // parts) + tiles * (beads // (n_ens // parts))
        if best is None or cost < best[0]:
            best = (cost, parts)
    return best[1]


def on_device(coords, counts, segments):
    local_n, _, beads = coords.shape
    n_tile = lax.axis_size("tile")
    n_ens = lax.axis_size("ens")
    structs = local_n * n_ens
    n_p = split_ens(n_ens, beads, n_tile)
    n_q = n_ens // n_p
    n_rows, piece = beads // n_p, beads // n_q
    n_cols = piece * n_tile
    tile, ens = lax.axis_index("tile"), lax.axis_index("ens")
    p, q = lax.rem(ens, n_p), lax.div(ens, n_p)

    col_send = jnp.moveaxis(coords.reshape(local_n, 3, n_q, piece), 2, 0)
    col_send = jnp.broadcast_to(col_send[:, None], (n_q, n_p, local_n, 3, piece)).reshape(n_ens, local_n, 3, piece)
    row_send = jnp.moveaxis(coords.reshape(local_n, 3, n_p, n_rows), 2, 0)
    row_send = jnp.broadcast_to(row_send[None], (n_q, n_p, local_n, 3, n_rows)).reshape(n_ens, local_n, 3, n_rows)
    own = lax.all_to_all(col_send, "ens", 0, 0, tiled=True).reshape(structs, 3, piece)
    cols = [own]
    for k in range(1, n_tile):
        cols.append(lax.ppermute(own, "tile", [(t, (t - k) % n_tile) for t in range(n_tile)]))
    rows = lax.all_to_all(row_send, "ens", 0, 0, tiled=True).reshape(structs, 3, n_rows)

    row_base = tile * beads + p * n_rows
    col_bases = [lax.rem(tile + k, n_tile) * beads + q * piece for k in range(n_tile)]
    own_counts = lax.dynamic_slice_in_dim(counts, p * n_rows, n_rows, 0)
    block = jnp.concatenate([lax.dynamic_slice_in_dim(own_counts, b, piece, 1) for b in col_bases], axis=1)
    seg_cols = jnp.concatenate([lax.dynamic_slice_in_dim(segments, b, piece) for b in col_bases])[None, :]
    col_ids = jnp.concatenate([b + jnp.arange(piece, dtype=jnp.int32) for b in col_bases])[None, :]
    seg_rows = lax.dynamic_slice_in_dim(segments, row_base, n_rows)[:, None]

    wide = -(-n_cols // LANES) * LANES
    vmem = pl.BlockSpec(memory_space=pltpu.VMEM)
    grad = pl.pallas_call(
        functools.partial(pair_kernel, structs, n_tile),
        out_shape=jax.ShapeDtypeStruct((structs, 3, n_rows), jnp.float32),
        in_specs=[pl.BlockSpec(memory_space=pltpu.SMEM)] + [vmem] * (5 + n_tile),
        out_specs=vmem,
        scratch_shapes=[
            pltpu.VMEM((structs, n_rows, 48), jnp.bfloat16),
            pltpu.VMEM((structs, 48, wide), jnp.bfloat16),
            pltpu.VMEM((n_rows, wide), jnp.float32),
        ],
        compiler_params=pltpu.CompilerParams(vmem_limit_bytes=48 << 20),
        name="pairs",
    )(row_base[None], rows, seg_rows, seg_cols, col_ids, block, *cols)

    back = lax.all_to_all(grad.reshape(n_ens, local_n, 3, n_rows), "ens", 0, 0, tiled=True)
    back = jnp.sum(back.reshape(n_q, n_p, local_n, 3, n_rows), axis=0)
    return jnp.moveaxis(back, 0, 2).reshape(local_n, 3, beads)


def solution(mesh):
    return jax.shard_map(
        on_device,
        mesh=mesh,
        in_specs=(P("ens", None, "tile"), P("tile", None), P()),
        out_specs=P("ens", None, "tile"),
        check_vma=False,
    )
```

```python
import functools

import jax
import jax.numpy as jnp
from jax import lax
from jax.experimental import pallas as pl
from jax.experimental.pallas import tpu as pltpu
from jax.sharding import PartitionSpec as P

LANES = 128
WIDE = 256


def split3(v):
    hi = v.astype(jnp.bfloat16).astype(jnp.float32)
    rest = v - hi
    mid = rest.astype(jnp.bfloat16).astype(jnp.float32)
    return hi, mid, rest - mid


def augment(v, norm_row, one_row):
    n = v.shape[1]
    norm = 1.5 - 0.5 * jnp.sum(v * v, axis=0, keepdims=True)
    v8 = jnp.concatenate([v, jnp.zeros((5, n), jnp.float32)], axis=0)
    row = lax.broadcasted_iota(jnp.int32, (8, n), 0)
    return jnp.where(row == norm_row, norm, jnp.where(row == one_row, 1.0, v8))


def pair_kernel(structs, tiles, base_ref, out_xyz_ref, seg_out_ref, seg_par_ref, par_ids_ref, counts_ref, *rest):
    par_refs = rest[:tiles]
    grad_ref, lhs_ref, rhs_ref, terms_ref, weight_ref = rest[tiles:]
    n_out = out_xyz_ref.shape[2]
    n_par = counts_ref.shape[0]
    wide = weight_ref.shape[1]
    deep = terms_ref.shape[2]
    starts = [(a, min(WIDE, n_par - a)) for a in range(0, n_par, WIDE)]

    def features(s, carry):
        par = [ref[s] for ref in par_refs]
        if deep > n_par:
            par.append(jnp.zeros((3, deep - n_par), jnp.float32))
        hi, mid, lo = split3(augment(jnp.concatenate(par, axis=1), 4, 3))
        left = jnp.concatenate([hi, mid, hi, mid, lo, hi], axis=0)
        lhs_ref[s] = left.T[:n_par].astype(jnp.bfloat16)
        terms_ref[s] = left[0:16].astype(jnp.bfloat16)
        out = out_xyz_ref[s]
        if wide > n_out:
            out = jnp.concatenate([out, jnp.zeros((3, wide - n_out), jnp.float32)], axis=1)
        hi, mid, lo = split3(augment(out, 3, 4))
        rhs_ref[s] = jnp.concatenate([hi, hi, mid, mid, hi, lo], axis=0).astype(jnp.bfloat16)
        return carry

    lax.fori_loop(0, structs, features, 0)
    weight_ref[...] = jnp.zeros_like(weight_ref)

    def tanh_block(s, start, size):
        half = jnp.dot(lhs_ref[s, pl.ds(start, size)], rhs_ref[s], preferred_element_type=jnp.float32)
        return jnp.tanh(half)

    def add_one(s, carry):
        for start, size in starts:
            weight_ref[pl.ds(start, size)] += tanh_block(s, start, size)
        return carry

    lax.fori_loop(0, structs, add_one, 0)

    count = counts_ref[...].astype(jnp.float32)
    target = count / (count + 8.0)
    pbar = 0.5 + (0.5 / structs) * weight_ref[:, pl.ds(0, n_out)]
    out_ids = base_ref[0] + lax.broadcasted_iota(jnp.int32, (n_par, n_out), 1)
    weight = jnp.where(seg_par_ref[...] == seg_out_ref[...], 1.0, 0.3)
    weight = jnp.where(out_ids == par_ids_ref[...], 0.0, weight)
    weight_ref[:, pl.ds(0, n_out)] = weight * (pbar - target)
    if wide > n_out:
        weight_ref[:, pl.ds(n_out, wide - n_out)] = jnp.zeros((n_par, wide - n_out), jnp.float32)

    def grad_one(s, carry):
        total = jnp.zeros((16, wide), jnp.float32)
        for start, size in starts:
            t = tanh_block(s, start, size)
            g = weight_ref[pl.ds(start, size)] * (1.0 - t * t)
            hi = g.astype(jnp.bfloat16)
            lo = (g - hi.astype(jnp.float32)).astype(jnp.bfloat16)
            terms = terms_ref[s, :, pl.ds(start, size)]
            total += jnp.dot(terms, hi, preferred_element_type=jnp.float32)
            total += jnp.dot(terms, lo, preferred_element_type=jnp.float32)
        total = total[:, :n_out]
        mixed = total[0:3] + total[8:11]
        grad_ref[s] = (0.25 / 16) * (mixed - total[3:4] * out_xyz_ref[s])
        return carry

    lax.fori_loop(0, structs, grad_one, 0)


def split_ens(n_ens, beads, tiles):
    best = None
    for parts in range(1, n_ens + 1):
        if n_ens % parts or beads % parts or beads % (n_ens // parts):
            continue
        cost = 2 * (beads // parts) + tiles * (beads // (n_ens // parts))
        if best is None or cost < best[0]:
            best = (cost, parts)
    return best[1]


def on_device(coords, counts, segments):
    local_n, _, beads = coords.shape
    n_tile = lax.axis_size("tile")
    n_ens = lax.axis_size("ens")
    structs = local_n * n_ens
    n_p = split_ens(n_ens, beads, n_tile)
    n_q = n_ens // n_p
    n_rows, piece = beads // n_p, beads // n_q
    n_cols = piece * n_tile
    tile, ens = lax.axis_index("tile"), lax.axis_index("ens")
    p, q = lax.rem(ens, n_p), lax.div(ens, n_p)

    col_send = jnp.moveaxis(coords.reshape(local_n, 3, n_q, piece), 2, 0)
    col_send = jnp.broadcast_to(col_send[:, None], (n_q, n_p, local_n, 3, piece)).reshape(n_ens, local_n, 3, piece)
    row_send = jnp.moveaxis(coords.reshape(local_n, 3, n_p, n_rows), 2, 0)
    row_send = jnp.broadcast_to(row_send[None], (n_q, n_p, local_n, 3, n_rows)).reshape(n_ens, local_n, 3, n_rows)
    own = lax.all_to_all(col_send, "ens", 0, 0, tiled=True).reshape(structs, 3, piece)
    cols = [own]
    for k in range(1, n_tile):
        cols.append(lax.ppermute(own, "tile", [(t, (t - k) % n_tile) for t in range(n_tile)]))
    rows = lax.all_to_all(row_send, "ens", 0, 0, tiled=True).reshape(structs, 3, n_rows)

    row_base = tile * beads + p * n_rows
    col_bases = [lax.rem(tile + k, n_tile) * beads + q * piece for k in range(n_tile)]
    own_counts = lax.dynamic_slice_in_dim(counts, p * n_rows, n_rows, 0)
    block = jnp.concatenate([lax.dynamic_slice_in_dim(own_counts, b, piece, 1) for b in col_bases], axis=1).T
    seg_cols = jnp.concatenate([lax.dynamic_slice_in_dim(segments, b, piece) for b in col_bases])[:, None]
    col_ids = jnp.concatenate([b + jnp.arange(piece, dtype=jnp.int32) for b in col_bases])[:, None]
    seg_rows = lax.dynamic_slice_in_dim(segments, row_base, n_rows)[None, :]

    wide = -(-n_rows // LANES) * LANES
    deep = -(-n_cols // LANES) * LANES
    vmem = pl.BlockSpec(memory_space=pltpu.VMEM)
    grad = pl.pallas_call(
        functools.partial(pair_kernel, structs, n_tile),
        out_shape=jax.ShapeDtypeStruct((structs, 3, n_rows), jnp.float32),
        in_specs=[pl.BlockSpec(memory_space=pltpu.SMEM)] + [vmem] * (5 + n_tile),
        out_specs=vmem,
        scratch_shapes=[
            pltpu.VMEM((structs, n_cols, 48), jnp.bfloat16),
            pltpu.VMEM((structs, 48, wide), jnp.bfloat16),
            pltpu.VMEM((structs, 16, deep), jnp.bfloat16),
            pltpu.VMEM((n_cols, wide), jnp.float32),
        ],
        compiler_params=pltpu.CompilerParams(vmem_limit_bytes=48 << 20),
        name="pairs",
    )(row_base[None], rows, seg_rows, seg_cols, col_ids, block, *cols)

    back = lax.all_to_all(grad.reshape(n_ens, local_n, 3, n_rows), "ens", 0, 0, tiled=True)
    back = jnp.sum(back.reshape(n_q, n_p, local_n, 3, n_rows), axis=0)
    return jnp.moveaxis(back, 0, 2).reshape(local_n, 3, beads)


def solution(mesh):
    return jax.shard_map(
        on_device,
        mesh=mesh,
        in_specs=(P("ens", None, "tile"), P("tile", None), P()),
        out_specs=P("ens", None, "tile"),
        check_vma=False,
    )
```

```python
import functools

import jax
import jax.numpy as jnp
from jax import lax
from jax.experimental import pallas as pl
from jax.experimental.pallas import tpu as pltpu
from jax.sharding import PartitionSpec as P

LANES = 128
WIDE = 256


def split3(v):
    hi = v.astype(jnp.bfloat16).astype(jnp.float32)
    rest = v - hi
    mid = rest.astype(jnp.bfloat16).astype(jnp.float32)
    return hi, mid, rest - mid


def augment(v, norm_row, one_row):
    n = v.shape[1]
    norm = 1.5 - 0.5 * jnp.sum(v * v, axis=0, keepdims=True)
    v8 = jnp.concatenate([v, jnp.zeros((5, n), jnp.float32)], axis=0)
    row = lax.broadcasted_iota(jnp.int32, (8, n), 0)
    return jnp.where(row == norm_row, norm, jnp.where(row == one_row, 1.0, v8))


def pair_kernel(structs, tiles, base_ref, out_xyz_ref, seg_out_ref, seg_par_ref, par_ids_ref, counts_ref, *rest):
    par_refs = rest[:tiles]
    grad_ref, lhs_ref, rhs_ref, terms_ref, weight_ref = rest[tiles:]
    n_out = out_xyz_ref.shape[2]
    n_par = counts_ref.shape[0]
    wide = weight_ref.shape[1]
    deep = terms_ref.shape[2]
    starts = [(a, min(WIDE, n_par - a)) for a in range(0, n_par, WIDE)]

    def features(s, carry):
        par = [ref[s] for ref in par_refs]
        if deep > n_par:
            par.append(jnp.zeros((3, deep - n_par), jnp.float32))
        hi, mid, lo = split3(augment(jnp.concatenate(par, axis=1), 4, 3))
        left = jnp.concatenate([hi, mid, hi, mid, lo, hi], axis=0)
        lhs_ref[s] = left.T[:n_par].astype(jnp.bfloat16)
        terms_ref[s] = left[0:16].astype(jnp.bfloat16)
        out = out_xyz_ref[s]
        if wide > n_out:
            out = jnp.concatenate([out, jnp.zeros((3, wide - n_out), jnp.float32)], axis=1)
        hi, mid, lo = split3(augment(out, 3, 4))
        rhs_ref[s] = jnp.concatenate([hi, hi, mid, mid, hi, lo], axis=0).astype(jnp.bfloat16)
        return carry

    lax.fori_loop(0, structs, features, 0, unroll=4)
    weight_ref[...] = jnp.zeros_like(weight_ref)

    def tanh_block(s, start, size):
        half = jnp.dot(lhs_ref[s, pl.ds(start, size)], rhs_ref[s], preferred_element_type=jnp.float32)
        return jnp.tanh(half)

    def add_one(s, carry):
        for start, size in starts:
            weight_ref[pl.ds(start, size)] += tanh_block(s, start, size)
        return carry

    lax.fori_loop(0, structs, add_one, 0, unroll=4)

    count = counts_ref[...].astype(jnp.float32)
    target = count / (count + 8.0)
    pbar = 0.5 + (0.5 / structs) * weight_ref[:, pl.ds(0, n_out)]
    out_ids = base_ref[0] + lax.broadcasted_iota(jnp.int32, (n_par, n_out), 1)
    weight = jnp.where(seg_par_ref[...] == seg_out_ref[...], 1.0, 0.3)
    weight = jnp.where(out_ids == par_ids_ref[...], 0.0, weight)
    weight_ref[:, pl.ds(0, n_out)] = weight * (pbar - target)
    if wide > n_out:
        weight_ref[:, pl.ds(n_out, wide - n_out)] = jnp.zeros((n_par, wide - n_out), jnp.float32)

    def grad_one(s, carry):
        total = jnp.zeros((16, wide), jnp.float32)
        for start, size in starts:
            t = tanh_block(s, start, size)
            g = weight_ref[pl.ds(start, size)] * (1.0 - t * t)
            hi = g.astype(jnp.bfloat16)
            lo = (g - hi.astype(jnp.float32)).astype(jnp.bfloat16)
            terms = terms_ref[s, :, pl.ds(start, size)]
            total += jnp.dot(terms, hi, preferred_element_type=jnp.float32)
            total += jnp.dot(terms, lo, preferred_element_type=jnp.float32)
        total = total[:, :n_out]
        mixed = total[0:3] + total[8:11]
        grad_ref[s] = (0.25 / 16) * (mixed - total[3:4] * out_xyz_ref[s])
        return carry

    lax.fori_loop(0, structs, grad_one, 0, unroll=2)


def split_ens(n_ens, beads, tiles):
    best = None
    for parts in range(1, n_ens + 1):
        if n_ens % parts or beads % parts or beads % (n_ens // parts):
            continue
        cost = 2 * (beads // parts) + tiles * (beads // (n_ens // parts))
        if best is None or cost < best[0]:
            best = (cost, parts)
    return best[1]


def on_device(coords, counts, segments):
    local_n, _, beads = coords.shape
    n_tile = lax.axis_size("tile")
    n_ens = lax.axis_size("ens")
    structs = local_n * n_ens
    n_p = split_ens(n_ens, beads, n_tile)
    n_q = n_ens // n_p
    n_rows, piece = beads // n_p, beads // n_q
    n_cols = piece * n_tile
    tile, ens = lax.axis_index("tile"), lax.axis_index("ens")
    p, q = lax.rem(ens, n_p), lax.div(ens, n_p)

    col_send = jnp.moveaxis(coords.reshape(local_n, 3, n_q, piece), 2, 0)
    col_send = jnp.broadcast_to(col_send[:, None], (n_q, n_p, local_n, 3, piece)).reshape(n_ens, local_n, 3, piece)
    row_send = jnp.moveaxis(coords.reshape(local_n, 3, n_p, n_rows), 2, 0)
    row_send = jnp.broadcast_to(row_send[None], (n_q, n_p, local_n, 3, n_rows)).reshape(n_ens, local_n, 3, n_rows)
    own = lax.all_to_all(col_send, "ens", 0, 0, tiled=True).reshape(structs, 3, piece)
    cols = [own]
    for k in range(1, n_tile):
        cols.append(lax.ppermute(own, "tile", [(t, (t - k) % n_tile) for t in range(n_tile)]))
    rows = lax.all_to_all(row_send, "ens", 0, 0, tiled=True).reshape(structs, 3, n_rows)

    row_base = tile * beads + p * n_rows
    col_bases = [lax.rem(tile + k, n_tile) * beads + q * piece for k in range(n_tile)]
    own_counts = lax.dynamic_slice_in_dim(counts, p * n_rows, n_rows, 0)
    block = jnp.concatenate([lax.dynamic_slice_in_dim(own_counts, b, piece, 1) for b in col_bases], axis=1).T
    seg_cols = jnp.concatenate([lax.dynamic_slice_in_dim(segments, b, piece) for b in col_bases])[:, None]
    col_ids = jnp.concatenate([b + jnp.arange(piece, dtype=jnp.int32) for b in col_bases])[:, None]
    seg_rows = lax.dynamic_slice_in_dim(segments, row_base, n_rows)[None, :]

    wide = -(-n_rows // LANES) * LANES
    deep = -(-n_cols // LANES) * LANES
    vmem = pl.BlockSpec(memory_space=pltpu.VMEM)
    grad = pl.pallas_call(
        functools.partial(pair_kernel, structs, n_tile),
        out_shape=jax.ShapeDtypeStruct((structs, 3, n_rows), jnp.float32),
        in_specs=[pl.BlockSpec(memory_space=pltpu.SMEM)] + [vmem] * (5 + n_tile),
        out_specs=vmem,
        scratch_shapes=[
            pltpu.VMEM((structs, n_cols, 48), jnp.bfloat16),
            pltpu.VMEM((structs, 48, wide), jnp.bfloat16),
            pltpu.VMEM((structs, 16, deep), jnp.bfloat16),
            pltpu.VMEM((n_cols, wide), jnp.float32),
        ],
        compiler_params=pltpu.CompilerParams(vmem_limit_bytes=48 << 20),
        name="pairs",
    )(row_base[None], rows, seg_rows, seg_cols, col_ids, block, *cols)

    back = lax.all_to_all(grad.reshape(n_ens, local_n, 3, n_rows), "ens", 0, 0, tiled=True)
    back = jnp.sum(back.reshape(n_q, n_p, local_n, 3, n_rows), axis=0)
    return jnp.moveaxis(back, 0, 2).reshape(local_n, 3, beads)


def solution(mesh):
    return jax.shard_map(
        on_device,
        mesh=mesh,
        in_specs=(P("ens", None, "tile"), P("tile", None), P()),
        out_specs=P("ens", None, "tile"),
        check_vma=False,
    )
```

```python
import functools

import jax
import jax.numpy as jnp
from jax import lax
from jax.experimental import pallas as pl
from jax.experimental.pallas import tpu as pltpu
from jax.sharding import PartitionSpec as P

LANES = 128
WIDE = 256


def split3(v):
    hi = v.astype(jnp.bfloat16).astype(jnp.float32)
    rest = v - hi
    mid = rest.astype(jnp.bfloat16).astype(jnp.float32)
    return hi, mid, rest - mid


def augment(v, norm_row, one_row):
    n = v.shape[1]
    norm = 1.5 - 0.5 * jnp.sum(v * v, axis=0, keepdims=True)
    v8 = jnp.concatenate([v, jnp.zeros((5, n), jnp.float32)], axis=0)
    row = lax.broadcasted_iota(jnp.int32, (8, n), 0)
    return jnp.where(row == norm_row, norm, jnp.where(row == one_row, 1.0, v8))


def pair_kernel(n_groups, n_mix, n_out_refs, base_ref, seg_out_ref, seg_par_ref, par_ids_ref, counts_ref, *rest):
    n_par_refs = len(rest) - 2 * n_out_refs - 6
    out_refs, rest = rest[:n_out_refs], rest[n_out_refs:]
    par_refs, rest = rest[:n_par_refs], rest[n_par_refs:]
    grad_refs, (xyz_ref, grad_ref, lhs_ref, rhs_ref, terms_ref, weight_ref) = rest[:n_out_refs], rest[n_out_refs:]
    structs, _, n_out = xyz_ref.shape
    per = structs // n_groups
    block = structs // n_out_refs
    n_par = counts_ref.shape[0]
    wide = weight_ref.shape[1]
    deep = terms_ref.shape[2]
    starts = [(a, min(WIDE, n_par - a)) for a in range(0, n_par, WIDE)]

    for r, ref in enumerate(out_refs):
        xyz_ref[pl.ds(r * block, block)] = ref[...]

    def features(s, carry):
        group, inside = lax.div(s, per), lax.rem(s, per)
        par = [ref[(group ^ (j % n_mix)) * per + inside] for j, ref in enumerate(par_refs)]
        if deep > n_par:
            par.append(jnp.zeros((3, deep - n_par), jnp.float32))
        hi, mid, lo = split3(augment(jnp.concatenate(par, axis=1), 4, 3))
        left = jnp.concatenate([hi, mid, hi, mid, lo, hi], axis=0)
        lhs_ref[s] = left.T[:n_par].astype(jnp.bfloat16)
        terms_ref[s] = left[0:16].astype(jnp.bfloat16)
        out = xyz_ref[s]
        if wide > n_out:
            out = jnp.concatenate([out, jnp.zeros((3, wide - n_out), jnp.float32)], axis=1)
        hi, mid, lo = split3(augment(out, 3, 4))
        rhs_ref[s] = jnp.concatenate([hi, hi, mid, mid, hi, lo], axis=0).astype(jnp.bfloat16)
        return carry

    lax.fori_loop(0, structs, features, 0, unroll=4)
    weight_ref[...] = jnp.zeros_like(weight_ref)

    def tanh_block(s, start, size):
        half = jnp.dot(lhs_ref[s, pl.ds(start, size)], rhs_ref[s], preferred_element_type=jnp.float32)
        return jnp.tanh(half)

    def add_one(s, carry):
        for start, size in starts:
            weight_ref[pl.ds(start, size)] += tanh_block(s, start, size)
        return carry

    lax.fori_loop(0, structs, add_one, 0, unroll=4)

    count = counts_ref[...].astype(jnp.float32)
    target = count / (count + 8.0)
    pbar = 0.5 + (0.5 / structs) * weight_ref[:, pl.ds(0, n_out)]
    out_ids = base_ref[0] + lax.broadcasted_iota(jnp.int32, (n_par, n_out), 1)
    weight = jnp.where(seg_par_ref[...] == seg_out_ref[...], 1.0, 0.3)
    weight = jnp.where(out_ids == par_ids_ref[...], 0.0, weight)
    weight_ref[:, pl.ds(0, n_out)] = weight * (pbar - target)
    if wide > n_out:
        weight_ref[:, pl.ds(n_out, wide - n_out)] = jnp.zeros((n_par, wide - n_out), jnp.float32)

    def grad_one(s, carry):
        total = jnp.zeros((16, wide), jnp.float32)
        for start, size in starts:
            t = tanh_block(s, start, size)
            g = weight_ref[pl.ds(start, size)] * (1.0 - t * t)
            hi = g.astype(jnp.bfloat16)
            lo = (g - hi.astype(jnp.float32)).astype(jnp.bfloat16)
            terms = terms_ref[s, :, pl.ds(start, size)]
            total += jnp.dot(terms, hi, preferred_element_type=jnp.float32)
            total += jnp.dot(terms, lo, preferred_element_type=jnp.float32)
        total = total[:, :n_out]
        grad_ref[s] = (0.25 / 16) * (total[0:3] + total[8:11] - total[3:4] * xyz_ref[s])
        return carry

    lax.fori_loop(0, structs, grad_one, 0, unroll=2)
    for r, ref in enumerate(grad_refs):
        ref[...] = grad_ref[pl.ds(r * block, block)]


def split_ens(n_ens, beads, tiles):
    best = None
    for parts in range(1, n_ens + 1):
        if n_ens % parts or beads % parts or beads % (n_ens // parts):
            continue
        cost = 2 * (beads // parts) + tiles * (beads // (n_ens // parts))
        if best is None or cost < best[0]:
            best = (cost, parts)
    return best[1]


def pair_gradients(out_list, par_list, par_bases, out_base, counts, segments, p, n_groups, n_mix):
    n_out, chunk = out_list[0].shape[2], par_list[0].shape[2]
    n_par = chunk * len(par_list)
    structs = par_list[0].shape[0]
    own_counts = lax.dynamic_slice_in_dim(counts, p * n_out, n_out, 0)
    block = jnp.concatenate([lax.dynamic_slice_in_dim(own_counts, b, chunk, 1) for b in par_bases], axis=1).T
    seg_par = jnp.concatenate([lax.dynamic_slice_in_dim(segments, b, chunk) for b in par_bases])[:, None]
    par_ids = jnp.concatenate([b + jnp.arange(chunk, dtype=jnp.int32) for b in par_bases])[:, None]
    seg_out = lax.dynamic_slice_in_dim(segments, out_base, n_out)[None, :]
    wide = -(-n_out // LANES) * LANES
    deep = -(-n_par // LANES) * LANES
    vmem = pl.BlockSpec(memory_space=pltpu.VMEM)
    return pl.pallas_call(
        functools.partial(pair_kernel, n_groups, n_mix, len(out_list)),
        out_shape=[jax.ShapeDtypeStruct(x.shape, jnp.float32) for x in out_list],
        in_specs=[pl.BlockSpec(memory_space=pltpu.SMEM)] + [vmem] * (4 + len(out_list) + len(par_list)),
        out_specs=[vmem] * len(out_list),
        scratch_shapes=[
            pltpu.VMEM((structs, 3, n_out), jnp.float32),
            pltpu.VMEM((structs, 3, n_out), jnp.float32),
            pltpu.VMEM((structs, n_par, 48), jnp.bfloat16),
            pltpu.VMEM((structs, 48, wide), jnp.bfloat16),
            pltpu.VMEM((structs, 16, deep), jnp.bfloat16),
            pltpu.VMEM((n_par, wide), jnp.float32),
        ],
        compiler_params=pltpu.CompilerParams(vmem_limit_bytes=48 << 20),
        name="pairs",
    )(out_base[None], seg_out, seg_par, par_ids, block, *out_list, *par_list)


def swap(x, axes, size, flip):
    return lax.ppermute(x, axes, [(i, flip(i)) for i in range(size)])


def by_permutes(coords, counts, segments, n_p, n_q, n_tile):
    local_n, _, beads = coords.shape
    n_ens, n_layer = n_p * n_q, n_p * n_tile
    n_out, chunk = beads // n_p, beads // n_ens
    tile, ens = lax.axis_index("tile"), lax.axis_index("ens")
    p, q = lax.rem(ens, n_p), lax.div(ens, n_p)
    halves = [lax.dynamic_slice_in_dim(coords, (p ^ h) * n_out, n_out, 2) for h in range(n_p)]
    out_list = [halves[0]] + [None] * (n_ens - 1)
    for k in reversed(range(1, n_ens)):
        out_list[k] = swap(halves[k % n_p], "ens", n_ens, lambda e, k=k: e ^ k)
    own = jnp.concatenate([lax.dynamic_slice_in_dim(x, q * chunk, chunk, 2) for x in out_list], axis=0)

    def layer_flip(r):
        dt, dp = divmod(r, n_p)

        def flip(i):
            e, t = divmod(i, n_tile)
            return (e ^ dp) * n_tile + (t ^ dt)

        return flip

    par_list = [own] + [None] * (n_layer - 1)
    par_bases = []
    for r in range(n_layer):
        par_bases.append((tile ^ (r // n_p)) * beads + (p ^ (r % n_p)) * n_out + q * chunk)
    for r in reversed(range(1, n_layer)):
        par_list[r] = swap(own, ("ens", "tile"), n_ens * n_tile, layer_flip(r))

    out_base = tile * beads + p * n_out
    grads = pair_gradients(out_list, par_list, par_bases, out_base, counts, segments, p, n_ens, n_p)
    back = [grads[0]] + [None] * (n_ens - 1)
    for k in reversed(range(1, n_ens)):
        back[k] = swap(grads[k], "ens", n_ens, lambda e, k=k: e ^ k)
    sums = [functools.reduce(jnp.add, back[h::n_p]) for h in range(n_p)]
    if n_p == 1:
        return sums[0]
    if n_p == 2:
        parts = [jnp.where(p == h, sums[0], sums[1]) for h in range(2)]
    else:
        stacked = jnp.stack(sums)
        parts = [lax.dynamic_index_in_dim(stacked, p ^ h, 0, keepdims=False) for h in range(n_p)]
    return jnp.concatenate(parts, axis=2)


def by_all_to_all(coords, counts, segments, n_p, n_q, n_tile):
    local_n, _, beads = coords.shape
    n_ens = n_p * n_q
    structs = local_n * n_ens
    n_out, piece = beads // n_p, beads // n_q
    tile, ens = lax.axis_index("tile"), lax.axis_index("ens")
    p, q = lax.rem(ens, n_p), lax.div(ens, n_p)
    par_send = jnp.moveaxis(coords.reshape(local_n, 3, n_q, piece), 2, 0)
    par_send = jnp.broadcast_to(par_send[:, None], (n_q, n_p, local_n, 3, piece)).reshape(n_ens, local_n, 3, piece)
    out_send = jnp.moveaxis(coords.reshape(local_n, 3, n_p, n_out), 2, 0)
    out_send = jnp.broadcast_to(out_send[None], (n_q, n_p, local_n, 3, n_out)).reshape(n_ens, local_n, 3, n_out)
    own = lax.all_to_all(par_send, "ens", 0, 0, tiled=True).reshape(structs, 3, piece)
    par_list = [own]
    for k in range(1, n_tile):
        par_list.append(lax.ppermute(own, "tile", [(t, (t - k) % n_tile) for t in range(n_tile)]))
    par_bases = [lax.rem(tile + k, n_tile) * beads + q * piece for k in range(n_tile)]
    out = lax.all_to_all(out_send, "ens", 0, 0, tiled=True).reshape(structs, 3, n_out)
    out_base = tile * beads + p * n_out
    (grad,) = pair_gradients([out], par_list, par_bases, out_base, counts, segments, p, n_ens, 1)
    back = lax.all_to_all(grad.reshape(n_ens, local_n, 3, n_out), "ens", 0, 0, tiled=True)
    back = jnp.sum(back.reshape(n_q, n_p, local_n, 3, n_out), axis=0)
    return jnp.moveaxis(back, 0, 2).reshape(local_n, 3, beads)


def power_of_two(n):
    return n & (n - 1) == 0


def on_device(coords, counts, segments):
    beads = coords.shape[2]
    n_tile, n_ens = lax.axis_size("tile"), lax.axis_size("ens")
    n_p = split_ens(n_ens, beads, n_tile)
    n_q = n_ens // n_p
    few = n_ens * n_tile <= 64 and beads % n_ens == 0 and power_of_two(n_ens) and power_of_two(n_tile)
    return (by_permutes if few else by_all_to_all)(coords, counts, segments, n_p, n_q, n_tile)


def solution(mesh):
    return jax.shard_map(
        on_device,
        mesh=mesh,
        in_specs=(P("ens", None, "tile"), P("tile", None), P()),
        out_specs=P("ens", None, "tile"),
        check_vma=False,
    )
```

```python
import functools

import jax
import jax.numpy as jnp
from jax import lax
from jax.experimental import pallas as pl
from jax.experimental.pallas import tpu as pltpu
from jax.sharding import PartitionSpec as P

LANES = 128
WIDE = 256


def split3(v):
    hi = v.astype(jnp.bfloat16).astype(jnp.float32)
    rest = v - hi
    mid = rest.astype(jnp.bfloat16).astype(jnp.float32)
    return hi, mid, rest - mid


def augment(v, norm_row, one_row):
    n = v.shape[1]
    norm = 1.5 - 0.5 * jnp.sum(v * v, axis=0, keepdims=True)
    v8 = jnp.concatenate([v, jnp.zeros((5, n), jnp.float32)], axis=0)
    row = lax.broadcasted_iota(jnp.int32, (8, n), 0)
    return jnp.where(row == norm_row, norm, jnp.where(row == one_row, 1.0, v8))


def pack_kernel(n_p, n_q, xyz_ref, send_ref):
    beads = xyz_ref.shape[2]
    n_rows, piece = beads // n_p, beads // n_q
    for c in range(3):
        for q in range(n_q):
            for p in range(n_p):
                send_ref[q * n_p + p, c, :, pl.ds(0, piece)] = xyz_ref[c, :, pl.ds(q * piece, piece)]
                send_ref[q * n_p + p, c, :, pl.ds(piece, n_rows)] = xyz_ref[c, :, pl.ds(p * n_rows, n_rows)]


def sum_kernel(n_p, n_q, back_ref, total_ref):
    n_rows = back_ref.shape[3]
    for c in range(3):
        for p in range(n_p):
            total = back_ref[p, c]
            for q in range(1, n_q):
                total += back_ref[q * n_p + p, c]
            total_ref[c, :, pl.ds(p * n_rows, n_rows)] = total


def pair_kernel(structs, tiles, base_ref, seg_out_ref, seg_par_ref, par_ids_ref, counts_ref, both_ref, *rest):
    par_refs = rest[:tiles - 1]
    grad_ref, xyz_ref, lhs_ref, rhs_ref, terms_ref, weight_ref = rest[tiles - 1:]
    n_out = seg_out_ref.shape[1]
    piece = both_ref.shape[2] - n_out
    n_par = counts_ref.shape[0]
    wide = weight_ref.shape[1]
    deep = terms_ref.shape[2]
    starts = [(a, min(WIDE, n_par - a)) for a in range(0, n_par, WIDE)]

    def features(s, carry):
        both = both_ref[s]
        par = [both[:, :piece]] + [ref[s] for ref in par_refs]
        if deep > n_par:
            par.append(jnp.zeros((3, deep - n_par), jnp.float32))
        hi, mid, lo = split3(augment(jnp.concatenate(par, axis=1), 4, 3))
        left = jnp.concatenate([hi, mid, hi, mid, lo, hi], axis=0)
        lhs_ref[s] = left.T[:n_par].astype(jnp.bfloat16)
        terms_ref[s] = left[0:16].astype(jnp.bfloat16)
        out = both[:, piece:]
        xyz_ref[s] = out
        if wide > n_out:
            out = jnp.concatenate([out, jnp.zeros((3, wide - n_out), jnp.float32)], axis=1)
        hi, mid, lo = split3(augment(out, 3, 4))
        rhs_ref[s] = jnp.concatenate([hi, hi, mid, mid, hi, lo], axis=0).astype(jnp.bfloat16)
        return carry

    lax.fori_loop(0, structs, features, 0, unroll=4)
    weight_ref[...] = jnp.zeros_like(weight_ref)

    def tanh_block(s, start, size):
        half = jnp.dot(lhs_ref[s, pl.ds(start, size)], rhs_ref[s], preferred_element_type=jnp.float32)
        return jnp.tanh(half)

    def add_one(s, carry):
        for start, size in starts:
            weight_ref[pl.ds(start, size)] += tanh_block(s, start, size)
        return carry

    lax.fori_loop(0, structs, add_one, 0, unroll=4)

    count = counts_ref[...].astype(jnp.float32)
    target = count / (count + 8.0)
    pbar = 0.5 + (0.5 / structs) * weight_ref[:, pl.ds(0, n_out)]
    out_ids = base_ref[0] + lax.broadcasted_iota(jnp.int32, (n_par, n_out), 1)
    weight = jnp.where(seg_par_ref[...] == seg_out_ref[...], 1.0, 0.3)
    weight = jnp.where(out_ids == par_ids_ref[...], 0.0, weight)
    weight_ref[:, pl.ds(0, n_out)] = weight * (pbar - target)
    if wide > n_out:
        weight_ref[:, pl.ds(n_out, wide - n_out)] = jnp.zeros((n_par, wide - n_out), jnp.float32)

    def grad_one(s, carry):
        total = jnp.zeros((16, wide), jnp.float32)
        for start, size in starts:
            t = tanh_block(s, start, size)
            g = weight_ref[pl.ds(start, size)] * (1.0 - t * t)
            hi = g.astype(jnp.bfloat16)
            lo = (g - hi.astype(jnp.float32)).astype(jnp.bfloat16)
            terms = terms_ref[s, :, pl.ds(start, size)]
            total += jnp.dot(terms, hi, preferred_element_type=jnp.float32)
            total += jnp.dot(terms, lo, preferred_element_type=jnp.float32)
        total = total[:, :n_out]
        mixed = total[0:3] + total[8:11]
        grad_ref[s] = (0.25 / 16) * (mixed - total[3:4] * xyz_ref[s])
        return carry

    lax.fori_loop(0, structs, grad_one, 0, unroll=2)


def split_ens(n_ens, beads, tiles):
    best = None
    for parts in range(1, n_ens + 1):
        if n_ens % parts or beads % parts or beads % (n_ens // parts):
            continue
        cost = 2 * (beads // parts) + tiles * (beads // (n_ens // parts))
        if best is None or cost < best[0]:
            best = (cost, parts)
    return best[1]


def on_device(coords, counts, segments):
    local_n, _, beads = coords.shape
    n_tile = lax.axis_size("tile")
    n_ens = lax.axis_size("ens")
    structs = local_n * n_ens
    n_p = split_ens(n_ens, beads, n_tile)
    n_q = n_ens // n_p
    n_rows, piece = beads // n_p, beads // n_q
    n_cols = piece * n_tile
    tile, ens = lax.axis_index("tile"), lax.axis_index("ens")
    p, q = lax.rem(ens, n_p), lax.div(ens, n_p)

    send = pl.pallas_call(
        functools.partial(pack_kernel, n_p, n_q),
        out_shape=jax.ShapeDtypeStruct((n_ens, 3, local_n, piece + n_rows), jnp.float32),
        in_specs=[pl.BlockSpec(memory_space=pltpu.VMEM)],
        out_specs=pl.BlockSpec(memory_space=pltpu.VMEM),
        name="pack",
    )(jnp.swapaxes(coords, 0, 1))
    both = lax.all_to_all(send, "ens", 0, 0, tiled=True)
    both = jnp.swapaxes(both, 1, 2).reshape(structs, 3, piece + n_rows)
    own = both[:, :, :piece]
    cols = [lax.ppermute(own, "tile", [(t, (t - k) % n_tile) for t in range(n_tile)]) for k in range(1, n_tile)]

    row_base = tile * beads + p * n_rows
    col_bases = [lax.rem(tile + k, n_tile) * beads + q * piece for k in range(n_tile)]
    own_counts = lax.dynamic_slice_in_dim(counts, p * n_rows, n_rows, 0)
    block = jnp.concatenate([lax.dynamic_slice_in_dim(own_counts, b, piece, 1) for b in col_bases], axis=1).T
    seg_cols = jnp.concatenate([lax.dynamic_slice_in_dim(segments, b, piece) for b in col_bases])[:, None]
    col_ids = jnp.concatenate([b + jnp.arange(piece, dtype=jnp.int32) for b in col_bases])[:, None]
    seg_rows = lax.dynamic_slice_in_dim(segments, row_base, n_rows)[None, :]

    wide = -(-n_rows // LANES) * LANES
    deep = -(-n_cols // LANES) * LANES
    vmem = pl.BlockSpec(memory_space=pltpu.VMEM)
    grad = pl.pallas_call(
        functools.partial(pair_kernel, structs, n_tile),
        out_shape=jax.ShapeDtypeStruct((structs, 3, n_rows), jnp.float32),
        in_specs=[pl.BlockSpec(memory_space=pltpu.SMEM)] + [vmem] * (4 + n_tile),
        out_specs=vmem,
        scratch_shapes=[
            pltpu.VMEM((structs, 3, n_rows), jnp.float32),
            pltpu.VMEM((structs, n_cols, 48), jnp.bfloat16),
            pltpu.VMEM((structs, 48, wide), jnp.bfloat16),
            pltpu.VMEM((structs, 16, deep), jnp.bfloat16),
            pltpu.VMEM((n_cols, wide), jnp.float32),
        ],
        compiler_params=pltpu.CompilerParams(vmem_limit_bytes=48 << 20),
        name="pairs",
    )(row_base[None], seg_rows, seg_cols, col_ids, block, both, *cols)

    back = jnp.swapaxes(grad.reshape(n_ens, local_n, 3, n_rows), 1, 2)
    back = lax.all_to_all(back, "ens", 0, 0, tiled=True)
    total = pl.pallas_call(
        functools.partial(sum_kernel, n_p, n_q),
        out_shape=jax.ShapeDtypeStruct((3, local_n, beads), jnp.float32),
        in_specs=[pl.BlockSpec(memory_space=pltpu.VMEM)],
        out_specs=pl.BlockSpec(memory_space=pltpu.VMEM),
        name="total",
    )(back)
    return jnp.swapaxes(total, 0, 1)


def solution(mesh):
    return jax.shard_map(
        on_device,
        mesh=mesh,
        in_specs=(P("ens", None, "tile"), P("tile", None), P()),
        out_specs=P("ens", None, "tile"),
        check_vma=False,
    )
```

```python
import functools

import jax
import jax.numpy as jnp
from jax import lax
from jax.experimental import pallas as pl
from jax.experimental.pallas import tpu as pltpu
from jax.sharding import PartitionSpec as P

LANES = 128
WIDE = 256
SLOT = 64
NT = (((1,), (1,)), ((), ()))


def up(n, unit):
    return -(-n // unit) * unit


def split3(v):
    hi = v.astype(jnp.bfloat16).astype(jnp.float32)
    rest = v - hi
    mid = rest.astype(jnp.bfloat16).astype(jnp.float32)
    return hi, mid, rest - mid


def pack_kernel(n_p, n_q, xyz_ref, send_ref):
    beads = xyz_ref.shape[2]
    n_rows, piece = beads // n_p, beads // n_q
    for c in range(3):
        for q in range(n_q):
            for p in range(n_p):
                e = q * n_p + p
                send_ref[e, :, pl.ds(c * piece, piece)] = xyz_ref[c, :, pl.ds(q * piece, piece)]
                send_ref[e, :, pl.ds(3 * piece + c * n_rows, n_rows)] = xyz_ref[c, :, pl.ds(p * n_rows, n_rows)]


def sum_kernel(n_p, n_q, back_ref, total_ref):
    n_rows = back_ref.shape[3]
    for c in range(3):
        for p in range(n_p):
            total = back_ref[p, c]
            for q in range(1, n_q):
                total += back_ref[q * n_p + p, c]
            total_ref[c, :, pl.ds(p * n_rows, n_rows)] = total


def put_terms(refs, xyz, norm_row):
    norm = 1.5 - 0.5 * (xyz[0] * xyz[0] + xyz[1] * xyz[1] + xyz[2] * xyz[2])
    n, size = norm.shape
    wide = refs[0].shape[0] * LANES
    for f, v in ((0, xyz[0]), (1, xyz[1]), (2, xyz[2]), (norm_row, norm)):
        if wide > size:
            v = jnp.concatenate([v, jnp.zeros((n, wide - size), jnp.float32)], axis=1)
        for ref, term in zip(refs, split3(v)):
            for k in range(wide // LANES):
                ref[k, pl.ds(f, n, 8), :] = term[:, k * LANES:(k + 1) * LANES]


def get_terms(refs, i):
    return [jnp.concatenate([ref[k, pl.ds(8 * i, 8), :] for k in range(ref.shape[0])], axis=1) for ref in refs]


def pair_kernel(tiles, fold, base_ref, seg_rows_ref, seg_cols_ref, col_ids_ref, counts_ref, both_ref, *rest):
    piece_refs = rest[:tiles - 1]
    (grad_ref, row_terms, col_terms, lhs_ref, lhs_end_ref, rhs_ref, rhs_end_ref, terms_end_ref, weight_ref,
     weight_end_ref) = rest[tiles - 1:]
    groups, per, _ = both_ref.shape
    structs = groups * per
    n_rows, n_cols = counts_ref.shape
    piece = n_cols // tiles
    deep = weight_ref.shape[0]
    full = rhs_ref.shape[2]
    end = n_cols - full
    chunks = [(a, min(WIDE, full - a)) for a in range(0, full, WIDE)]

    for norm_row, one_row, refs in ((3, 4, row_terms), (4, 3, col_terms)):
        for ref in refs:
            ref[...] = jnp.zeros_like(ref)
        for k in range(refs[0].shape[0]):
            refs[0][k, pl.ds(one_row, per, 8), :] = jnp.ones((per, LANES), jnp.float32)
    if end:
        rhs_end_ref[...] = jnp.zeros_like(rhs_end_ref)

    def features(g, carry):
        both = both_ref[g]
        parts = [both] + [ref[g] for ref in piece_refs]
        cols = [jnp.concatenate([v[:, c * piece:(c + 1) * piece] for v in parts], axis=1) for c in range(3)]
        rows = [both[:, 3 * piece + c * n_rows:3 * piece + (c + 1) * n_rows] for c in range(3)]
        put_terms(row_terms, rows, 3)
        put_terms(col_terms, cols, 4)
        for block in range(per // fold):
            lefts = []
            for inside in range(fold):
                i = block * fold + inside
                s = g * per + i
                hi, mid, lo = get_terms(row_terms, i)
                left = jnp.concatenate([hi, hi, mid, mid, hi, lo], axis=0)
                lhs_ref[s] = left.T[:deep].astype(jnp.bfloat16)
                if end:
                    lefts += [left, jnp.zeros((SLOT - 48, left.shape[1]), jnp.float32)]
                hi, mid, lo = get_terms(col_terms, i)
                right = jnp.concatenate([hi, mid, hi, mid, lo, hi], axis=0)
                rhs_ref[s] = right[:, :full].astype(jnp.bfloat16)
                if end:
                    lane = lax.broadcasted_iota(jnp.int32, (48, LANES), 1)
                    last = jnp.where(lane < end, right[:, full:full + LANES], 0.0)
                    if inside:
                        last = pltpu.roll(last, inside * end, 1)
                    last = last.astype(jnp.bfloat16)
                    b = g * (per // fold) + block
                    rhs_end_ref[b, pl.ds(SLOT * inside, 48), :] = last
                    terms_end_ref[b, pl.ds(16 * inside, 16), :] = last[0:16]
            if end:
                lhs_end_ref[g * (per // fold) + block] = jnp.concatenate(lefts, axis=0).T[:deep].astype(jnp.bfloat16)
        return carry

    lax.fori_loop(0, groups, features, 0)
    weight_ref[...] = jnp.zeros_like(weight_ref)
    if end:
        weight_end_ref[...] = jnp.zeros_like(weight_end_ref)

    def tanh_block(s, start, size):
        return jnp.tanh(jnp.dot(lhs_ref[s], rhs_ref[s, :, pl.ds(start, size)], preferred_element_type=jnp.float32))

    def tanh_end(b):
        return jnp.tanh(jnp.dot(lhs_end_ref[b], rhs_end_ref[b], preferred_element_type=jnp.float32))

    def add_some(b, carry):
        for inside in range(fold):
            for start, size in chunks:
                weight_ref[:, pl.ds(start, size)] += tanh_block(b * fold + inside, start, size)
        if end:
            weight_end_ref[...] += tanh_end(b)
        return carry

    lax.fori_loop(0, structs // fold, add_some, 0)

    def mask_and_target(start, size):
        count = counts_ref[:, pl.ds(start, size)].astype(jnp.float32)
        row_ids = base_ref[0] + lax.broadcasted_iota(jnp.int32, (n_rows, size), 0)
        mask = jnp.where(seg_rows_ref[...] == seg_cols_ref[:, pl.ds(start, size)], 1.0, 0.3)
        mask = jnp.where(row_ids == col_ids_ref[:, pl.ds(start, size)], 0.0, mask)
        return mask, mask * (count / (count + 8.0))

    scale = 0.5 / structs
    for start, size in chunks:
        mask, goal = mask_and_target(start, size)
        total = weight_ref[pl.ds(0, n_rows), pl.ds(start, size)]
        weight_ref[pl.ds(0, n_rows), pl.ds(start, size)] = mask * (0.5 + scale * total) - goal
    if deep > n_rows:
        weight_ref[pl.ds(n_rows, deep - n_rows), :] = jnp.zeros((deep - n_rows, full), jnp.float32)
    if end:
        def spread(v):
            v = jnp.concatenate([v, jnp.zeros((n_rows, LANES - end), jnp.float32)], axis=1)
            return sum((pltpu.roll(v, k * end, 1) for k in range(1, fold)), v)

        mask, goal = [spread(v) for v in mask_and_target(full, end)]
        part = weight_end_ref[pl.ds(0, n_rows), :]
        total = sum((pltpu.roll(part, k * end, 1) for k in range(1, fold)), part)
        weight_end_ref[pl.ds(0, n_rows), :] = mask * (0.5 + scale * total) - goal
        if deep > n_rows:
            weight_end_ref[pl.ds(n_rows, deep - n_rows), :] = jnp.zeros((deep - n_rows, LANES), jnp.float32)

    def sums(terms, weight, t):
        g = weight * (1.0 - t * t)
        hi = g.astype(jnp.bfloat16)
        lo = (g - hi.astype(jnp.float32)).astype(jnp.bfloat16)
        return (lax.dot_general(terms, hi, NT, preferred_element_type=jnp.float32)
                + lax.dot_general(terms, lo, NT, preferred_element_type=jnp.float32))

    def grad_some(b, carry):
        if end:
            last = sums(terms_end_ref[b], weight_end_ref[...], tanh_end(b))
        for inside in range(fold):
            s = b * fold + inside
            total = last[16 * inside:16 * inside + 16] if end else jnp.zeros((16, deep), jnp.float32)
            for start, size in chunks:
                total += sums(rhs_ref[s, pl.ds(0, 16), pl.ds(start, size)], weight_ref[:, pl.ds(start, size)],
                              tanh_block(s, start, size))
            total = total[:, :n_rows]
            g, i = lax.div(s, per), lax.rem(s, per)
            both = both_ref[g, pl.ds(i, 1), :]
            for c in range(3):
                xyz = both[:, 3 * piece + c * n_rows:3 * piece + (c + 1) * n_rows]
                grad_ref[g, c, pl.ds(i, 1), :] = (0.25 / 16) * (
                    total[c:c + 1] + total[8 + c:9 + c] - total[3:4] * xyz)
        return carry

    lax.fori_loop(0, structs // fold, grad_some, 0)


def split_ens(n_ens, beads, tiles):
    best = None
    for parts in range(1, n_ens + 1):
        if n_ens % parts or beads % parts or beads % (n_ens // parts):
            continue
        cost = 2 * (beads // parts) + tiles * (beads // (n_ens // parts))
        if best is None or cost < best[0]:
            best = (cost, parts)
    return best[1]


def on_device(coords, counts, segments):
    local_n, _, beads = coords.shape
    n_tile = lax.axis_size("tile")
    n_ens = lax.axis_size("ens")
    structs = local_n * n_ens
    n_p = split_ens(n_ens, beads, n_tile)
    n_q = n_ens // n_p
    n_rows, piece = beads // n_p, beads // n_q
    n_cols = piece * n_tile
    tile, ens = lax.axis_index("tile"), lax.axis_index("ens")
    p, q = lax.rem(ens, n_p), lax.div(ens, n_p)
    vmem = pl.BlockSpec(memory_space=pltpu.VMEM)

    send = pl.pallas_call(
        functools.partial(pack_kernel, n_p, n_q),
        out_shape=jax.ShapeDtypeStruct((n_ens, local_n, 3 * (piece + n_rows)), jnp.float32),
        in_specs=[vmem],
        out_specs=vmem,
        name="pack",
    )(jnp.swapaxes(coords, 0, 1))
    both = lax.all_to_all(send, "ens", 0, 0, tiled=True)
    own = both[:, :, :3 * piece]
    pieces = [lax.ppermute(own, "tile", [(t, (t - k) % n_tile) for t in range(n_tile)]) for k in range(1, n_tile)]

    row_base = tile * beads + p * n_rows
    col_bases = [lax.rem(tile + k, n_tile) * beads + q * piece for k in range(n_tile)]
    own_counts = lax.dynamic_slice_in_dim(counts, p * n_rows, n_rows, 0)
    block = jnp.concatenate([lax.dynamic_slice_in_dim(own_counts, b, piece, 1) for b in col_bases], axis=1)
    seg_cols = jnp.concatenate([lax.dynamic_slice_in_dim(segments, b, piece) for b in col_bases])[None, :]
    col_ids = jnp.concatenate([b + jnp.arange(piece, dtype=jnp.int32) for b in col_bases])[None, :]
    seg_rows = lax.dynamic_slice_in_dim(segments, row_base, n_rows)[:, None]

    full = n_cols // LANES * LANES
    end = n_cols - full
    fold = LANES // end if end and LANES % end == 0 and local_n % (LANES // end) == 0 else 1
    deep = up(n_rows, 16)
    row_wide, col_wide = up(n_rows, LANES), up(n_cols, LANES)
    blocks = structs // fold
    grad = pl.pallas_call(
        functools.partial(pair_kernel, n_tile, fold),
        out_shape=jax.ShapeDtypeStruct((n_ens, 3, local_n, n_rows), jnp.float32),
        in_specs=[pl.BlockSpec(memory_space=pltpu.SMEM)] + [vmem] * (4 + n_tile),
        out_specs=vmem,
        scratch_shapes=[
            [pltpu.VMEM((row_wide // LANES, 8 * local_n, LANES), jnp.float32)] * 3,
            [pltpu.VMEM((col_wide // LANES, 8 * local_n, LANES), jnp.float32)] * 3,
            pltpu.VMEM((structs, deep, 48), jnp.bfloat16),
            pltpu.VMEM((blocks, deep, fold * SLOT), jnp.bfloat16),
            pltpu.VMEM((structs, 48, full), jnp.bfloat16),
            pltpu.VMEM((blocks, fold * SLOT, LANES), jnp.bfloat16),
            pltpu.VMEM((blocks, fold * 16, LANES), jnp.bfloat16),
            pltpu.VMEM((deep, full), jnp.float32),
            pltpu.VMEM((deep, LANES), jnp.float32),
        ],
        compiler_params=pltpu.CompilerParams(vmem_limit_bytes=48 << 20),
        name="pairs",
    )(row_base[None], seg_rows, seg_cols, col_ids, block, both, *pieces)

    back = lax.all_to_all(grad, "ens", 0, 0, tiled=True)
    total = pl.pallas_call(
        functools.partial(sum_kernel, n_p, n_q),
        out_shape=jax.ShapeDtypeStruct((3, local_n, beads), jnp.float32),
        in_specs=[vmem],
        out_specs=vmem,
        name="total",
    )(back)
    return jnp.swapaxes(total, 0, 1)


def solution(mesh):
    return jax.shard_map(
        on_device,
        mesh=mesh,
        in_specs=(P("ens", None, "tile"), P("tile", None), P()),
        out_specs=P("ens", None, "tile"),
        check_vma=False,
    )
```

```python
import functools

import jax
import jax.numpy as jnp
from jax import lax
from jax.experimental import pallas as pl
from jax.experimental.pallas import tpu as pltpu
from jax.sharding import PartitionSpec as P

LANES = 128
WIDE = 256
SLOT = 64
NT = (((1,), (1,)), ((), ()))


def up(n, unit):
    return -(-n // unit) * unit


def split3(v):
    hi = v.astype(jnp.bfloat16).astype(jnp.float32)
    rest = v - hi
    mid = rest.astype(jnp.bfloat16).astype(jnp.float32)
    return hi, mid, rest - mid


def pack_kernel(n_p, n_q, xyz_ref, send_ref):
    beads = xyz_ref.shape[2]
    n_rows, piece = beads // n_p, beads // n_q
    for c in range(3):
        for q in range(n_q):
            for p in range(n_p):
                e = q * n_p + p
                send_ref[e, :, pl.ds(c * piece, piece)] = xyz_ref[c, :, pl.ds(q * piece, piece)]
                send_ref[e, :, pl.ds(3 * piece + c * n_rows, n_rows)] = xyz_ref[c, :, pl.ds(p * n_rows, n_rows)]


def sum_kernel(n_p, n_q, back_ref, total_ref):
    n_rows = back_ref.shape[3]
    for c in range(3):
        for p in range(n_p):
            total = back_ref[p, c]
            for q in range(1, n_q):
                total += back_ref[q * n_p + p, c]
            total_ref[c, :, pl.ds(p * n_rows, n_rows)] = total


def put_terms(refs, xyz, norm_row):
    norm = 1.5 - 0.5 * (xyz[0] * xyz[0] + xyz[1] * xyz[1] + xyz[2] * xyz[2])
    n, size = norm.shape
    wide = refs[0].shape[0] * LANES
    for f, v in ((0, xyz[0]), (1, xyz[1]), (2, xyz[2]), (norm_row, norm)):
        if wide > size:
            v = jnp.concatenate([v, jnp.zeros((n, wide - size), jnp.float32)], axis=1)
        for ref, term in zip(refs, split3(v)):
            for k in range(wide // LANES):
                ref[k, pl.ds(f, n, 8), :] = term[:, k * LANES:(k + 1) * LANES]


def get_terms(refs, i):
    return [jnp.concatenate([ref[k, pl.ds(8 * i, 8), :] for k in range(ref.shape[0])], axis=1) for ref in refs]


def init_terms(refs, one_row, per):
    for ref in refs:
        ref[...] = jnp.zeros_like(ref)
    for k in range(refs[0].shape[0]):
        refs[0][k, pl.ds(one_row, per, 8), :] = jnp.ones((per, LANES), jnp.float32)


def tanh_product(left, right):
    return jnp.tanh(jnp.dot(left, right, preferred_element_type=jnp.float32))


def row_kernel(n_rows, piece, fold, both_ref, lhs_ref, lhs_end_ref, first_ref, row_terms, col_terms, rhs_ref):
    groups, per, _ = both_ref.shape
    deep = first_ref.shape[0]
    init_terms(row_terms, 4, per)
    init_terms(col_terms, 3, per)

    def features(g, carry):
        both = both_ref[g]
        put_terms(row_terms, [both[:, 3 * piece + c * n_rows:3 * piece + (c + 1) * n_rows] for c in range(3)], 3)
        put_terms(col_terms, [both[:, c * piece:c * piece + LANES] for c in range(3)], 4)
        for block in range(per // fold):
            lefts = []
            for inside in range(fold):
                i = block * fold + inside
                hi, mid, lo = get_terms(row_terms, i)
                left = jnp.concatenate([hi, hi, mid, mid, hi, lo], axis=0)
                lhs_ref[g * per + i] = left.T[:deep].astype(jnp.bfloat16)
                lefts += [left, jnp.zeros((SLOT - 48, left.shape[1]), jnp.float32)]
                hi, mid, lo = get_terms(col_terms, i)
                rhs_ref[g * per + i] = jnp.concatenate([hi, mid, hi, mid, lo, hi], axis=0).astype(jnp.bfloat16)
            lhs_end_ref[g * (per // fold) + block] = jnp.concatenate(lefts, axis=0).T[:deep].astype(jnp.bfloat16)
        return carry

    lax.fori_loop(0, groups, features, 0)
    first_ref[...] = jnp.zeros_like(first_ref)

    def add_one(s, carry):
        first_ref[...] += tanh_product(lhs_ref[s], rhs_ref[s])
        return carry

    lax.fori_loop(0, groups * per, add_one, 0, unroll=8)


def pair_kernel(tiles, fold, head, base_ref, seg_rows_ref, seg_cols_ref, col_ids_ref, counts_ref, lhs_ref,
                lhs_end_ref, first_ref, both_ref, *rest):
    piece_refs = rest[:tiles - 1]
    grad_ref, col_terms, rhs_ref, rhs_end_ref, terms_end_ref, weight_ref, weight_end_ref = rest[tiles - 1:]
    groups, per, _ = both_ref.shape
    structs = groups * per
    n_rows, n_cols = counts_ref.shape
    piece = n_cols // tiles
    deep = weight_ref.shape[0]
    full = rhs_ref.shape[2]
    end = n_cols - full
    chunks = [(a, min(WIDE, full - a)) for a in range(0, full, WIDE)]
    tail = [(a, min(WIDE, full - a)) for a in range(head, full, WIDE)]

    init_terms(col_terms, 3, per)
    if end:
        rhs_end_ref[...] = jnp.zeros_like(rhs_end_ref)

    def features(g, carry):
        both = both_ref[g]
        parts = [both] + [ref[g] for ref in piece_refs]
        cols = [jnp.concatenate([v[:, c * piece:(c + 1) * piece] for v in parts], axis=1) for c in range(3)]
        put_terms(col_terms, cols, 4)
        for block in range(per // fold):
            for inside in range(fold):
                i = block * fold + inside
                s = g * per + i
                hi, mid, lo = get_terms(col_terms, i)
                right = jnp.concatenate([hi, mid, hi, mid, lo, hi], axis=0)
                rhs_ref[s] = right[:, :full].astype(jnp.bfloat16)
                if end:
                    lane = lax.broadcasted_iota(jnp.int32, (48, LANES), 1)
                    last = jnp.where(lane < end, right[:, full:full + LANES], 0.0)
                    if inside:
                        last = pltpu.roll(last, inside * end, 1)
                    last = last.astype(jnp.bfloat16)
                    b = g * (per // fold) + block
                    rhs_end_ref[b, pl.ds(SLOT * inside, 48), :] = last
                    terms_end_ref[b, pl.ds(16 * inside, 16), :] = last[0:16]
        return carry

    lax.fori_loop(0, groups, features, 0)
    weight_ref[...] = jnp.zeros_like(weight_ref)
    if head:
        weight_ref[:, pl.ds(0, head)] = first_ref[...]
    if end:
        weight_end_ref[...] = jnp.zeros_like(weight_end_ref)

    def tanh_block(s, start, size):
        return tanh_product(lhs_ref[s], rhs_ref[s, :, pl.ds(start, size)])

    def tanh_end(b):
        return tanh_product(lhs_end_ref[b], rhs_end_ref[b])

    def add_some(b, carry):
        for inside in range(fold):
            for start, size in tail:
                weight_ref[:, pl.ds(start, size)] += tanh_block(b * fold + inside, start, size)
        if end:
            weight_end_ref[...] += tanh_end(b)
        return carry

    lax.fori_loop(0, structs // fold, add_some, 0)

    def mask_and_target(start, size):
        count = counts_ref[:, pl.ds(start, size)].astype(jnp.float32)
        row_ids = base_ref[0] + lax.broadcasted_iota(jnp.int32, (n_rows, size), 0)
        mask = jnp.where(seg_rows_ref[...] == seg_cols_ref[:, pl.ds(start, size)], 1.0, 0.3)
        mask = jnp.where(row_ids == col_ids_ref[:, pl.ds(start, size)], 0.0, mask)
        return mask, mask * (count / (count + 8.0))

    scale = 0.5 / structs
    for start, size in chunks:
        mask, goal = mask_and_target(start, size)
        total = weight_ref[pl.ds(0, n_rows), pl.ds(start, size)]
        weight_ref[pl.ds(0, n_rows), pl.ds(start, size)] = mask * (0.5 + scale * total) - goal
    if deep > n_rows:
        weight_ref[pl.ds(n_rows, deep - n_rows), :] = jnp.zeros((deep - n_rows, full), jnp.float32)
    if end:
        def spread(v):
            v = jnp.concatenate([v, jnp.zeros((n_rows, LANES - end), jnp.float32)], axis=1)
            return sum((pltpu.roll(v, k * end, 1) for k in range(1, fold)), v)

        mask, goal = [spread(v) for v in mask_and_target(full, end)]
        part = weight_end_ref[pl.ds(0, n_rows), :]
        total = sum((pltpu.roll(part, k * end, 1) for k in range(1, fold)), part)
        weight_end_ref[pl.ds(0, n_rows), :] = mask * (0.5 + scale * total) - goal
        if deep > n_rows:
            weight_end_ref[pl.ds(n_rows, deep - n_rows), :] = jnp.zeros((deep - n_rows, LANES), jnp.float32)

    def sums(terms, weight, t):
        g = weight * (1.0 - t * t)
        hi = g.astype(jnp.bfloat16)
        lo = (g - hi.astype(jnp.float32)).astype(jnp.bfloat16)
        return (lax.dot_general(terms, hi, NT, preferred_element_type=jnp.float32)
                + lax.dot_general(terms, lo, NT, preferred_element_type=jnp.float32))

    def grad_some(b, carry):
        if end:
            last = sums(terms_end_ref[b], weight_end_ref[...], tanh_end(b))
        for inside in range(fold):
            s = b * fold + inside
            total = last[16 * inside:16 * inside + 16] if end else jnp.zeros((16, deep), jnp.float32)
            for start, size in chunks:
                total += sums(rhs_ref[s, pl.ds(0, 16), pl.ds(start, size)], weight_ref[:, pl.ds(start, size)],
                              tanh_block(s, start, size))
            total = total[:, :n_rows]
            g, i = lax.div(s, per), lax.rem(s, per)
            both = both_ref[g, pl.ds(i, 1), :]
            for c in range(3):
                xyz = both[:, 3 * piece + c * n_rows:3 * piece + (c + 1) * n_rows]
                grad_ref[g, c, pl.ds(i, 1), :] = (0.25 / 16) * (
                    total[c:c + 1] + total[8 + c:9 + c] - total[3:4] * xyz)
        return carry

    lax.fori_loop(0, structs // fold, grad_some, 0)


def split_ens(n_ens, beads, tiles):
    best = None
    for parts in range(1, n_ens + 1):
        if n_ens % parts or beads % parts or beads % (n_ens // parts):
            continue
        cost = 2 * (beads // parts) + tiles * (beads // (n_ens // parts))
        if best is None or cost < best[0]:
            best = (cost, parts)
    return best[1]


def on_device(coords, counts, segments):
    local_n, _, beads = coords.shape
    n_tile = lax.axis_size("tile")
    n_ens = lax.axis_size("ens")
    structs = local_n * n_ens
    n_p = split_ens(n_ens, beads, n_tile)
    n_q = n_ens // n_p
    n_rows, piece = beads // n_p, beads // n_q
    n_cols = piece * n_tile
    tile, ens = lax.axis_index("tile"), lax.axis_index("ens")
    p, q = lax.rem(ens, n_p), lax.div(ens, n_p)
    vmem = pl.BlockSpec(memory_space=pltpu.VMEM)

    send = pl.pallas_call(
        functools.partial(pack_kernel, n_p, n_q),
        out_shape=jax.ShapeDtypeStruct((n_ens, local_n, 3 * (piece + n_rows)), jnp.float32),
        in_specs=[vmem],
        out_specs=vmem,
        name="pack",
    )(jnp.swapaxes(coords, 0, 1))
    both = lax.all_to_all(send, "ens", 0, 0, tiled=True)
    own = both[:, :, :3 * piece]
    pieces = [lax.ppermute(own, "tile", [(t, (t - k) % n_tile) for t in range(n_tile)]) for k in range(1, n_tile)]

    row_base = tile * beads + p * n_rows
    col_bases = [lax.rem(tile + k, n_tile) * beads + q * piece for k in range(n_tile)]
    own_counts = lax.dynamic_slice_in_dim(counts, p * n_rows, n_rows, 0)
    block = jnp.concatenate([lax.dynamic_slice_in_dim(own_counts, b, piece, 1) for b in col_bases], axis=1)
    seg_cols = jnp.concatenate([lax.dynamic_slice_in_dim(segments, b, piece) for b in col_bases])[None, :]
    col_ids = jnp.concatenate([b + jnp.arange(piece, dtype=jnp.int32) for b in col_bases])[None, :]
    seg_rows = lax.dynamic_slice_in_dim(segments, row_base, n_rows)[:, None]

    full = n_cols // LANES * LANES
    end = n_cols - full
    fold = LANES // end if end and LANES % end == 0 and local_n % (LANES // end) == 0 else 1
    deep = up(n_rows, 16)
    row_wide, col_wide = up(n_rows, LANES), up(n_cols, LANES)
    blocks = structs // fold
    head = LANES if piece >= LANES else 0
    lhs, lhs_end, first = pl.pallas_call(
        functools.partial(row_kernel, n_rows, piece, fold),
        out_shape=[
            jax.ShapeDtypeStruct((structs, deep, 48), jnp.bfloat16),
            jax.ShapeDtypeStruct((blocks, deep, fold * SLOT), jnp.bfloat16),
            jax.ShapeDtypeStruct((deep, LANES), jnp.float32),
        ],
        in_specs=[vmem],
        out_specs=[vmem] * 3,
        scratch_shapes=[
            [pltpu.VMEM((row_wide // LANES, 8 * local_n, LANES), jnp.float32)] * 3,
            [pltpu.VMEM((1, 8 * local_n, LANES), jnp.float32)] * 3,
            pltpu.VMEM((structs, 48, LANES), jnp.bfloat16),
        ],
        compiler_params=pltpu.CompilerParams(vmem_limit_bytes=32 << 20),
        name="rows",
    )(both)
    grad = pl.pallas_call(
        functools.partial(pair_kernel, n_tile, fold, head),
        out_shape=jax.ShapeDtypeStruct((n_ens, 3, local_n, n_rows), jnp.float32),
        in_specs=[pl.BlockSpec(memory_space=pltpu.SMEM)] + [vmem] * (7 + n_tile),
        out_specs=vmem,
        scratch_shapes=[
            [pltpu.VMEM((col_wide // LANES, 8 * local_n, LANES), jnp.float32)] * 3,
            pltpu.VMEM((structs, 48, full), jnp.bfloat16),
            pltpu.VMEM((blocks, fold * SLOT, LANES), jnp.bfloat16),
            pltpu.VMEM((blocks, fold * 16, LANES), jnp.bfloat16),
            pltpu.VMEM((deep, full), jnp.float32),
            pltpu.VMEM((deep, LANES), jnp.float32),
        ],
        compiler_params=pltpu.CompilerParams(vmem_limit_bytes=40 << 20),
        name="pairs",
    )(row_base[None], seg_rows, seg_cols, col_ids, block, lhs, lhs_end, first, both, *pieces)

    back = lax.all_to_all(grad, "ens", 0, 0, tiled=True)
    total = pl.pallas_call(
        functools.partial(sum_kernel, n_p, n_q),
        out_shape=jax.ShapeDtypeStruct((3, local_n, beads), jnp.float32),
        in_specs=[vmem],
        out_specs=vmem,
        name="total",
    )(back)
    return jnp.swapaxes(total, 0, 1)


def solution(mesh):
    return jax.shard_map(
        on_device,
        mesh=mesh,
        in_specs=(P("ens", None, "tile"), P("tile", None), P()),
        out_specs=P("ens", None, "tile"),
        check_vma=False,
    )
```

```python
import functools

import jax
import jax.numpy as jnp
from jax import lax
from jax.experimental import pallas as pl
from jax.experimental.pallas import tpu as pltpu
from jax.sharding import PartitionSpec as P

LANES = 128
WIDE = 256
SLOT = 64
NT = (((1,), (1,)), ((), ()))


def up(n, unit):
    return -(-n // unit) * unit


def split3(v):
    hi = v.astype(jnp.bfloat16).astype(jnp.float32)
    rest = v - hi
    mid = rest.astype(jnp.bfloat16).astype(jnp.float32)
    return hi, mid, rest - mid


def pack_kernel(n_p, n_q, xyz_ref, send_ref):
    beads = xyz_ref.shape[2]
    n_rows, piece = beads // n_p, beads // n_q
    for c in range(3):
        for q in range(n_q):
            for p in range(n_p):
                e = q * n_p + p
                send_ref[e, :, pl.ds(c * piece, piece)] = xyz_ref[c, :, pl.ds(q * piece, piece)]
                send_ref[e, :, pl.ds(3 * piece + c * n_rows, n_rows)] = xyz_ref[c, :, pl.ds(p * n_rows, n_rows)]


def sum_kernel(n_p, n_q, back_ref, total_ref):
    n_rows = back_ref.shape[3]
    for c in range(3):
        for p in range(n_p):
            total = back_ref[p, c]
            for q in range(1, n_q):
                total += back_ref[q * n_p + p, c]
            total_ref[c, :, pl.ds(p * n_rows, n_rows)] = total


def put_terms(refs, xyz, norm_row):
    norm = 1.5 - 0.5 * (xyz[0] * xyz[0] + xyz[1] * xyz[1] + xyz[2] * xyz[2])
    n, size = norm.shape
    wide = refs[0].shape[0] * LANES
    for f, v in ((0, xyz[0]), (1, xyz[1]), (2, xyz[2]), (norm_row, norm)):
        if wide > size:
            v = jnp.concatenate([v, jnp.zeros((n, wide - size), jnp.float32)], axis=1)
        for ref, term in zip(refs, split3(v)):
            for k in range(wide // LANES):
                ref[k, pl.ds(f, n, 8), :] = term[:, k * LANES:(k + 1) * LANES]


def get_terms(refs, i):
    return [jnp.concatenate([ref[k, pl.ds(8 * i, 8), :] for k in range(ref.shape[0])], axis=1) for ref in refs]


def pair_kernel(tiles, fold, base_ref, seg_rows_ref, seg_cols_ref, col_ids_ref, counts_ref, both_ref, *rest):
    piece_refs = rest[:tiles - 1]
    (grad_ref, row_terms, col_terms, lhs_ref, lhs_end_ref, rhs_ref, rhs_end_ref, terms_end_ref, weight_ref,
     weight_end_ref) = rest[tiles - 1:]
    groups, per, _ = both_ref.shape
    structs = groups * per
    n_rows, n_cols = counts_ref.shape
    piece = n_cols // tiles
    deep = weight_ref.shape[0]
    full = rhs_ref.shape[2]
    end = n_cols - full
    chunks = [(a, min(WIDE, full - a)) for a in range(0, full, WIDE)]

    for norm_row, one_row, refs in ((3, 4, row_terms), (4, 3, col_terms)):
        for ref in refs:
            ref[...] = jnp.zeros_like(ref)
        for k in range(refs[0].shape[0]):
            refs[0][k, pl.ds(one_row, per, 8), :] = jnp.ones((per, LANES), jnp.float32)
    if end:
        rhs_end_ref[...] = jnp.zeros_like(rhs_end_ref)

    def features(g, carry):
        both = both_ref[g]
        parts = [both] + [ref[g] for ref in piece_refs]
        cols = [jnp.concatenate([v[:, c * piece:(c + 1) * piece] for v in parts], axis=1) for c in range(3)]
        rows = [both[:, 3 * piece + c * n_rows:3 * piece + (c + 1) * n_rows] for c in range(3)]
        put_terms(row_terms, rows, 3)
        put_terms(col_terms, cols, 4)
        for block in range(per // fold):
            lefts = []
            for inside in range(fold):
                i = block * fold + inside
                s = g * per + i
                hi, mid, lo = get_terms(row_terms, i)
                left = jnp.concatenate([hi, hi, mid, mid, hi, lo], axis=0)
                lhs_ref[s] = left.T[:deep].astype(jnp.bfloat16)
                if end:
                    lefts += [left, jnp.zeros((SLOT - 48, left.shape[1]), jnp.float32)]
                hi, mid, lo = get_terms(col_terms, i)
                right = jnp.concatenate([hi, mid, hi, mid, lo, hi], axis=0)
                rhs_ref[s] = right[:, :full].astype(jnp.bfloat16)
                if end:
                    lane = lax.broadcasted_iota(jnp.int32, (48, LANES), 1)
                    last = jnp.where(lane < end, right[:, full:full + LANES], 0.0)
                    if inside:
                        last = pltpu.roll(last, inside * end, 1)
                    last = last.astype(jnp.bfloat16)
                    b = g * (per // fold) + block
                    rhs_end_ref[b, pl.ds(SLOT * inside, 48), :] = last
                    terms_end_ref[b, pl.ds(16 * inside, 16), :] = last[0:16]
            if end:
                lhs_end_ref[g * (per // fold) + block] = jnp.concatenate(lefts, axis=0).T[:deep].astype(jnp.bfloat16)
        return carry

    lax.fori_loop(0, groups, features, 0)
    weight_ref[...] = jnp.zeros_like(weight_ref)
    if end:
        weight_end_ref[...] = jnp.zeros_like(weight_end_ref)

    def tanh_block(s, start, size):
        return jnp.tanh(jnp.dot(lhs_ref[s], rhs_ref[s, :, pl.ds(start, size)], preferred_element_type=jnp.float32))

    def tanh_end(b):
        return jnp.tanh(jnp.dot(lhs_end_ref[b], rhs_end_ref[b], preferred_element_type=jnp.float32))

    def add_some(b, carry):
        for inside in range(fold):
            for start, size in chunks:
                weight_ref[:, pl.ds(start, size)] += tanh_block(b * fold + inside, start, size)
        if end:
            weight_end_ref[...] += tanh_end(b)
        return carry

    lax.fori_loop(0, structs // fold, add_some, 0)

    def mask_and_target(start, size):
        count = counts_ref[:, pl.ds(start, size)].astype(jnp.float32)
        row_ids = base_ref[0] + lax.broadcasted_iota(jnp.int32, (n_rows, size), 0)
        mask = jnp.where(seg_rows_ref[...] == seg_cols_ref[:, pl.ds(start, size)], 1.0, 0.3)
        mask = jnp.where(row_ids == col_ids_ref[:, pl.ds(start, size)], 0.0, mask)
        return mask, mask * (count / (count + 8.0))

    scale = 0.5 / structs
    for start, size in chunks:
        mask, goal = mask_and_target(start, size)
        total = weight_ref[pl.ds(0, n_rows), pl.ds(start, size)]
        weight_ref[pl.ds(0, n_rows), pl.ds(start, size)] = mask * (0.5 + scale * total) - goal
    if deep > n_rows:
        weight_ref[pl.ds(n_rows, deep - n_rows), :] = jnp.zeros((deep - n_rows, full), jnp.float32)
    if end:
        def spread(v):
            v = jnp.concatenate([v, jnp.zeros((n_rows, LANES - end), jnp.float32)], axis=1)
            return sum((pltpu.roll(v, k * end, 1) for k in range(1, fold)), v)

        mask, goal = [spread(v) for v in mask_and_target(full, end)]
        part = weight_end_ref[pl.ds(0, n_rows), :]
        total = sum((pltpu.roll(part, k * end, 1) for k in range(1, fold)), part)
        weight_end_ref[pl.ds(0, n_rows), :] = mask * (0.5 + scale * total) - goal
        if deep > n_rows:
            weight_end_ref[pl.ds(n_rows, deep - n_rows), :] = jnp.zeros((deep - n_rows, LANES), jnp.float32)

    def sums(terms, weight, t):
        g = weight * (1.0 - t * t)
        hi = g.astype(jnp.bfloat16)
        lo = (g - hi.astype(jnp.float32)).astype(jnp.bfloat16)
        return (lax.dot_general(hi, terms, NT, preferred_element_type=jnp.float32)
                + lax.dot_general(lo, terms, NT, preferred_element_type=jnp.float32))

    def grad_some(b, carry):
        if end:
            last = sums(terms_end_ref[b], weight_end_ref[...], tanh_end(b)).T
        for inside in range(fold):
            s = b * fold + inside
            total = jnp.zeros((deep, 16), jnp.float32)
            for start, size in chunks:
                total += sums(rhs_ref[s, pl.ds(0, 16), pl.ds(start, size)], weight_ref[:, pl.ds(start, size)],
                              tanh_block(s, start, size))
            total = total.T
            if end:
                total += last[16 * inside:16 * inside + 16]
            total = total[:, :n_rows]
            g, i = lax.div(s, per), lax.rem(s, per)
            both = both_ref[g, pl.ds(i, 1), :]
            for c in range(3):
                xyz = both[:, 3 * piece + c * n_rows:3 * piece + (c + 1) * n_rows]
                grad_ref[g, c, pl.ds(i, 1), :] = (0.25 / 16) * (
                    total[c:c + 1] + total[8 + c:9 + c] - total[3:4] * xyz)
        return carry

    lax.fori_loop(0, structs // fold, grad_some, 0)


def split_ens(n_ens, beads, tiles):
    best = None
    for parts in range(1, n_ens + 1):
        if n_ens % parts or beads % parts or beads % (n_ens // parts):
            continue
        cost = 2 * (beads // parts) + tiles * (beads // (n_ens // parts))
        if best is None or cost < best[0]:
            best = (cost, parts)
    return best[1]


def on_device(coords, counts, segments):
    local_n, _, beads = coords.shape
    n_tile = lax.axis_size("tile")
    n_ens = lax.axis_size("ens")
    structs = local_n * n_ens
    n_p = split_ens(n_ens, beads, n_tile)
    n_q = n_ens // n_p
    n_rows, piece = beads // n_p, beads // n_q
    n_cols = piece * n_tile
    tile, ens = lax.axis_index("tile"), lax.axis_index("ens")
    p, q = lax.rem(ens, n_p), lax.div(ens, n_p)
    vmem = pl.BlockSpec(memory_space=pltpu.VMEM)

    send = pl.pallas_call(
        functools.partial(pack_kernel, n_p, n_q),
        out_shape=jax.ShapeDtypeStruct((n_ens, local_n, 3 * (piece + n_rows)), jnp.float32),
        in_specs=[vmem],
        out_specs=vmem,
        name="pack",
    )(jnp.swapaxes(coords, 0, 1))
    both = lax.all_to_all(send, "ens", 0, 0, tiled=True)
    own = both[:, :, :3 * piece]
    pieces = [lax.ppermute(own, "tile", [(t, (t - k) % n_tile) for t in range(n_tile)]) for k in range(1, n_tile)]

    row_base = tile * beads + p * n_rows
    col_bases = [lax.rem(tile + k, n_tile) * beads + q * piece for k in range(n_tile)]
    own_counts = lax.dynamic_slice_in_dim(counts, p * n_rows, n_rows, 0)
    block = jnp.concatenate([lax.dynamic_slice_in_dim(own_counts, b, piece, 1) for b in col_bases], axis=1)
    seg_cols = jnp.concatenate([lax.dynamic_slice_in_dim(segments, b, piece) for b in col_bases])[None, :]
    col_ids = jnp.concatenate([b + jnp.arange(piece, dtype=jnp.int32) for b in col_bases])[None, :]
    seg_rows = lax.dynamic_slice_in_dim(segments, row_base, n_rows)[:, None]

    full = n_cols // LANES * LANES
    end = n_cols - full
    fold = LANES // end if end and LANES % end == 0 and local_n % (LANES // end) == 0 else 1
    deep = up(n_rows, 16)
    row_wide, col_wide = up(n_rows, LANES), up(n_cols, LANES)
    blocks = structs // fold
    grad = pl.pallas_call(
        functools.partial(pair_kernel, n_tile, fold),
        out_shape=jax.ShapeDtypeStruct((n_ens, 3, local_n, n_rows), jnp.float32),
        in_specs=[pl.BlockSpec(memory_space=pltpu.SMEM)] + [vmem] * (4 + n_tile),
        out_specs=vmem,
        scratch_shapes=[
            [pltpu.VMEM((row_wide // LANES, 8 * local_n, LANES), jnp.float32)] * 3,
            [pltpu.VMEM((col_wide // LANES, 8 * local_n, LANES), jnp.float32)] * 3,
            pltpu.VMEM((structs, deep, 48), jnp.bfloat16),
            pltpu.VMEM((blocks, deep, fold * SLOT), jnp.bfloat16),
            pltpu.VMEM((structs, 48, full), jnp.bfloat16),
            pltpu.VMEM((blocks, fold * SLOT, LANES), jnp.bfloat16),
            pltpu.VMEM((blocks, fold * 16, LANES), jnp.bfloat16),
            pltpu.VMEM((deep, full), jnp.float32),
            pltpu.VMEM((deep, LANES), jnp.float32),
        ],
        compiler_params=pltpu.CompilerParams(vmem_limit_bytes=48 << 20),
        name="pairs",
    )(row_base[None], seg_rows, seg_cols, col_ids, block, both, *pieces)

    back = lax.all_to_all(grad, "ens", 0, 0, tiled=True)
    total = pl.pallas_call(
        functools.partial(sum_kernel, n_p, n_q),
        out_shape=jax.ShapeDtypeStruct((3, local_n, beads), jnp.float32),
        in_specs=[vmem],
        out_specs=vmem,
        name="total",
    )(back)
    return jnp.swapaxes(total, 0, 1)


def solution(mesh):
    return jax.shard_map(
        on_device,
        mesh=mesh,
        in_specs=(P("ens", None, "tile"), P("tile", None), P()),
        out_specs=P("ens", None, "tile"),
        check_vma=False,
    )
```

```python
import functools

import jax
import jax.numpy as jnp
from jax import lax
from jax.experimental import pallas as pl
from jax.experimental.pallas import tpu as pltpu
from jax.sharding import PartitionSpec as P

LANES = 128
WIDE = 256
SLOT = 64
NT = (((1,), (1,)), ((), ()))


def up(n, unit):
    return -(-n // unit) * unit


def split3(v):
    hi = v.astype(jnp.bfloat16).astype(jnp.float32)
    rest = v - hi
    mid = rest.astype(jnp.bfloat16).astype(jnp.float32)
    return hi, mid, rest - mid


def pack_kernel(n_p, n_q, xyz_ref, send_ref):
    beads = xyz_ref.shape[2]
    n_rows, piece = beads // n_p, beads // n_q
    for c in range(3):
        for q in range(n_q):
            for p in range(n_p):
                e = q * n_p + p
                send_ref[e, :, pl.ds(c * piece, piece)] = xyz_ref[c, :, pl.ds(q * piece, piece)]
                send_ref[e, :, pl.ds(3 * piece + c * n_rows, n_rows)] = xyz_ref[c, :, pl.ds(p * n_rows, n_rows)]


def sum_kernel(n_p, n_q, back_ref, total_ref):
    n_rows = back_ref.shape[3]
    for c in range(3):
        for p in range(n_p):
            total = back_ref[p, c]
            for q in range(1, n_q):
                total += back_ref[q * n_p + p, c]
            total_ref[c, :, pl.ds(p * n_rows, n_rows)] = total


def put_terms(refs, xyz, norm_row):
    norm = 1.5 - 0.5 * (xyz[0] * xyz[0] + xyz[1] * xyz[1] + xyz[2] * xyz[2])
    n, size = norm.shape
    wide = refs[0].shape[0] * LANES
    for f, v in ((0, xyz[0]), (1, xyz[1]), (2, xyz[2]), (norm_row, norm)):
        if wide > size:
            v = jnp.concatenate([v, jnp.zeros((n, wide - size), jnp.float32)], axis=1)
        for ref, term in zip(refs, split3(v)):
            for k in range(wide // LANES):
                ref[k, pl.ds(f, n, 8), :] = term[:, k * LANES:(k + 1) * LANES]


def get_terms(refs, i):
    return [jnp.concatenate([ref[k, pl.ds(8 * i, 8), :] for k in range(ref.shape[0])], axis=1) for ref in refs]


def pair_kernel(tiles, fold, base_ref, seg_rows_ref, seg_cols_ref, col_ids_ref, counts_ref, both_ref, *rest):
    piece_refs = rest[:tiles - 1]
    (grad_ref, row_terms, col_terms, lhs_ref, lhs_end_ref, rhs_ref, rhs_end_ref, terms_end_ref, weight_ref,
     weight_end_ref) = rest[tiles - 1:]
    groups, per, _ = both_ref.shape
    structs = groups * per
    n_rows, n_cols = counts_ref.shape
    piece = n_cols // tiles
    deep = weight_ref.shape[0]
    full = rhs_ref.shape[2]
    end = n_cols - full
    chunks = [(a, min(WIDE, full - a)) for a in range(0, full, WIDE)]

    for norm_row, one_row, refs in ((3, 4, row_terms), (4, 3, col_terms)):
        for ref in refs:
            ref[...] = jnp.zeros_like(ref)
        for k in range(refs[0].shape[0]):
            refs[0][k, pl.ds(one_row, per, 8), :] = jnp.ones((per, LANES), jnp.float32)
    if end:
        rhs_end_ref[...] = jnp.zeros_like(rhs_end_ref)

    def features(g, carry):
        both = both_ref[g]
        parts = [both] + [ref[g] for ref in piece_refs]
        cols = [jnp.concatenate([v[:, c * piece:(c + 1) * piece] for v in parts], axis=1) for c in range(3)]
        rows = [both[:, 3 * piece + c * n_rows:3 * piece + (c + 1) * n_rows] for c in range(3)]
        put_terms(row_terms, rows, 3)
        put_terms(col_terms, cols, 4)
        for block in range(per // fold):
            lefts = []
            for inside in range(fold):
                i = block * fold + inside
                s = g * per + i
                hi, mid, lo = get_terms(row_terms, i)
                left = jnp.concatenate([hi, hi, mid, mid, hi, lo], axis=0)
                lhs_ref[s] = left.T[:deep].astype(jnp.bfloat16)
                if end:
                    lefts += [left, jnp.zeros((SLOT - 48, left.shape[1]), jnp.float32)]
                hi, mid, lo = get_terms(col_terms, i)
                right = jnp.concatenate([hi, mid, hi, mid, lo, hi], axis=0)
                rhs_ref[s] = right[:, :full].astype(jnp.bfloat16)
                if end:
                    lane = lax.broadcasted_iota(jnp.int32, (48, LANES), 1)
                    last = jnp.where(lane < end, right[:, full:full + LANES], 0.0)
                    if inside:
                        last = pltpu.roll(last, inside * end, 1)
                    last = last.astype(jnp.bfloat16)
                    b = g * (per // fold) + block
                    rhs_end_ref[b, pl.ds(SLOT * inside, 48), :] = last
                    terms_end_ref[b, pl.ds(16 * inside, 16), :] = last[0:16]
            if end:
                lhs_end_ref[g * (per // fold) + block] = jnp.concatenate(lefts, axis=0).T[:deep].astype(jnp.bfloat16)
        return carry

    lax.fori_loop(0, groups, features, 0)
    weight_ref[...] = jnp.zeros_like(weight_ref)
    if end:
        weight_end_ref[...] = jnp.zeros_like(weight_end_ref)

    def tanh_block(s, start, size):
        return jnp.tanh(jnp.dot(lhs_ref[s], rhs_ref[s, :, pl.ds(start, size)], preferred_element_type=jnp.float32))

    def tanh_end(b):
        return jnp.tanh(jnp.dot(lhs_end_ref[b], rhs_end_ref[b], preferred_element_type=jnp.float32))

    def add_some(b, carry):
        for inside in range(fold):
            for start, size in chunks:
                weight_ref[:, pl.ds(start, size)] += tanh_block(b * fold + inside, start, size)
        if end:
            weight_end_ref[...] += tanh_end(b)
        return carry

    lax.fori_loop(0, structs // fold, add_some, 0)

    def mask_and_target(start, size):
        count = counts_ref[:, pl.ds(start, size)].astype(jnp.float32)
        row_ids = base_ref[0] + lax.broadcasted_iota(jnp.int32, (n_rows, size), 0)
        mask = jnp.where(seg_rows_ref[...] == seg_cols_ref[:, pl.ds(start, size)], 1.0, 0.3)
        mask = jnp.where(row_ids == col_ids_ref[:, pl.ds(start, size)], 0.0, mask)
        return mask, mask * (count / (count + 8.0))

    scale = 0.5 / structs
    for start, size in chunks:
        mask, goal = mask_and_target(start, size)
        total = weight_ref[pl.ds(0, n_rows), pl.ds(start, size)]
        weight_ref[pl.ds(0, n_rows), pl.ds(start, size)] = mask * (0.5 + scale * total) - goal
    if deep > n_rows:
        weight_ref[pl.ds(n_rows, deep - n_rows), :] = jnp.zeros((deep - n_rows, full), jnp.float32)
    if end:
        def spread(v):
            v = jnp.concatenate([v, jnp.zeros((n_rows, LANES - end), jnp.float32)], axis=1)
            return sum((pltpu.roll(v, k * end, 1) for k in range(1, fold)), v)

        mask, goal = [spread(v) for v in mask_and_target(full, end)]
        part = weight_end_ref[pl.ds(0, n_rows), :]
        total = sum((pltpu.roll(part, k * end, 1) for k in range(1, fold)), part)
        weight_end_ref[pl.ds(0, n_rows), :] = mask * (0.5 + scale * total) - goal
        if deep > n_rows:
            weight_end_ref[pl.ds(n_rows, deep - n_rows), :] = jnp.zeros((deep - n_rows, LANES), jnp.float32)

    def split2(weight, t):
        g = weight * (1.0 - t * t)
        hi = g.astype(jnp.bfloat16)
        return [hi, (g - hi.astype(jnp.float32)).astype(jnp.bfloat16)]

    def sums(terms, parts):
        return lax.dot_general(jnp.concatenate(parts, axis=1), jnp.concatenate(terms, axis=1), NT,
                               preferred_element_type=jnp.float32)

    def grad_some(b, carry):
        if end:
            last = sums([terms_end_ref[b]] * 2, split2(weight_end_ref[...], tanh_end(b))).T
        for inside in range(fold):
            s = b * fold + inside
            terms, parts = [], []
            for start, size in chunks:
                terms += [rhs_ref[s, pl.ds(0, 16), pl.ds(start, size)]] * 2
                parts += split2(weight_ref[:, pl.ds(start, size)], tanh_block(s, start, size))
            total = sums(terms, parts)
            total = total.T
            if end:
                total += last[16 * inside:16 * inside + 16]
            total = total[:, :n_rows]
            g, i = lax.div(s, per), lax.rem(s, per)
            both = both_ref[g, pl.ds(i, 1), :]
            for c in range(3):
                xyz = both[:, 3 * piece + c * n_rows:3 * piece + (c + 1) * n_rows]
                grad_ref[g, c, pl.ds(i, 1), :] = (0.25 / 16) * (
                    total[c:c + 1] + total[8 + c:9 + c] - total[3:4] * xyz)
        return carry

    lax.fori_loop(0, structs // fold, grad_some, 0)


def split_ens(n_ens, beads, tiles):
    best = None
    for parts in range(1, n_ens + 1):
        if n_ens % parts or beads % parts or beads % (n_ens // parts):
            continue
        cost = 2 * (beads // parts) + tiles * (beads // (n_ens // parts))
        if best is None or cost < best[0]:
            best = (cost, parts)
    return best[1]


def on_device(coords, counts, segments):
    local_n, _, beads = coords.shape
    n_tile = lax.axis_size("tile")
    n_ens = lax.axis_size("ens")
    structs = local_n * n_ens
    n_p = split_ens(n_ens, beads, n_tile)
    n_q = n_ens // n_p
    n_rows, piece = beads // n_p, beads // n_q
    n_cols = piece * n_tile
    tile, ens = lax.axis_index("tile"), lax.axis_index("ens")
    p, q = lax.rem(ens, n_p), lax.div(ens, n_p)
    vmem = pl.BlockSpec(memory_space=pltpu.VMEM)

    send = pl.pallas_call(
        functools.partial(pack_kernel, n_p, n_q),
        out_shape=jax.ShapeDtypeStruct((n_ens, local_n, 3 * (piece + n_rows)), jnp.float32),
        in_specs=[vmem],
        out_specs=vmem,
        name="pack",
    )(jnp.swapaxes(coords, 0, 1))
    both = lax.all_to_all(send, "ens", 0, 0, tiled=True)
    own = both[:, :, :3 * piece]
    pieces = [lax.ppermute(own, "tile", [(t, (t - k) % n_tile) for t in range(n_tile)]) for k in range(1, n_tile)]

    row_base = tile * beads + p * n_rows
    col_bases = [lax.rem(tile + k, n_tile) * beads + q * piece for k in range(n_tile)]
    own_counts = lax.dynamic_slice_in_dim(counts, p * n_rows, n_rows, 0)
    block = jnp.concatenate([lax.dynamic_slice_in_dim(own_counts, b, piece, 1) for b in col_bases], axis=1)
    seg_cols = jnp.concatenate([lax.dynamic_slice_in_dim(segments, b, piece) for b in col_bases])[None, :]
    col_ids = jnp.concatenate([b + jnp.arange(piece, dtype=jnp.int32) for b in col_bases])[None, :]
    seg_rows = lax.dynamic_slice_in_dim(segments, row_base, n_rows)[:, None]

    full = n_cols // LANES * LANES
    end = n_cols - full
    fold = LANES // end if end and LANES % end == 0 and local_n % (LANES // end) == 0 else 1
    deep = up(n_rows, 16)
    row_wide, col_wide = up(n_rows, LANES), up(n_cols, LANES)
    blocks = structs // fold
    grad = pl.pallas_call(
        functools.partial(pair_kernel, n_tile, fold),
        out_shape=jax.ShapeDtypeStruct((n_ens, 3, local_n, n_rows), jnp.float32),
        in_specs=[pl.BlockSpec(memory_space=pltpu.SMEM)] + [vmem] * (4 + n_tile),
        out_specs=vmem,
        scratch_shapes=[
            [pltpu.VMEM((row_wide // LANES, 8 * local_n, LANES), jnp.float32)] * 3,
            [pltpu.VMEM((col_wide // LANES, 8 * local_n, LANES), jnp.float32)] * 3,
            pltpu.VMEM((structs, deep, 48), jnp.bfloat16),
            pltpu.VMEM((blocks, deep, fold * SLOT), jnp.bfloat16),
            pltpu.VMEM((structs, 48, full), jnp.bfloat16),
            pltpu.VMEM((blocks, fold * SLOT, LANES), jnp.bfloat16),
            pltpu.VMEM((blocks, fold * 16, LANES), jnp.bfloat16),
            pltpu.VMEM((deep, full), jnp.float32),
            pltpu.VMEM((deep, LANES), jnp.float32),
        ],
        compiler_params=pltpu.CompilerParams(vmem_limit_bytes=48 << 20),
        name="pairs",
    )(row_base[None], seg_rows, seg_cols, col_ids, block, both, *pieces)

    back = lax.all_to_all(grad, "ens", 0, 0, tiled=True)
    total = pl.pallas_call(
        functools.partial(sum_kernel, n_p, n_q),
        out_shape=jax.ShapeDtypeStruct((3, local_n, beads), jnp.float32),
        in_specs=[vmem],
        out_specs=vmem,
        name="total",
    )(back)
    return jnp.swapaxes(total, 0, 1)


def solution(mesh):
    return jax.shard_map(
        on_device,
        mesh=mesh,
        in_specs=(P("ens", None, "tile"), P("tile", None), P()),
        out_specs=P("ens", None, "tile"),
        check_vma=False,
    )
```

```python
import functools

import jax
import jax.numpy as jnp
from jax import lax
from jax.experimental import pallas as pl
from jax.experimental.pallas import tpu as pltpu
from jax.sharding import PartitionSpec as P

LANES = 128
WIDE = 256
SLOT = 64
FINE = 32768.0
NT = (((1,), (1,)), ((), ()))


def up(n, unit):
    return -(-n // unit) * unit


def split3(v):
    hi = v.astype(jnp.bfloat16).astype(jnp.float32)
    rest = v - hi
    mid = rest.astype(jnp.bfloat16).astype(jnp.float32)
    return hi, mid, rest - mid


def pack_kernel(n_p, n_q, xyz_ref, send_ref):
    beads = xyz_ref.shape[2]
    n_rows, piece = beads // n_p, beads // n_q
    for c in range(3):
        for q in range(n_q):
            for p in range(n_p):
                e = q * n_p + p
                send_ref[e, :, pl.ds(c * piece, piece)] = xyz_ref[c, :, pl.ds(q * piece, piece)]
                send_ref[e, :, pl.ds(3 * piece + c * n_rows, n_rows)] = xyz_ref[c, :, pl.ds(p * n_rows, n_rows)]


def sum_kernel(n_p, n_q, back_ref, total_ref):
    n_rows = back_ref.shape[3]
    for c in range(3):
        for p in range(n_p):
            total = back_ref[p, c]
            for q in range(1, n_q):
                total += back_ref[q * n_p + p, c]
            total_ref[c, :, pl.ds(p * n_rows, n_rows)] = total


def put_terms(refs, xyz, norm_row):
    norm = 1.5 - 0.5 * (xyz[0] * xyz[0] + xyz[1] * xyz[1] + xyz[2] * xyz[2])
    n, size = norm.shape
    wide = refs[0].shape[0] * LANES
    for f, v in ((0, xyz[0]), (1, xyz[1]), (2, xyz[2]), (norm_row, norm)):
        if wide > size:
            v = jnp.concatenate([v, jnp.zeros((n, wide - size), jnp.float32)], axis=1)
        for ref, term in zip(refs, split3(v)):
            for k in range(wide // LANES):
                ref[k, pl.ds(f, n, 8), :] = term[:, k * LANES:(k + 1) * LANES]


def get_terms(refs, i):
    return [jnp.concatenate([ref[k, pl.ds(8 * i, 8), :] for k in range(ref.shape[0])], axis=1) for ref in refs]


def pair_kernel(tiles, fold, base_ref, seg_rows_ref, seg_cols_ref, col_ids_ref, counts_ref, both_ref, *rest):
    piece_refs = rest[:tiles - 1]
    (grad_ref, row_terms, col_terms, lhs_ref, lhs_end_ref, rhs_ref, rhs_end_ref, terms_end_ref, weight_ref,
     weight_end_ref) = rest[tiles - 1:]
    groups, per, _ = both_ref.shape
    structs = groups * per
    n_rows, n_cols = counts_ref.shape
    piece = n_cols // tiles
    deep = weight_ref.shape[0]
    full = rhs_ref.shape[2]
    end = n_cols - full
    chunks = [(a, min(WIDE, full - a)) for a in range(0, full, WIDE)]

    for norm_row, one_row, refs in ((3, 4, row_terms), (4, 3, col_terms)):
        for ref in refs:
            ref[...] = jnp.zeros_like(ref)
        for k in range(refs[0].shape[0]):
            refs[0][k, pl.ds(one_row, per, 8), :] = jnp.ones((per, LANES), jnp.float32)
    if end:
        rhs_end_ref[...] = jnp.zeros_like(rhs_end_ref)

    def features(g, carry):
        both = both_ref[g]
        parts = [both] + [ref[g] for ref in piece_refs]
        cols = [jnp.concatenate([v[:, c * piece:(c + 1) * piece] for v in parts], axis=1) for c in range(3)]
        rows = [both[:, 3 * piece + c * n_rows:3 * piece + (c + 1) * n_rows] for c in range(3)]
        put_terms(row_terms, rows, 3)
        put_terms(col_terms, cols, 4)
        for block in range(per // fold):
            lefts = []
            for inside in range(fold):
                i = block * fold + inside
                s = g * per + i
                hi, mid, lo = get_terms(row_terms, i)
                left = jnp.concatenate([hi, hi, mid, mid, hi, lo], axis=0)
                lhs_ref[s] = left.T[:deep].astype(jnp.bfloat16)
                if end:
                    lefts += [left, jnp.zeros((SLOT - 48, left.shape[1]), jnp.float32)]
                hi, mid, lo = get_terms(col_terms, i)
                right = jnp.concatenate([hi, mid, hi, mid, lo, hi], axis=0)
                rhs_ref[s] = right[:, :full].astype(jnp.bfloat16)
                if end:
                    lane = lax.broadcasted_iota(jnp.int32, (48, LANES), 1)
                    last = jnp.where(lane < end, right[:, full:full + LANES], 0.0)
                    if inside:
                        last = pltpu.roll(last, inside * end, 1)
                    last = last.astype(jnp.bfloat16)
                    b = g * (per // fold) + block
                    rhs_end_ref[b, pl.ds(SLOT * inside, 48), :] = last
                    terms_end_ref[b, pl.ds(16 * inside, 16), :] = last[0:16]
            if end:
                lhs_end_ref[g * (per // fold) + block] = jnp.concatenate(lefts, axis=0).T[:deep].astype(jnp.bfloat16)
        return carry

    lax.fori_loop(0, groups, features, 0)
    weight_ref[...] = jnp.zeros_like(weight_ref)
    if end:
        weight_end_ref[...] = jnp.zeros_like(weight_end_ref)

    def tanh_block(s, start, size):
        return jnp.tanh(jnp.dot(lhs_ref[s], rhs_ref[s, :, pl.ds(start, size)], preferred_element_type=jnp.float32))

    def tanh_end(b):
        return jnp.tanh(jnp.dot(lhs_end_ref[b], rhs_end_ref[b], preferred_element_type=jnp.float32))

    def add_some(b, carry):
        for inside in range(fold):
            for start, size in chunks:
                weight_ref[:, pl.ds(start, size)] += tanh_block(b * fold + inside, start, size)
        if end:
            weight_end_ref[...] += tanh_end(b)
        return carry

    lax.fori_loop(0, structs // fold, add_some, 0)

    def mask_and_target(start, size):
        count = counts_ref[:, pl.ds(start, size)].astype(jnp.float32)
        row_ids = base_ref[0] + lax.broadcasted_iota(jnp.int32, (n_rows, size), 0)
        mask = jnp.where(seg_rows_ref[...] == seg_cols_ref[:, pl.ds(start, size)], 1.0, 0.3)
        mask = jnp.where(row_ids == col_ids_ref[:, pl.ds(start, size)], 0.0, mask)
        return mask, mask * (count / (count + 8.0))

    scale = 0.5 / structs
    for start, size in chunks:
        mask, goal = mask_and_target(start, size)
        total = weight_ref[pl.ds(0, n_rows), pl.ds(start, size)]
        weight_ref[pl.ds(0, n_rows), pl.ds(start, size)] = FINE * (mask * (0.5 + scale * total) - goal)
    if deep > n_rows:
        weight_ref[pl.ds(n_rows, deep - n_rows), :] = jnp.zeros((deep - n_rows, full), jnp.float32)
    if end:
        def spread(v):
            v = jnp.concatenate([v, jnp.zeros((n_rows, LANES - end), jnp.float32)], axis=1)
            return sum((pltpu.roll(v, k * end, 1) for k in range(1, fold)), v)

        mask, goal = [spread(v) for v in mask_and_target(full, end)]
        part = weight_end_ref[pl.ds(0, n_rows), :]
        total = sum((pltpu.roll(part, k * end, 1) for k in range(1, fold)), part)
        weight_end_ref[pl.ds(0, n_rows), :] = FINE * (mask * (0.5 + scale * total) - goal)
        if deep > n_rows:
            weight_end_ref[pl.ds(n_rows, deep - n_rows), :] = jnp.zeros((deep - n_rows, LANES), jnp.float32)

    def split2(weight, t):
        g = weight * (1.0 - t * t)
        hi = g.astype(jnp.bfloat16)
        return hi, (g - hi.astype(jnp.float32)).astype(jnp.float8_e4m3fn)

    def sums(terms, parts):
        hi, lo = [jnp.concatenate(v, axis=1) for v in zip(*parts)]
        return (lax.dot_general(hi, terms, NT, preferred_element_type=jnp.float32)
                + lax.dot_general(lo, terms.astype(jnp.float8_e4m3fn), NT, preferred_element_type=jnp.float32))

    def grad_some(b, carry):
        if end:
            last = sums(terms_end_ref[b], [split2(weight_end_ref[...], tanh_end(b))]).T
        for inside in range(fold):
            s = b * fold + inside
            total = sums(rhs_ref[s, pl.ds(0, 16), :],
                         [split2(weight_ref[:, pl.ds(start, size)], tanh_block(s, start, size)) for start, size in chunks])
            total = total.T
            if end:
                total += last[16 * inside:16 * inside + 16]
            total = total[:, :n_rows]
            g, i = lax.div(s, per), lax.rem(s, per)
            both = both_ref[g, pl.ds(i, 1), :]
            for c in range(3):
                xyz = both[:, 3 * piece + c * n_rows:3 * piece + (c + 1) * n_rows]
                grad_ref[g, c, pl.ds(i, 1), :] = (0.25 / 16 / FINE) * (
                    total[c:c + 1] + total[8 + c:9 + c] - total[3:4] * xyz)
        return carry

    lax.fori_loop(0, structs // fold, grad_some, 0)


def split_ens(n_ens, beads, tiles):
    best = None
    for parts in range(1, n_ens + 1):
        if n_ens % parts or beads % parts or beads % (n_ens // parts):
            continue
        cost = 2 * (beads // parts) + tiles * (beads // (n_ens // parts))
        if best is None or cost < best[0]:
            best = (cost, parts)
    return best[1]


def on_device(coords, counts, segments):
    local_n, _, beads = coords.shape
    n_tile = lax.axis_size("tile")
    n_ens = lax.axis_size("ens")
    structs = local_n * n_ens
    n_p = split_ens(n_ens, beads, n_tile)
    n_q = n_ens // n_p
    n_rows, piece = beads // n_p, beads // n_q
    n_cols = piece * n_tile
    tile, ens = lax.axis_index("tile"), lax.axis_index("ens")
    p, q = lax.rem(ens, n_p), lax.div(ens, n_p)
    vmem = pl.BlockSpec(memory_space=pltpu.VMEM)

    send = pl.pallas_call(
        functools.partial(pack_kernel, n_p, n_q),
        out_shape=jax.ShapeDtypeStruct((n_ens, local_n, 3 * (piece + n_rows)), jnp.float32),
        in_specs=[vmem],
        out_specs=vmem,
        name="pack",
    )(jnp.swapaxes(coords, 0, 1))
    both = lax.all_to_all(send, "ens", 0, 0, tiled=True)
    own = both[:, :, :3 * piece]
    pieces = [lax.ppermute(own, "tile", [(t, (t - k) % n_tile) for t in range(n_tile)]) for k in range(1, n_tile)]

    row_base = tile * beads + p * n_rows
    col_bases = [lax.rem(tile + k, n_tile) * beads + q * piece for k in range(n_tile)]
    own_counts = lax.dynamic_slice_in_dim(counts, p * n_rows, n_rows, 0)
    block = jnp.concatenate([lax.dynamic_slice_in_dim(own_counts, b, piece, 1) for b in col_bases], axis=1)
    seg_cols = jnp.concatenate([lax.dynamic_slice_in_dim(segments, b, piece) for b in col_bases])[None, :]
    col_ids = jnp.concatenate([b + jnp.arange(piece, dtype=jnp.int32) for b in col_bases])[None, :]
    seg_rows = lax.dynamic_slice_in_dim(segments, row_base, n_rows)[:, None]

    full = n_cols // LANES * LANES
    end = n_cols - full
    fold = LANES // end if end and LANES % end == 0 and local_n % (LANES // end) == 0 else 1
    deep = up(n_rows, 16)
    row_wide, col_wide = up(n_rows, LANES), up(n_cols, LANES)
    blocks = structs // fold
    grad = pl.pallas_call(
        functools.partial(pair_kernel, n_tile, fold),
        out_shape=jax.ShapeDtypeStruct((n_ens, 3, local_n, n_rows), jnp.float32),
        in_specs=[pl.BlockSpec(memory_space=pltpu.SMEM)] + [vmem] * (4 + n_tile),
        out_specs=vmem,
        scratch_shapes=[
            [pltpu.VMEM((row_wide // LANES, 8 * local_n, LANES), jnp.float32)] * 3,
            [pltpu.VMEM((col_wide // LANES, 8 * local_n, LANES), jnp.float32)] * 3,
            pltpu.VMEM((structs, deep, 48), jnp.bfloat16),
            pltpu.VMEM((blocks, deep, fold * SLOT), jnp.bfloat16),
            pltpu.VMEM((structs, 48, full), jnp.bfloat16),
            pltpu.VMEM((blocks, fold * SLOT, LANES), jnp.bfloat16),
            pltpu.VMEM((blocks, fold * 16, LANES), jnp.bfloat16),
            pltpu.VMEM((deep, full), jnp.float32),
            pltpu.VMEM((deep, LANES), jnp.float32),
        ],
        compiler_params=pltpu.CompilerParams(vmem_limit_bytes=48 << 20),
        name="pairs",
    )(row_base[None], seg_rows, seg_cols, col_ids, block, both, *pieces)

    back = lax.all_to_all(grad, "ens", 0, 0, tiled=True)
    total = pl.pallas_call(
        functools.partial(sum_kernel, n_p, n_q),
        out_shape=jax.ShapeDtypeStruct((3, local_n, beads), jnp.float32),
        in_specs=[vmem],
        out_specs=vmem,
        name="total",
    )(back)
    return jnp.swapaxes(total, 0, 1)


def solution(mesh):
    return jax.shard_map(
        on_device,
        mesh=mesh,
        in_specs=(P("ens", None, "tile"), P("tile", None), P()),
        out_specs=P("ens", None, "tile"),
        check_vma=False,
    )
```

```python
import functools

import jax
import jax.numpy as jnp
from jax import lax
from jax.experimental import pallas as pl
from jax.experimental.pallas import tpu as pltpu
from jax.sharding import PartitionSpec as P

LANES = 128
WIDE = 256
SLOT = 64
ROW_BLOCKS = 4
NT = (((1,), (1,)), ((), ()))


def up(n, unit):
    return -(-n // unit) * unit


def split3(v):
    hi = v.astype(jnp.bfloat16).astype(jnp.float32)
    rest = v - hi
    mid = rest.astype(jnp.bfloat16).astype(jnp.float32)
    return hi, mid, rest - mid


def pack_kernel(n_p, n_q, xyz_ref, send_ref):
    beads = xyz_ref.shape[2]
    n_rows, piece = beads // n_p, beads // n_q
    for c in range(3):
        for q in range(n_q):
            for p in range(n_p):
                e = q * n_p + p
                send_ref[e, :, pl.ds(c * piece, piece)] = xyz_ref[c, :, pl.ds(q * piece, piece)]
                send_ref[e, :, pl.ds(3 * piece + c * n_rows, n_rows)] = xyz_ref[c, :, pl.ds(p * n_rows, n_rows)]


def sum_kernel(n_p, n_q, back_ref, total_ref):
    n_rows = back_ref.shape[3]
    for c in range(3):
        for p in range(n_p):
            total = back_ref[p, c]
            for q in range(1, n_q):
                total += back_ref[q * n_p + p, c]
            total_ref[c, :, pl.ds(p * n_rows, n_rows)] = total


def put_terms(refs, xyz, norm_row):
    norm = 1.5 - 0.5 * (xyz[0] * xyz[0] + xyz[1] * xyz[1] + xyz[2] * xyz[2])
    n, size = norm.shape
    wide = refs[0].shape[0] * LANES
    for f, v in ((0, xyz[0]), (1, xyz[1]), (2, xyz[2]), (norm_row, norm)):
        if wide > size:
            v = jnp.concatenate([v, jnp.zeros((n, wide - size), jnp.float32)], axis=1)
        for ref, term in zip(refs, split3(v)):
            for k in range(wide // LANES):
                ref[k, pl.ds(f, n, 8), :] = term[:, k * LANES:(k + 1) * LANES]


def get_terms(refs, i):
    return [jnp.concatenate([ref[k, pl.ds(8 * i, 8), :] for k in range(ref.shape[0])], axis=1) for ref in refs]


def pair_kernel(tiles, fold, base_ref, seg_rows_ref, seg_cols_ref, col_ids_ref, counts_ref, both_ref, *rest):
    piece_refs = rest[:tiles - 1]
    (grad_ref, row_terms, col_terms, lhs_ref, lhs_end_ref, rhs_ref, rhs_end_ref, terms_end_ref, weight_ref,
     weight_end_ref) = rest[tiles - 1:]
    groups, per, _ = both_ref.shape
    structs = groups * per
    n_rows, n_cols = counts_ref.shape
    piece = n_cols // tiles
    deep = weight_ref.shape[0]
    full = rhs_ref.shape[2]
    end = n_cols - full
    chunks = [(a, min(WIDE, full - a)) for a in range(0, full, WIDE)]
    tall = up(-(-deep // ROW_BLOCKS), 16)
    row_blocks = [pl.ds(a, min(tall, deep - a)) for a in range(0, deep, tall)]

    for norm_row, one_row, refs in ((3, 4, row_terms), (4, 3, col_terms)):
        for ref in refs:
            ref[...] = jnp.zeros_like(ref)
        for k in range(refs[0].shape[0]):
            refs[0][k, pl.ds(one_row, per, 8), :] = jnp.ones((per, LANES), jnp.float32)
    if end:
        rhs_end_ref[...] = jnp.zeros_like(rhs_end_ref)

    def features(g, carry):
        both = both_ref[g]
        parts = [both] + [ref[g] for ref in piece_refs]
        cols = [jnp.concatenate([v[:, c * piece:(c + 1) * piece] for v in parts], axis=1) for c in range(3)]
        rows = [both[:, 3 * piece + c * n_rows:3 * piece + (c + 1) * n_rows] for c in range(3)]
        put_terms(row_terms, rows, 3)
        put_terms(col_terms, cols, 4)
        for block in range(per // fold):
            lefts = []
            for inside in range(fold):
                i = block * fold + inside
                s = g * per + i
                hi, mid, lo = get_terms(row_terms, i)
                left = jnp.concatenate([hi, hi, mid, mid, hi, lo], axis=0)
                lhs_ref[s] = left.T[:deep].astype(jnp.bfloat16)
                if end:
                    lefts += [left, jnp.zeros((SLOT - 48, left.shape[1]), jnp.float32)]
                hi, mid, lo = get_terms(col_terms, i)
                right = jnp.concatenate([hi, mid, hi, mid, lo, hi], axis=0)
                rhs_ref[s] = right[:, :full].astype(jnp.bfloat16)
                if end:
                    lane = lax.broadcasted_iota(jnp.int32, (48, LANES), 1)
                    last = jnp.where(lane < end, right[:, full:full + LANES], 0.0)
                    if inside:
                        last = pltpu.roll(last, inside * end, 1)
                    last = last.astype(jnp.bfloat16)
                    b = g * (per // fold) + block
                    rhs_end_ref[b, pl.ds(SLOT * inside, 48), :] = last
                    terms_end_ref[b, pl.ds(16 * inside, 16), :] = last[0:16]
            if end:
                lhs_end_ref[g * (per // fold) + block] = jnp.concatenate(lefts, axis=0).T[:deep].astype(jnp.bfloat16)
        return carry

    lax.fori_loop(0, groups, features, 0)
    weight_ref[...] = jnp.zeros_like(weight_ref)
    if end:
        weight_end_ref[...] = jnp.zeros_like(weight_end_ref)

    def tanh_block(s, rows, start, size):
        return jnp.tanh(jnp.dot(lhs_ref[s, rows], rhs_ref[s, :, pl.ds(start, size)], preferred_element_type=jnp.float32))

    def tanh_end(b):
        return jnp.tanh(jnp.dot(lhs_end_ref[b], rhs_end_ref[b], preferred_element_type=jnp.float32))

    def add_some(b, carry):
        for inside in range(fold):
            for rows in row_blocks:
                for start, size in chunks:
                    weight_ref[rows, pl.ds(start, size)] += tanh_block(b * fold + inside, rows, start, size)
        if end:
            weight_end_ref[...] += tanh_end(b)
        return carry

    lax.fori_loop(0, structs // fold, add_some, 0)

    def mask_and_target(start, size):
        count = counts_ref[:, pl.ds(start, size)].astype(jnp.float32)
        row_ids = base_ref[0] + lax.broadcasted_iota(jnp.int32, (n_rows, size), 0)
        mask = jnp.where(seg_rows_ref[...] == seg_cols_ref[:, pl.ds(start, size)], 1.0, 0.3)
        mask = jnp.where(row_ids == col_ids_ref[:, pl.ds(start, size)], 0.0, mask)
        return mask, mask * (count / (count + 8.0))

    scale = 0.5 / structs
    for start, size in chunks:
        mask, goal = mask_and_target(start, size)
        total = weight_ref[pl.ds(0, n_rows), pl.ds(start, size)]
        weight_ref[pl.ds(0, n_rows), pl.ds(start, size)] = mask * (0.5 + scale * total) - goal
    if deep > n_rows:
        weight_ref[pl.ds(n_rows, deep - n_rows), :] = jnp.zeros((deep - n_rows, full), jnp.float32)
    if end:
        def spread(v):
            v = jnp.concatenate([v, jnp.zeros((n_rows, LANES - end), jnp.float32)], axis=1)
            return sum((pltpu.roll(v, k * end, 1) for k in range(1, fold)), v)

        mask, goal = [spread(v) for v in mask_and_target(full, end)]
        part = weight_end_ref[pl.ds(0, n_rows), :]
        total = sum((pltpu.roll(part, k * end, 1) for k in range(1, fold)), part)
        weight_end_ref[pl.ds(0, n_rows), :] = mask * (0.5 + scale * total) - goal
        if deep > n_rows:
            weight_end_ref[pl.ds(n_rows, deep - n_rows), :] = jnp.zeros((deep - n_rows, LANES), jnp.float32)

    def split2(weight, t):
        g = weight * (1.0 - t * t)
        hi = g.astype(jnp.bfloat16)
        return [hi, (g - hi.astype(jnp.float32)).astype(jnp.bfloat16)]

    def sums(terms, parts):
        return lax.dot_general(jnp.concatenate(parts, axis=1), jnp.concatenate(terms, axis=1), NT,
                               preferred_element_type=jnp.float32)

    def grad_some(b, carry):
        if end:
            last = sums([terms_end_ref[b]] * 2, split2(weight_end_ref[...], tanh_end(b))).T
        for inside in range(fold):
            s = b * fold + inside
            blocks = []
            for rows in row_blocks:
                terms, parts = [], []
                for start, size in chunks:
                    terms += [rhs_ref[s, pl.ds(0, 16), pl.ds(start, size)]] * 2
                    parts += split2(weight_ref[rows, pl.ds(start, size)], tanh_block(s, rows, start, size))
                blocks.append(sums(terms, parts))
            total = jnp.concatenate(blocks, axis=0)
            total = total.T
            if end:
                total += last[16 * inside:16 * inside + 16]
            total = total[:, :n_rows]
            g, i = lax.div(s, per), lax.rem(s, per)
            both = both_ref[g, pl.ds(i, 1), :]
            for c in range(3):
                xyz = both[:, 3 * piece + c * n_rows:3 * piece + (c + 1) * n_rows]
                grad_ref[g, c, pl.ds(i, 1), :] = (0.25 / 16) * (
                    total[c:c + 1] + total[8 + c:9 + c] - total[3:4] * xyz)
        return carry

    lax.fori_loop(0, structs // fold, grad_some, 0)


def split_ens(n_ens, beads, tiles):
    best = None
    for parts in range(1, n_ens + 1):
        if n_ens % parts or beads % parts or beads % (n_ens // parts):
            continue
        cost = 2 * (beads // parts) + tiles * (beads // (n_ens // parts))
        if best is None or cost < best[0]:
            best = (cost, parts)
    return best[1]


def on_device(coords, counts, segments):
    local_n, _, beads = coords.shape
    n_tile = lax.axis_size("tile")
    n_ens = lax.axis_size("ens")
    structs = local_n * n_ens
    n_p = split_ens(n_ens, beads, n_tile)
    n_q = n_ens // n_p
    n_rows, piece = beads // n_p, beads // n_q
    n_cols = piece * n_tile
    tile, ens = lax.axis_index("tile"), lax.axis_index("ens")
    p, q = lax.rem(ens, n_p), lax.div(ens, n_p)
    vmem = pl.BlockSpec(memory_space=pltpu.VMEM)

    send = pl.pallas_call(
        functools.partial(pack_kernel, n_p, n_q),
        out_shape=jax.ShapeDtypeStruct((n_ens, local_n, 3 * (piece + n_rows)), jnp.float32),
        in_specs=[vmem],
        out_specs=vmem,
        name="pack",
    )(jnp.swapaxes(coords, 0, 1))
    both = lax.all_to_all(send, "ens", 0, 0, tiled=True)
    own = both[:, :, :3 * piece]
    pieces = [lax.ppermute(own, "tile", [(t, (t - k) % n_tile) for t in range(n_tile)]) for k in range(1, n_tile)]

    row_base = tile * beads + p * n_rows
    col_bases = [lax.rem(tile + k, n_tile) * beads + q * piece for k in range(n_tile)]
    own_counts = lax.dynamic_slice_in_dim(counts, p * n_rows, n_rows, 0)
    block = jnp.concatenate([lax.dynamic_slice_in_dim(own_counts, b, piece, 1) for b in col_bases], axis=1)
    seg_cols = jnp.concatenate([lax.dynamic_slice_in_dim(segments, b, piece) for b in col_bases])[None, :]
    col_ids = jnp.concatenate([b + jnp.arange(piece, dtype=jnp.int32) for b in col_bases])[None, :]
    seg_rows = lax.dynamic_slice_in_dim(segments, row_base, n_rows)[:, None]

    full = n_cols // LANES * LANES
    end = n_cols - full
    fold = LANES // end if end and LANES % end == 0 and local_n % (LANES // end) == 0 else 1
    deep = up(n_rows, 16)
    row_wide, col_wide = up(n_rows, LANES), up(n_cols, LANES)
    blocks = structs // fold
    grad = pl.pallas_call(
        functools.partial(pair_kernel, n_tile, fold),
        out_shape=jax.ShapeDtypeStruct((n_ens, 3, local_n, n_rows), jnp.float32),
        in_specs=[pl.BlockSpec(memory_space=pltpu.SMEM)] + [vmem] * (4 + n_tile),
        out_specs=vmem,
        scratch_shapes=[
            [pltpu.VMEM((row_wide // LANES, 8 * local_n, LANES), jnp.float32)] * 3,
            [pltpu.VMEM((col_wide // LANES, 8 * local_n, LANES), jnp.float32)] * 3,
            pltpu.VMEM((structs, deep, 48), jnp.bfloat16),
            pltpu.VMEM((blocks, deep, fold * SLOT), jnp.bfloat16),
            pltpu.VMEM((structs, 48, full), jnp.bfloat16),
            pltpu.VMEM((blocks, fold * SLOT, LANES), jnp.bfloat16),
            pltpu.VMEM((blocks, fold * 16, LANES), jnp.bfloat16),
            pltpu.VMEM((deep, full), jnp.float32),
            pltpu.VMEM((deep, LANES), jnp.float32),
        ],
        compiler_params=pltpu.CompilerParams(vmem_limit_bytes=48 << 20),
        name="pairs",
    )(row_base[None], seg_rows, seg_cols, col_ids, block, both, *pieces)

    back = lax.all_to_all(grad, "ens", 0, 0, tiled=True)
    total = pl.pallas_call(
        functools.partial(sum_kernel, n_p, n_q),
        out_shape=jax.ShapeDtypeStruct((3, local_n, beads), jnp.float32),
        in_specs=[vmem],
        out_specs=vmem,
        name="total",
    )(back)
    return jnp.swapaxes(total, 0, 1)


def solution(mesh):
    return jax.shard_map(
        on_device,
        mesh=mesh,
        in_specs=(P("ens", None, "tile"), P("tile", None), P()),
        out_specs=P("ens", None, "tile"),
        check_vma=False,
    )
```

```python
import functools

import jax
import jax.numpy as jnp
from jax import lax
from jax.experimental import pallas as pl
from jax.experimental.pallas import tpu as pltpu
from jax.sharding import PartitionSpec as P

LANES = 128
WIDE = 256
SLOT = 32
KEEP_BYTES = 36 << 20
NT = (((1,), (1,)), ((), ()))
ROW_FEATURES = "hhnmmhl1"
COL_FEATURES = "hm1hmlhn"


def up(n, unit):
    return -(-n // unit) * unit


def split3(v):
    hi = v.astype(jnp.bfloat16).astype(jnp.float32)
    rest = v - hi
    mid = rest.astype(jnp.bfloat16).astype(jnp.float32)
    return hi, mid, rest - mid


def pack_kernel(n_p, n_q, xyz_ref, send_ref):
    beads = xyz_ref.shape[2]
    n_rows, piece = beads // n_p, beads // n_q
    for c in range(3):
        for q in range(n_q):
            for p in range(n_p):
                e = q * n_p + p
                send_ref[e, :, pl.ds(c * piece, piece)] = xyz_ref[c, :, pl.ds(q * piece, piece)]
                send_ref[e, :, pl.ds(3 * piece + c * n_rows, n_rows)] = xyz_ref[c, :, pl.ds(p * n_rows, n_rows)]


def sum_kernel(n_p, n_q, back_ref, total_ref):
    n_rows = back_ref.shape[2] // 3
    for p in range(n_p):
        total = back_ref[p]
        for q in range(1, n_q):
            total += back_ref[q * n_p + p]
        for c in range(3):
            total_ref[c, :, pl.ds(p * n_rows, n_rows)] = total[:, c * n_rows:(c + 1) * n_rows]


def put_terms(ref, xyz, layout):
    norm = 1.5 - 0.5 * (xyz[0] * xyz[0] + xyz[1] * xyz[1] + xyz[2] * xyz[2])
    n, size = norm.shape
    blocks = ref.shape[0]
    if blocks * LANES > size:
        pad = jnp.zeros((n, blocks * LANES - size), jnp.float32)
        xyz, norm = [jnp.concatenate([v, pad], axis=1) for v in xyz], jnp.concatenate([norm, pad], axis=1)
    terms = dict(zip("hml", zip(*[split3(v) for v in xyz])))
    terms["n"] = split3(norm)
    for r, name in enumerate(layout):
        if name != "1":
            for c in range(3):
                for k in range(blocks):
                    ref[k, pl.ds(3 * r + c, n, SLOT), :] = terms[name][c][:, k * LANES:(k + 1) * LANES]


def init_terms(ref, n, layout):
    ref[...] = jnp.zeros_like(ref)
    for k in range(ref.shape[0]):
        for c in range(3):
            ref[k, pl.ds(3 * layout.index("1") + c, n, SLOT), :] = jnp.ones((n, LANES), jnp.float32)


def get_terms(ref, i, n):
    return jnp.concatenate([ref[k, pl.ds(SLOT * i, SLOT * n), :] for k in range(ref.shape[0])], axis=1)


def pair_kernel(tiles, fold, base_ref, seg_rows_ref, seg_cols_ref, col_ids_ref, counts_ref, both_ref, *rest):
    piece_refs = rest[:tiles - 1]
    (grad_ref, row_terms, col_terms, lhs_ref, rhs_ref, rhs_end_ref, terms_end_ref, weight_ref, weight_end_ref, kept_ref,
     kept_end_ref) = rest[tiles - 1:]
    groups, per, _ = both_ref.shape
    structs = groups * per
    n_rows, n_cols = counts_ref.shape
    piece = n_cols // tiles
    blocks, deep, _ = lhs_ref.shape
    kept = kept_end_ref.shape[0]
    full = rhs_ref.shape[2]
    end = n_cols - full
    chunks = [(a, min(WIDE, full - a)) for a in range(0, full, WIDE)]

    init_terms(row_terms, per, ROW_FEATURES)
    init_terms(col_terms, per, COL_FEATURES)
    if end:
        rhs_end_ref[...] = jnp.zeros_like(rhs_end_ref)

    def features(g, carry):
        both = both_ref[g]
        parts = [both] + [ref[g] for ref in piece_refs]
        cols = [jnp.concatenate([v[:, c * piece:(c + 1) * piece] for v in parts], axis=1) for c in range(3)]
        rows = [both[:, 3 * piece + c * n_rows:3 * piece + (c + 1) * n_rows] for c in range(3)]
        put_terms(row_terms, rows, ROW_FEATURES)
        put_terms(col_terms, cols, COL_FEATURES)
        for block in range(per // fold):
            b = g * (per // fold) + block
            lhs_ref[b] = get_terms(row_terms, block * fold, fold).T[:deep].astype(jnp.bfloat16)
            for inside in range(fold):
                right = get_terms(col_terms, block * fold + inside, 1)
                rhs_ref[b * fold + inside] = right[:, :full].astype(jnp.bfloat16)
                if end:
                    lane = lax.broadcasted_iota(jnp.int32, (SLOT, LANES), 1)
                    last = jnp.where(lane < end, right[:, full:full + LANES], 0.0)
                    if inside:
                        last = pltpu.roll(last, inside * end, 1)
                    last = last.astype(jnp.bfloat16)
                    rhs_end_ref[b, pl.ds(SLOT * inside, SLOT), :] = last
                    terms_end_ref[b, pl.ds(16 * inside, 16), :] = last[0:16]
        return carry

    lax.fori_loop(0, groups, features, 0)
    weight_ref[...] = jnp.zeros_like(weight_ref)
    if end:
        weight_end_ref[...] = jnp.zeros_like(weight_end_ref)

    def tanh_block(b, inside, start, size):
        left = lhs_ref[b, :, pl.ds(SLOT * inside, SLOT)]
        right = rhs_ref[b * fold + inside, :, pl.ds(start, size)]
        return jnp.tanh(jnp.dot(left, right, preferred_element_type=jnp.float32))

    def tanh_end(b):
        return jnp.tanh(jnp.dot(lhs_ref[b], rhs_end_ref[b], preferred_element_type=jnp.float32))

    def add_some(keep, b, carry):
        for inside in range(fold):
            for start, size in chunks:
                t = tanh_block(b, inside, start, size)
                if keep:
                    kept_ref[b * fold + inside, :, pl.ds(start, size)] = t
                weight_ref[:, pl.ds(start, size)] += t
        if end:
            t = tanh_end(b)
            if keep:
                kept_end_ref[b] = t
            weight_end_ref[...] += t
        return carry

    lax.fori_loop(0, kept, functools.partial(add_some, True), 0)
    lax.fori_loop(kept, blocks, functools.partial(add_some, False), 0)

    def mask_and_target(start, size):
        count = counts_ref[:, pl.ds(start, size)].astype(jnp.float32)
        row_ids = base_ref[0] + lax.broadcasted_iota(jnp.int32, (n_rows, size), 0)
        mask = jnp.where(seg_rows_ref[...] == seg_cols_ref[:, pl.ds(start, size)], 1.0, 0.3)
        mask = jnp.where(row_ids == col_ids_ref[:, pl.ds(start, size)], 0.0, mask)
        return mask, mask * (count / (count + 8.0))

    scale = 0.5 / structs
    for start, size in chunks:
        mask, goal = mask_and_target(start, size)
        total = weight_ref[pl.ds(0, n_rows), pl.ds(start, size)]
        weight_ref[pl.ds(0, n_rows), pl.ds(start, size)] = mask * (0.5 + scale * total) - goal
    if deep > n_rows:
        weight_ref[pl.ds(n_rows, deep - n_rows), :] = jnp.zeros((deep - n_rows, full), jnp.float32)
    if end:
        def spread(v):
            v = jnp.concatenate([v, jnp.zeros((n_rows, LANES - end), jnp.float32)], axis=1)
            return sum((pltpu.roll(v, k * end, 1) for k in range(1, fold)), v)

        mask, goal = [spread(v) for v in mask_and_target(full, end)]
        part = weight_end_ref[pl.ds(0, n_rows), :]
        total = sum((pltpu.roll(part, k * end, 1) for k in range(1, fold)), part)
        weight_end_ref[pl.ds(0, n_rows), :] = mask * (0.5 + scale * total) - goal
        if deep > n_rows:
            weight_end_ref[pl.ds(n_rows, deep - n_rows), :] = jnp.zeros((deep - n_rows, LANES), jnp.float32)

    def split2(weight, t):
        g = weight * (1.0 - t * t)
        hi = g.astype(jnp.bfloat16)
        return [hi, (g - hi.astype(jnp.float32)).astype(jnp.bfloat16)]

    def sums(terms, parts):
        return lax.dot_general(jnp.concatenate(parts, axis=1), jnp.concatenate(terms, axis=1), NT,
                               preferred_element_type=jnp.float32)

    def grad_some(keep, b, carry):
        if end:
            t = kept_end_ref[b] if keep else tanh_end(b)
            last = sums([terms_end_ref[b]] * 2, split2(weight_end_ref[...], t)).T
        for inside in range(fold):
            s = b * fold + inside
            terms, parts = [], []
            for start, size in chunks:
                t = kept_ref[s, :, pl.ds(start, size)] if keep else tanh_block(b, inside, start, size)
                terms += [rhs_ref[s, pl.ds(0, 16), pl.ds(start, size)]] * 2
                parts += split2(weight_ref[:, pl.ds(start, size)], t)
            total = sums(terms, parts).T
            if end:
                total += last[16 * inside:16 * inside + 16]
            total = total[:, :n_rows]
            g, i = lax.div(s, per), lax.rem(s, per)
            both = both_ref[g, pl.ds(i, 1), :]
            grad = []
            for c in range(3):
                xyz = both[:, 3 * piece + c * n_rows:3 * piece + (c + 1) * n_rows]
                grad.append((0.25 / 16) * (total[c:c + 1] + total[3 + c:4 + c] - total[6:7] * xyz))
            grad_ref[g, pl.ds(i, 1), :] = jnp.concatenate(grad, axis=1)
        return carry

    lax.fori_loop(0, kept, functools.partial(grad_some, True), 0)
    lax.fori_loop(kept, blocks, functools.partial(grad_some, False), 0)


def split_ens(n_ens, beads, tiles):
    best = None
    for parts in range(1, n_ens + 1):
        if n_ens % parts or beads % parts or beads % (n_ens // parts):
            continue
        cost = 2 * (beads // parts) + tiles * (beads // (n_ens // parts))
        if best is None or cost < best[0]:
            best = (cost, parts)
    return best[1]


def on_device(coords, counts, segments):
    local_n, _, beads = coords.shape
    n_tile = lax.axis_size("tile")
    n_ens = lax.axis_size("ens")
    structs = local_n * n_ens
    n_p = split_ens(n_ens, beads, n_tile)
    n_q = n_ens // n_p
    n_rows, piece = beads // n_p, beads // n_q
    n_cols = piece * n_tile
    tile, ens = lax.axis_index("tile"), lax.axis_index("ens")
    p, q = lax.rem(ens, n_p), lax.div(ens, n_p)
    vmem = pl.BlockSpec(memory_space=pltpu.VMEM)

    send = pl.pallas_call(
        functools.partial(pack_kernel, n_p, n_q),
        out_shape=jax.ShapeDtypeStruct((n_ens, local_n, 3 * (piece + n_rows)), jnp.float32),
        in_specs=[vmem],
        out_specs=vmem,
        name="pack",
    )(jnp.swapaxes(coords, 0, 1))
    both = lax.all_to_all(send, "ens", 0, 0, tiled=True)
    own = both[:, :, :3 * piece]
    pieces = [lax.ppermute(own, "tile", [(t, (t - k) % n_tile) for t in range(n_tile)]) for k in range(1, n_tile)]

    row_base = tile * beads + p * n_rows
    col_bases = [lax.rem(tile + k, n_tile) * beads + q * piece for k in range(n_tile)]
    own_counts = lax.dynamic_slice_in_dim(counts, p * n_rows, n_rows, 0)
    block = jnp.concatenate([lax.dynamic_slice_in_dim(own_counts, b, piece, 1) for b in col_bases], axis=1)
    seg_cols = jnp.concatenate([lax.dynamic_slice_in_dim(segments, b, piece) for b in col_bases])[None, :]
    col_ids = jnp.concatenate([b + jnp.arange(piece, dtype=jnp.int32) for b in col_bases])[None, :]
    seg_rows = lax.dynamic_slice_in_dim(segments, row_base, n_rows)[:, None]

    full = n_cols // LANES * LANES
    end = n_cols - full
    fold = LANES // end if end and LANES % end == 0 and local_n % (LANES // end) == 0 else 1
    deep = up(n_rows, 16)
    row_wide, col_wide = up(n_rows, LANES), up(n_cols, LANES)
    blocks = structs // fold
    kept = max(1, min(blocks, KEEP_BYTES // (4 * deep * (fold * full + LANES))))
    grad = pl.pallas_call(
        functools.partial(pair_kernel, n_tile, fold),
        out_shape=jax.ShapeDtypeStruct((n_ens, local_n, 3 * n_rows), jnp.float32),
        in_specs=[pl.BlockSpec(memory_space=pltpu.SMEM)] + [vmem] * (4 + n_tile),
        out_specs=vmem,
        scratch_shapes=[
            pltpu.VMEM((row_wide // LANES, SLOT * local_n, LANES), jnp.float32),
            pltpu.VMEM((col_wide // LANES, SLOT * local_n, LANES), jnp.float32),
            pltpu.VMEM((blocks, deep, fold * SLOT), jnp.bfloat16),
            pltpu.VMEM((structs, SLOT, full), jnp.bfloat16),
            pltpu.VMEM((blocks, fold * SLOT, LANES), jnp.bfloat16),
            pltpu.VMEM((blocks, fold * 16, LANES), jnp.bfloat16),
            pltpu.VMEM((deep, full), jnp.float32),
            pltpu.VMEM((deep, LANES), jnp.float32),
            pltpu.VMEM((kept * fold, deep, full), jnp.float32),
            pltpu.VMEM((kept, deep, LANES), jnp.float32),
        ],
        compiler_params=pltpu.CompilerParams(vmem_limit_bytes=56 << 20),
        name="pairs",
    )(row_base[None], seg_rows, seg_cols, col_ids, block, both, *pieces)

    back = lax.all_to_all(grad, "ens", 0, 0, tiled=True)
    total = pl.pallas_call(
        functools.partial(sum_kernel, n_p, n_q),
        out_shape=jax.ShapeDtypeStruct((3, local_n, beads), jnp.float32),
        in_specs=[vmem],
        out_specs=vmem,
        name="total",
    )(back)
    return jnp.swapaxes(total, 0, 1)


def solution(mesh):
    return jax.shard_map(
        on_device,
        mesh=mesh,
        in_specs=(P("ens", None, "tile"), P("tile", None), P()),
        out_specs=P("ens", None, "tile"),
        check_vma=False,
    )
```

```python
import functools

import jax
import jax.numpy as jnp
from jax import lax
from jax.experimental import pallas as pl
from jax.experimental.pallas import tpu as pltpu
from jax.sharding import PartitionSpec as P

LANES = 128
WIDE = 256
SLOT = 32
NT = (((1,), (1,)), ((), ()))
ROW_FEATURES = "hhnmmhl1"
COL_FEATURES = "hm1hmlhn"


def up(n, unit):
    return -(-n // unit) * unit


def split3(v):
    hi = v.astype(jnp.bfloat16).astype(jnp.float32)
    rest = v - hi
    mid = rest.astype(jnp.bfloat16).astype(jnp.float32)
    return hi, mid, rest - mid


def pack_kernel(n_p, n_q, xyz_ref, send_ref):
    beads = xyz_ref.shape[2]
    n_rows, piece = beads // n_p, beads // n_q
    for c in range(3):
        for q in range(n_q):
            for p in range(n_p):
                e = q * n_p + p
                send_ref[e, :, pl.ds(c * piece, piece)] = xyz_ref[c, :, pl.ds(q * piece, piece)]
                send_ref[e, :, pl.ds(3 * piece + c * n_rows, n_rows)] = xyz_ref[c, :, pl.ds(p * n_rows, n_rows)]


def sum_kernel(n_p, n_q, back_ref, total_ref):
    n_rows = back_ref.shape[2] // 3
    for p in range(n_p):
        total = back_ref[p]
        for q in range(1, n_q):
            total += back_ref[q * n_p + p]
        for c in range(3):
            total_ref[c, :, pl.ds(p * n_rows, n_rows)] = total[:, c * n_rows:(c + 1) * n_rows]


def put_terms(ref, xyz, layout):
    norm = 1.5 - 0.5 * (xyz[0] * xyz[0] + xyz[1] * xyz[1] + xyz[2] * xyz[2])
    n, size = norm.shape
    blocks = ref.shape[0]
    if blocks * LANES > size:
        pad = jnp.zeros((n, blocks * LANES - size), jnp.float32)
        xyz, norm = [jnp.concatenate([v, pad], axis=1) for v in xyz], jnp.concatenate([norm, pad], axis=1)
    terms = dict(zip("hml", zip(*[split3(v) for v in xyz])))
    terms["n"] = split3(norm)
    for r, name in enumerate(layout):
        if name != "1":
            for c in range(3):
                for k in range(blocks):
                    ref[k, pl.ds(3 * r + c, n, SLOT), :] = terms[name][c][:, k * LANES:(k + 1) * LANES]


def init_terms(ref, n, layout):
    ref[...] = jnp.zeros_like(ref)
    for k in range(ref.shape[0]):
        for c in range(3):
            ref[k, pl.ds(3 * layout.index("1") + c, n, SLOT), :] = jnp.ones((n, LANES), jnp.float32)


def get_terms(ref, i, n):
    return jnp.concatenate([ref[k, pl.ds(SLOT * i, SLOT * n), :] for k in range(ref.shape[0])], axis=1)


def pair_kernel(tiles, fold, base_ref, seg_rows_ref, seg_cols_ref, col_ids_ref, counts_ref, both_ref, *rest):
    piece_refs = rest[:tiles - 1]
    (grad_ref, row_terms, col_terms, lhs_ref, lhs_end_ref, rhs_ref, rhs_end_ref, terms_end_ref, weight_ref,
     weight_end_ref) = rest[tiles - 1:]
    groups, per, _ = both_ref.shape
    structs = groups * per
    n_rows, n_cols = counts_ref.shape
    piece = n_cols // tiles
    blocks, deep, _ = lhs_end_ref.shape
    full = rhs_ref.shape[2]
    end = n_cols - full
    chunks = [(a, min(WIDE, full - a)) for a in range(0, full, WIDE)]

    init_terms(row_terms, per, ROW_FEATURES)
    init_terms(col_terms, per, COL_FEATURES)
    if end:
        rhs_end_ref[...] = jnp.zeros_like(rhs_end_ref)

    def features(g, carry):
        both = both_ref[g]
        parts = [both] + [ref[g] for ref in piece_refs]
        cols = [jnp.concatenate([v[:, c * piece:(c + 1) * piece] for v in parts], axis=1) for c in range(3)]
        rows = [both[:, 3 * piece + c * n_rows:3 * piece + (c + 1) * n_rows] for c in range(3)]
        put_terms(row_terms, rows, ROW_FEATURES)
        put_terms(col_terms, cols, COL_FEATURES)
        for block in range(per // fold):
            b = g * (per // fold) + block
            left = get_terms(row_terms, block * fold, fold).T[:deep].astype(jnp.bfloat16)
            lhs_end_ref[b] = left
            for inside in range(fold):
                lhs_ref[b * fold + inside] = left[:, SLOT * inside:SLOT * (inside + 1)]
                right = get_terms(col_terms, block * fold + inside, 1)
                rhs_ref[b * fold + inside] = right[:, :full].astype(jnp.bfloat16)
                if end:
                    lane = lax.broadcasted_iota(jnp.int32, (SLOT, LANES), 1)
                    last = jnp.where(lane < end, right[:, full:full + LANES], 0.0)
                    if inside:
                        last = pltpu.roll(last, inside * end, 1)
                    last = last.astype(jnp.bfloat16)
                    rhs_end_ref[b, pl.ds(SLOT * inside, SLOT), :] = last
                    terms_end_ref[b, pl.ds(16 * inside, 16), :] = last[0:16]
        return carry

    lax.fori_loop(0, groups, features, 0)
    weight_ref[...] = jnp.zeros_like(weight_ref)
    if end:
        weight_end_ref[...] = jnp.zeros_like(weight_end_ref)

    def tanh_block(s, start, size):
        return jnp.tanh(jnp.dot(lhs_ref[s], rhs_ref[s, :, pl.ds(start, size)], preferred_element_type=jnp.float32))

    def tanh_end(b):
        return jnp.tanh(jnp.dot(lhs_end_ref[b], rhs_end_ref[b], preferred_element_type=jnp.float32))

    def add_some(b, carry):
        for start, size in chunks:
            some = [tanh_block(b * fold + inside, start, size) for inside in range(fold)]
            weight_ref[:, pl.ds(start, size)] += functools.reduce(jnp.add, some)
        if end:
            weight_end_ref[...] += tanh_end(b)
        return carry

    lax.fori_loop(0, blocks, add_some, 0)

    def mask_and_target(start, size):
        count = counts_ref[:, pl.ds(start, size)].astype(jnp.float32)
        row_ids = base_ref[0] + lax.broadcasted_iota(jnp.int32, (n_rows, size), 0)
        mask = jnp.where(seg_rows_ref[...] == seg_cols_ref[:, pl.ds(start, size)], 1.0, 0.3)
        mask = jnp.where(row_ids == col_ids_ref[:, pl.ds(start, size)], 0.0, mask)
        return mask, mask * (count / (count + 8.0))

    scale = 0.5 / structs
    for start, size in chunks:
        mask, goal = mask_and_target(start, size)
        total = weight_ref[pl.ds(0, n_rows), pl.ds(start, size)]
        weight_ref[pl.ds(0, n_rows), pl.ds(start, size)] = mask * (0.5 + scale * total) - goal
    if deep > n_rows:
        weight_ref[pl.ds(n_rows, deep - n_rows), :] = jnp.zeros((deep - n_rows, full), jnp.float32)
    if end:
        def spread(v):
            v = jnp.concatenate([v, jnp.zeros((n_rows, LANES - end), jnp.float32)], axis=1)
            return sum((pltpu.roll(v, k * end, 1) for k in range(1, fold)), v)

        mask, goal = [spread(v) for v in mask_and_target(full, end)]
        part = weight_end_ref[pl.ds(0, n_rows), :]
        total = sum((pltpu.roll(part, k * end, 1) for k in range(1, fold)), part)
        weight_end_ref[pl.ds(0, n_rows), :] = mask * (0.5 + scale * total) - goal
        if deep > n_rows:
            weight_end_ref[pl.ds(n_rows, deep - n_rows), :] = jnp.zeros((deep - n_rows, LANES), jnp.float32)

    def split2(weight, t):
        g = weight * (1.0 - t * t)
        hi = g.astype(jnp.bfloat16)
        return [hi, (g - hi.astype(jnp.float32)).astype(jnp.bfloat16)]

    def sums(terms, parts):
        return lax.dot_general(jnp.concatenate(parts, axis=1), jnp.concatenate(terms, axis=1), NT,
                               preferred_element_type=jnp.float32)

    def grad_some(b, carry):
        if end:
            last = sums([terms_end_ref[b]] * 2, split2(weight_end_ref[...], tanh_end(b))).T
        for inside in range(fold):
            s = b * fold + inside
            terms, parts = [], []
            for start, size in chunks:
                terms += [rhs_ref[s, pl.ds(0, 16), pl.ds(start, size)]] * 2
                parts += split2(weight_ref[:, pl.ds(start, size)], tanh_block(s, start, size))
            total = sums(terms, parts).T
            if end:
                total += last[16 * inside:16 * inside + 16]
            total = total[:, :n_rows]
            g, i = lax.div(s, per), lax.rem(s, per)
            both = both_ref[g, pl.ds(i, 1), :]
            grad = []
            for c in range(3):
                xyz = both[:, 3 * piece + c * n_rows:3 * piece + (c + 1) * n_rows]
                grad.append((0.25 / 16) * (total[c:c + 1] + total[3 + c:4 + c] - total[6:7] * xyz))
            grad_ref[g, pl.ds(i, 1), :] = jnp.concatenate(grad, axis=1)
        return carry

    lax.fori_loop(0, blocks, grad_some, 0)


def split_ens(n_ens, beads, tiles):
    best = None
    for parts in range(1, n_ens + 1):
        if n_ens % parts or beads % parts or beads % (n_ens // parts):
            continue
        cost = 2 * (beads // parts) + tiles * (beads // (n_ens // parts))
        if best is None or cost < best[0]:
            best = (cost, parts)
    return best[1]


def on_device(coords, counts, segments):
    local_n, _, beads = coords.shape
    n_tile = lax.axis_size("tile")
    n_ens = lax.axis_size("ens")
    structs = local_n * n_ens
    n_p = split_ens(n_ens, beads, n_tile)
    n_q = n_ens // n_p
    n_rows, piece = beads // n_p, beads // n_q
    n_cols = piece * n_tile
    tile, ens = lax.axis_index("tile"), lax.axis_index("ens")
    p, q = lax.rem(ens, n_p), lax.div(ens, n_p)
    vmem = pl.BlockSpec(memory_space=pltpu.VMEM)

    send = pl.pallas_call(
        functools.partial(pack_kernel, n_p, n_q),
        out_shape=jax.ShapeDtypeStruct((n_ens, local_n, 3 * (piece + n_rows)), jnp.float32),
        in_specs=[vmem],
        out_specs=vmem,
        name="pack",
    )(jnp.swapaxes(coords, 0, 1))
    both = lax.all_to_all(send, "ens", 0, 0, tiled=True)
    own = both[:, :, :3 * piece]
    pieces = [lax.ppermute(own, "tile", [(t, (t - k) % n_tile) for t in range(n_tile)]) for k in range(1, n_tile)]

    row_base = tile * beads + p * n_rows
    col_bases = [lax.rem(tile + k, n_tile) * beads + q * piece for k in range(n_tile)]
    own_counts = lax.dynamic_slice_in_dim(counts, p * n_rows, n_rows, 0)
    block = jnp.concatenate([lax.dynamic_slice_in_dim(own_counts, b, piece, 1) for b in col_bases], axis=1)
    seg_cols = jnp.concatenate([lax.dynamic_slice_in_dim(segments, b, piece) for b in col_bases])[None, :]
    col_ids = jnp.concatenate([b + jnp.arange(piece, dtype=jnp.int32) for b in col_bases])[None, :]
    seg_rows = lax.dynamic_slice_in_dim(segments, row_base, n_rows)[:, None]

    full = n_cols // LANES * LANES
    end = n_cols - full
    fold = LANES // end if end and LANES % end == 0 and local_n % (LANES // end) == 0 else 1
    deep = up(n_rows, 16)
    row_wide, col_wide = up(n_rows, LANES), up(n_cols, LANES)
    blocks = structs // fold
    grad = pl.pallas_call(
        functools.partial(pair_kernel, n_tile, fold),
        out_shape=jax.ShapeDtypeStruct((n_ens, local_n, 3 * n_rows), jnp.float32),
        in_specs=[pl.BlockSpec(memory_space=pltpu.SMEM)] + [vmem] * (4 + n_tile),
        out_specs=vmem,
        scratch_shapes=[
            pltpu.VMEM((row_wide // LANES, SLOT * local_n, LANES), jnp.float32),
            pltpu.VMEM((col_wide // LANES, SLOT * local_n, LANES), jnp.float32),
            pltpu.VMEM((structs, deep, SLOT), jnp.bfloat16),
            pltpu.VMEM((blocks, deep, fold * SLOT), jnp.bfloat16),
            pltpu.VMEM((structs, SLOT, full), jnp.bfloat16),
            pltpu.VMEM((blocks, fold * SLOT, LANES), jnp.bfloat16),
            pltpu.VMEM((blocks, fold * 16, LANES), jnp.bfloat16),
            pltpu.VMEM((deep, full), jnp.float32),
            pltpu.VMEM((deep, LANES), jnp.float32),
        ],
        compiler_params=pltpu.CompilerParams(vmem_limit_bytes=48 << 20),
        name="pairs",
    )(row_base[None], seg_rows, seg_cols, col_ids, block, both, *pieces)

    back = lax.all_to_all(grad, "ens", 0, 0, tiled=True)
    total = pl.pallas_call(
        functools.partial(sum_kernel, n_p, n_q),
        out_shape=jax.ShapeDtypeStruct((3, local_n, beads), jnp.float32),
        in_specs=[vmem],
        out_specs=vmem,
        name="total",
    )(back)
    return jnp.swapaxes(total, 0, 1)


def solution(mesh):
    return jax.shard_map(
        on_device,
        mesh=mesh,
        in_specs=(P("ens", None, "tile"), P("tile", None), P()),
        out_specs=P("ens", None, "tile"),
        check_vma=False,
    )
```

```python
import functools

import jax
import jax.numpy as jnp
from jax import lax
from jax.experimental import pallas as pl
from jax.experimental.pallas import tpu as pltpu
from jax.sharding import PartitionSpec as P

LANES = 128
WIDE = 256
SLOT = 64
SLICE = 16
NT = (((1,), (1,)), ((), ()))


def up(n, unit):
    return -(-n // unit) * unit


def split3(v):
    hi = v.astype(jnp.bfloat16).astype(jnp.float32)
    rest = v - hi
    mid = rest.astype(jnp.bfloat16).astype(jnp.float32)
    return hi, mid, rest - mid


def pack_kernel(n_p, n_q, xyz_ref, send_ref):
    beads = xyz_ref.shape[2]
    n_rows, piece = beads // n_p, beads // n_q
    for c in range(3):
        for q in range(n_q):
            for p in range(n_p):
                e = q * n_p + p
                send_ref[e, :, pl.ds(c * piece, piece)] = xyz_ref[c, :, pl.ds(q * piece, piece)]
                send_ref[e, :, pl.ds(3 * piece + c * n_rows, n_rows)] = xyz_ref[c, :, pl.ds(p * n_rows, n_rows)]


def sum_kernel(n_p, n_q, back_ref, total_ref):
    n_rows = back_ref.shape[3]
    for c in range(3):
        for p in range(n_p):
            total = back_ref[p, c]
            for q in range(1, n_q):
                total += back_ref[q * n_p + p, c]
            total_ref[c, :, pl.ds(p * n_rows, n_rows)] = total


def put_terms(refs, xyz, norm_row):
    norm = 1.5 - 0.5 * (xyz[0] * xyz[0] + xyz[1] * xyz[1] + xyz[2] * xyz[2])
    n, size = norm.shape
    wide = refs[0].shape[0] * LANES
    for f, v in ((0, xyz[0]), (1, xyz[1]), (2, xyz[2]), (norm_row, norm)):
        if wide > size:
            v = jnp.concatenate([v, jnp.zeros((n, wide - size), jnp.float32)], axis=1)
        for ref, term in zip(refs, split3(v)):
            for k in range(wide // LANES):
                ref[k, pl.ds(f, n, 8), :] = term[:, k * LANES:(k + 1) * LANES]


def get_terms(refs, i):
    return [jnp.concatenate([ref[k, pl.ds(8 * i, 8), :] for k in range(ref.shape[0])], axis=1) for ref in refs]


def pair_kernel(tiles, fold, base_ref, seg_rows_ref, seg_cols_ref, col_ids_ref, counts_ref, both_ref, *rest):
    piece_refs = rest[:tiles - 1]
    (grad_ref, row_terms, col_terms, lhs_ref, lhs_end_ref, rhs_ref, rhs_end_ref, terms_end_ref, weight_ref,
     weight_end_ref) = rest[tiles - 1:]
    groups, per, _ = both_ref.shape
    structs = groups * per
    n_rows, n_cols = counts_ref.shape
    piece = n_cols // tiles
    deep = weight_ref.shape[0]
    full = rhs_ref.shape[2]
    end = n_cols - full
    chunks = [(a, min(WIDE, full - a)) for a in range(0, full, WIDE)]
    slices = [(a, min(SLICE, deep - a)) for a in range(0, deep, SLICE)]

    for norm_row, one_row, refs in ((3, 4, row_terms), (4, 3, col_terms)):
        for ref in refs:
            ref[...] = jnp.zeros_like(ref)
        for k in range(refs[0].shape[0]):
            refs[0][k, pl.ds(one_row, per, 8), :] = jnp.ones((per, LANES), jnp.float32)
    if end:
        rhs_end_ref[...] = jnp.zeros_like(rhs_end_ref)

    def features(g, carry):
        both = both_ref[g]
        parts = [both] + [ref[g] for ref in piece_refs]
        cols = [jnp.concatenate([v[:, c * piece:(c + 1) * piece] for v in parts], axis=1) for c in range(3)]
        rows = [both[:, 3 * piece + c * n_rows:3 * piece + (c + 1) * n_rows] for c in range(3)]
        put_terms(row_terms, rows, 3)
        put_terms(col_terms, cols, 4)
        for block in range(per // fold):
            lefts = []
            for inside in range(fold):
                i = block * fold + inside
                s = g * per + i
                hi, mid, lo = get_terms(row_terms, i)
                left = jnp.concatenate([hi, hi, mid, mid, hi, lo], axis=0)
                lhs_ref[s] = left.T[:deep].astype(jnp.bfloat16)
                if end:
                    lefts += [left, jnp.zeros((SLOT - 48, left.shape[1]), jnp.float32)]
                hi, mid, lo = get_terms(col_terms, i)
                right = jnp.concatenate([hi, mid, hi, mid, lo, hi], axis=0)
                rhs_ref[s] = right[:, :full].astype(jnp.bfloat16)
                if end:
                    lane = lax.broadcasted_iota(jnp.int32, (48, LANES), 1)
                    last = jnp.where(lane < end, right[:, full:full + LANES], 0.0)
                    if inside:
                        last = pltpu.roll(last, inside * end, 1)
                    last = last.astype(jnp.bfloat16)
                    b = g * (per // fold) + block
                    rhs_end_ref[b, pl.ds(SLOT * inside, 48), :] = last
                    terms_end_ref[b, pl.ds(16 * inside, 16), :] = last[0:16]
            if end:
                lhs_end_ref[g * (per // fold) + block] = jnp.concatenate(lefts, axis=0).T[:deep].astype(jnp.bfloat16)
        return carry

    lax.fori_loop(0, groups, features, 0)
    weight_ref[...] = jnp.zeros_like(weight_ref)
    if end:
        weight_end_ref[...] = jnp.zeros_like(weight_end_ref)

    def half_block(s, start, size):
        return jnp.dot(lhs_ref[s], rhs_ref[s, :, pl.ds(start, size)], preferred_element_type=jnp.float32)

    def half_end(b):
        return jnp.dot(lhs_end_ref[b], rhs_end_ref[b], preferred_element_type=jnp.float32)

    def add_some(b, carry):
        for inside in range(fold):
            for start, size in chunks:
                half = half_block(b * fold + inside, start, size)
                for a, n in slices:
                    weight_ref[pl.ds(a, n), pl.ds(start, size)] += jnp.tanh(half[a:a + n])
        if end:
            half = half_end(b)
            for a, n in slices:
                weight_end_ref[pl.ds(a, n), :] += jnp.tanh(half[a:a + n])
        return carry

    lax.fori_loop(0, structs // fold, add_some, 0)

    def mask_and_target(start, size):
        count = counts_ref[:, pl.ds(start, size)].astype(jnp.float32)
        row_ids = base_ref[0] + lax.broadcasted_iota(jnp.int32, (n_rows, size), 0)
        mask = jnp.where(seg_rows_ref[...] == seg_cols_ref[:, pl.ds(start, size)], 1.0, 0.3)
        mask = jnp.where(row_ids == col_ids_ref[:, pl.ds(start, size)], 0.0, mask)
        return mask, mask * (count / (count + 8.0))

    scale = 0.5 / structs
    for start, size in chunks:
        mask, goal = mask_and_target(start, size)
        total = weight_ref[pl.ds(0, n_rows), pl.ds(start, size)]
        weight_ref[pl.ds(0, n_rows), pl.ds(start, size)] = mask * (0.5 + scale * total) - goal
    if deep > n_rows:
        weight_ref[pl.ds(n_rows, deep - n_rows), :] = jnp.zeros((deep - n_rows, full), jnp.float32)
    if end:
        def spread(v):
            v = jnp.concatenate([v, jnp.zeros((n_rows, LANES - end), jnp.float32)], axis=1)
            return sum((pltpu.roll(v, k * end, 1) for k in range(1, fold)), v)

        mask, goal = [spread(v) for v in mask_and_target(full, end)]
        part = weight_end_ref[pl.ds(0, n_rows), :]
        total = sum((pltpu.roll(part, k * end, 1) for k in range(1, fold)), part)
        weight_end_ref[pl.ds(0, n_rows), :] = mask * (0.5 + scale * total) - goal
        if deep > n_rows:
            weight_end_ref[pl.ds(n_rows, deep - n_rows), :] = jnp.zeros((deep - n_rows, LANES), jnp.float32)

    def split2(ref, start, size, half):
        his, los = [], []
        for a, n in slices:
            t = jnp.tanh(half[a:a + n])
            g = ref[pl.ds(a, n), pl.ds(start, size)] * (1.0 - t * t)
            hi = g.astype(jnp.bfloat16)
            his.append(hi)
            los.append((g - hi.astype(jnp.float32)).astype(jnp.bfloat16))
        return [jnp.concatenate(his, axis=0), jnp.concatenate(los, axis=0)]

    def sums(terms, parts):
        return lax.dot_general(jnp.concatenate(parts, axis=1), jnp.concatenate(terms, axis=1), NT,
                               preferred_element_type=jnp.float32)

    def grad_some(b, carry):
        if end:
            last = sums([terms_end_ref[b]] * 2, split2(weight_end_ref, 0, LANES, half_end(b))).T
        for inside in range(fold):
            s = b * fold + inside
            terms, parts = [], []
            for start, size in chunks:
                terms += [rhs_ref[s, pl.ds(0, 16), pl.ds(start, size)]] * 2
                parts += split2(weight_ref, start, size, half_block(s, start, size))
            total = sums(terms, parts)
            total = total.T
            if end:
                total += last[16 * inside:16 * inside + 16]
            total = total[:, :n_rows]
            g, i = lax.div(s, per), lax.rem(s, per)
            both = both_ref[g, pl.ds(i, 1), :]
            for c in range(3):
                xyz = both[:, 3 * piece + c * n_rows:3 * piece + (c + 1) * n_rows]
                grad_ref[g, c, pl.ds(i, 1), :] = (0.25 / 16) * (
                    total[c:c + 1] + total[8 + c:9 + c] - total[3:4] * xyz)
        return carry

    lax.fori_loop(0, structs // fold, grad_some, 0)


def split_ens(n_ens, beads, tiles):
    best = None
    for parts in range(1, n_ens + 1):
        if n_ens % parts or beads % parts or beads % (n_ens // parts):
            continue
        cost = 2 * (beads // parts) + tiles * (beads // (n_ens // parts))
        if best is None or cost < best[0]:
            best = (cost, parts)
    return best[1]


def on_device(coords, counts, segments):
    local_n, _, beads = coords.shape
    n_tile = lax.axis_size("tile")
    n_ens = lax.axis_size("ens")
    structs = local_n * n_ens
    n_p = split_ens(n_ens, beads, n_tile)
    n_q = n_ens // n_p
    n_rows, piece = beads // n_p, beads // n_q
    n_cols = piece * n_tile
    tile, ens = lax.axis_index("tile"), lax.axis_index("ens")
    p, q = lax.rem(ens, n_p), lax.div(ens, n_p)
    vmem = pl.BlockSpec(memory_space=pltpu.VMEM)

    send = pl.pallas_call(
        functools.partial(pack_kernel, n_p, n_q),
        out_shape=jax.ShapeDtypeStruct((n_ens, local_n, 3 * (piece + n_rows)), jnp.float32),
        in_specs=[vmem],
        out_specs=vmem,
        name="pack",
    )(jnp.swapaxes(coords, 0, 1))
    both = lax.all_to_all(send, "ens", 0, 0, tiled=True)
    own = both[:, :, :3 * piece]
    pieces = [lax.ppermute(own, "tile", [(t, (t - k) % n_tile) for t in range(n_tile)]) for k in range(1, n_tile)]

    row_base = tile * beads + p * n_rows
    col_bases = [lax.rem(tile + k, n_tile) * beads + q * piece for k in range(n_tile)]
    own_counts = lax.dynamic_slice_in_dim(counts, p * n_rows, n_rows, 0)
    block = jnp.concatenate([lax.dynamic_slice_in_dim(own_counts, b, piece, 1) for b in col_bases], axis=1)
    seg_cols = jnp.concatenate([lax.dynamic_slice_in_dim(segments, b, piece) for b in col_bases])[None, :]
    col_ids = jnp.concatenate([b + jnp.arange(piece, dtype=jnp.int32) for b in col_bases])[None, :]
    seg_rows = lax.dynamic_slice_in_dim(segments, row_base, n_rows)[:, None]

    full = n_cols // LANES * LANES
    end = n_cols - full
    fold = LANES // end if end and LANES % end == 0 and local_n % (LANES // end) == 0 else 1
    deep = up(n_rows, 16)
    row_wide, col_wide = up(n_rows, LANES), up(n_cols, LANES)
    blocks = structs // fold
    grad = pl.pallas_call(
        functools.partial(pair_kernel, n_tile, fold),
        out_shape=jax.ShapeDtypeStruct((n_ens, 3, local_n, n_rows), jnp.float32),
        in_specs=[pl.BlockSpec(memory_space=pltpu.SMEM)] + [vmem] * (4 + n_tile),
        out_specs=vmem,
        scratch_shapes=[
            [pltpu.VMEM((row_wide // LANES, 8 * local_n, LANES), jnp.float32)] * 3,
            [pltpu.VMEM((col_wide // LANES, 8 * local_n, LANES), jnp.float32)] * 3,
            pltpu.VMEM((structs, deep, 48), jnp.bfloat16),
            pltpu.VMEM((blocks, deep, fold * SLOT), jnp.bfloat16),
            pltpu.VMEM((structs, 48, full), jnp.bfloat16),
            pltpu.VMEM((blocks, fold * SLOT, LANES), jnp.bfloat16),
            pltpu.VMEM((blocks, fold * 16, LANES), jnp.bfloat16),
            pltpu.VMEM((deep, full), jnp.float32),
            pltpu.VMEM((deep, LANES), jnp.float32),
        ],
        compiler_params=pltpu.CompilerParams(vmem_limit_bytes=48 << 20),
        name="pairs",
    )(row_base[None], seg_rows, seg_cols, col_ids, block, both, *pieces)

    back = lax.all_to_all(grad, "ens", 0, 0, tiled=True)
    total = pl.pallas_call(
        functools.partial(sum_kernel, n_p, n_q),
        out_shape=jax.ShapeDtypeStruct((3, local_n, beads), jnp.float32),
        in_specs=[vmem],
        out_specs=vmem,
        name="total",
    )(back)
    return jnp.swapaxes(total, 0, 1)


def solution(mesh):
    return jax.shard_map(
        on_device,
        mesh=mesh,
        in_specs=(P("ens", None, "tile"), P("tile", None), P()),
        out_specs=P("ens", None, "tile"),
        check_vma=False,
    )
```

```python
import functools

import jax
import jax.numpy as jnp
from jax import lax
from jax.experimental import pallas as pl
from jax.experimental.pallas import tpu as pltpu
from jax.sharding import PartitionSpec as P

LANES = 128
WIDE = 256
SLOT = 64
UNROLL = 2
NT = (((1,), (1,)), ((), ()))


def up(n, unit):
    return -(-n // unit) * unit


def split3(v):
    hi = v.astype(jnp.bfloat16).astype(jnp.float32)
    rest = v - hi
    mid = rest.astype(jnp.bfloat16).astype(jnp.float32)
    return hi, mid, rest - mid


def pack_kernel(n_p, n_q, xyz_ref, send_ref):
    beads = xyz_ref.shape[2]
    n_rows, piece = beads // n_p, beads // n_q
    for c in range(3):
        for q in range(n_q):
            for p in range(n_p):
                e = q * n_p + p
                send_ref[e, :, pl.ds(c * piece, piece)] = xyz_ref[c, :, pl.ds(q * piece, piece)]
                send_ref[e, :, pl.ds(3 * piece + c * n_rows, n_rows)] = xyz_ref[c, :, pl.ds(p * n_rows, n_rows)]


def sum_kernel(n_p, n_q, back_ref, total_ref):
    n_rows = back_ref.shape[3]
    for c in range(3):
        for p in range(n_p):
            total = back_ref[p, c]
            for q in range(1, n_q):
                total += back_ref[q * n_p + p, c]
            total_ref[c, :, pl.ds(p * n_rows, n_rows)] = total


def put_terms(refs, xyz, norm_row):
    norm = 1.5 - 0.5 * (xyz[0] * xyz[0] + xyz[1] * xyz[1] + xyz[2] * xyz[2])
    n, size = norm.shape
    wide = refs[0].shape[0] * LANES
    for f, v in ((0, xyz[0]), (1, xyz[1]), (2, xyz[2]), (norm_row, norm)):
        if wide > size:
            v = jnp.concatenate([v, jnp.zeros((n, wide - size), jnp.float32)], axis=1)
        for ref, term in zip(refs, split3(v)):
            for k in range(wide // LANES):
                ref[k, pl.ds(f, n, 8), :] = term[:, k * LANES:(k + 1) * LANES]


def get_terms(refs, i):
    return [jnp.concatenate([ref[k, pl.ds(8 * i, 8), :] for k in range(ref.shape[0])], axis=1) for ref in refs]


def init_terms(refs, one_row, per):
    for ref in refs:
        ref[...] = jnp.zeros_like(ref)
    for k in range(refs[0].shape[0]):
        refs[0][k, pl.ds(one_row, per, 8), :] = jnp.ones((per, LANES), jnp.float32)


def row_kernel(n_rows, fold, both_ref, lhs_ref, lhs_end_ref, row_terms):
    groups, per, width = both_ref.shape
    deep = lhs_ref.shape[1]
    first = width - 3 * n_rows
    init_terms(row_terms, 4, per)

    def features(g, carry):
        both = both_ref[g]
        put_terms(row_terms, [both[:, first + c * n_rows:first + (c + 1) * n_rows] for c in range(3)], 3)
        for block in range(per // fold):
            lefts = []
            for inside in range(fold):
                i = block * fold + inside
                hi, mid, lo = get_terms(row_terms, i)
                left = jnp.concatenate([hi, hi, mid, mid, hi, lo], axis=0)
                lhs_ref[g * per + i] = left.T[:deep].astype(jnp.bfloat16)
                lefts += [left, jnp.zeros((SLOT - 48, left.shape[1]), jnp.float32)]
            lhs_end_ref[g * (per // fold) + block] = jnp.concatenate(lefts, axis=0).T[:deep].astype(jnp.bfloat16)
        return carry

    lax.fori_loop(0, groups, features, 0)


def pair_kernel(tiles, fold, base_ref, seg_rows_ref, seg_cols_ref, col_ids_ref, counts_ref, lhs_ref, lhs_end_ref,
                both_ref, *rest):
    piece_refs = rest[:tiles - 1]
    grad_ref, col_terms, rhs_ref, rhs_end_ref, terms_end_ref, weight_ref, weight_end_ref = rest[tiles - 1:]
    groups, per, _ = both_ref.shape
    structs = groups * per
    n_rows, n_cols = counts_ref.shape
    piece = n_cols // tiles
    deep = weight_ref.shape[0]
    full = rhs_ref.shape[2]
    end = n_cols - full
    chunks = [(a, min(WIDE, full - a)) for a in range(0, full, WIDE)]

    init_terms(col_terms, 3, per)
    if end:
        rhs_end_ref[...] = jnp.zeros_like(rhs_end_ref)

    def features(g, carry):
        both = both_ref[g]
        parts = [both] + [ref[g] for ref in piece_refs]
        cols = [jnp.concatenate([v[:, c * piece:(c + 1) * piece] for v in parts], axis=1) for c in range(3)]
        put_terms(col_terms, cols, 4)
        for block in range(per // fold):
            for inside in range(fold):
                i = block * fold + inside
                s = g * per + i
                hi, mid, lo = get_terms(col_terms, i)
                right = jnp.concatenate([hi, mid, hi, mid, lo, hi], axis=0)
                rhs_ref[s] = right[:, :full].astype(jnp.bfloat16)
                if end:
                    lane = lax.broadcasted_iota(jnp.int32, (48, LANES), 1)
                    last = jnp.where(lane < end, right[:, full:full + LANES], 0.0)
                    if inside:
                        last = pltpu.roll(last, inside * end, 1)
                    last = last.astype(jnp.bfloat16)
                    b = g * (per // fold) + block
                    rhs_end_ref[b, pl.ds(SLOT * inside, 48), :] = last
                    terms_end_ref[b, pl.ds(16 * inside, 16), :] = last[0:16]
        return carry

    lax.fori_loop(0, groups, features, 0)
    weight_ref[...] = jnp.zeros_like(weight_ref)
    if end:
        weight_end_ref[...] = jnp.zeros_like(weight_end_ref)

    def tanh_block(s, start, size):
        return jnp.tanh(jnp.dot(lhs_ref[s], rhs_ref[s, :, pl.ds(start, size)], preferred_element_type=jnp.float32))

    def tanh_end(b):
        return jnp.tanh(jnp.dot(lhs_end_ref[b], rhs_end_ref[b], preferred_element_type=jnp.float32))

    def add_some(b, carry):
        for inside in range(fold):
            for start, size in chunks:
                weight_ref[:, pl.ds(start, size)] += tanh_block(b * fold + inside, start, size)
        if end:
            weight_end_ref[...] += tanh_end(b)
        return carry

    lax.fori_loop(0, structs // fold, add_some, 0, unroll=UNROLL)

    def mask_and_target(start, size):
        count = counts_ref[:, pl.ds(start, size)].astype(jnp.float32)
        row_ids = base_ref[0] + lax.broadcasted_iota(jnp.int32, (n_rows, size), 0)
        mask = jnp.where(seg_rows_ref[...] == seg_cols_ref[:, pl.ds(start, size)], 1.0, 0.3)
        mask = jnp.where(row_ids == col_ids_ref[:, pl.ds(start, size)], 0.0, mask)
        return mask, mask * (count / (count + 8.0))

    scale = 0.5 / structs
    for start, size in chunks:
        mask, goal = mask_and_target(start, size)
        total = weight_ref[pl.ds(0, n_rows), pl.ds(start, size)]
        weight_ref[pl.ds(0, n_rows), pl.ds(start, size)] = mask * (0.5 + scale * total) - goal
    if deep > n_rows:
        weight_ref[pl.ds(n_rows, deep - n_rows), :] = jnp.zeros((deep - n_rows, full), jnp.float32)
    if end:
        def spread(v):
            v = jnp.concatenate([v, jnp.zeros((n_rows, LANES - end), jnp.float32)], axis=1)
            return sum((pltpu.roll(v, k * end, 1) for k in range(1, fold)), v)

        mask, goal = [spread(v) for v in mask_and_target(full, end)]
        part = weight_end_ref[pl.ds(0, n_rows), :]
        total = sum((pltpu.roll(part, k * end, 1) for k in range(1, fold)), part)
        weight_end_ref[pl.ds(0, n_rows), :] = mask * (0.5 + scale * total) - goal
        if deep > n_rows:
            weight_end_ref[pl.ds(n_rows, deep - n_rows), :] = jnp.zeros((deep - n_rows, LANES), jnp.float32)

    def split2(weight, t):
        g = weight * (1.0 - t * t)
        hi = g.astype(jnp.bfloat16)
        return [hi, (g - hi.astype(jnp.float32)).astype(jnp.bfloat16)]

    def sums(terms, parts):
        return lax.dot_general(jnp.concatenate(parts, axis=1), jnp.concatenate(terms, axis=1), NT,
                               preferred_element_type=jnp.float32)

    def grad_some(b, carry):
        if end:
            last = sums([terms_end_ref[b]] * 2, split2(weight_end_ref[...], tanh_end(b))).T
        for inside in range(fold):
            s = b * fold + inside
            terms, parts = [], []
            for start, size in chunks:
                terms += [rhs_ref[s, pl.ds(0, 16), pl.ds(start, size)]] * 2
                parts += split2(weight_ref[:, pl.ds(start, size)], tanh_block(s, start, size))
            total = sums(terms, parts)
            total = total.T
            if end:
                total += last[16 * inside:16 * inside + 16]
            total = total[:, :n_rows]
            g, i = lax.div(s, per), lax.rem(s, per)
            both = both_ref[g, pl.ds(i, 1), :]
            for c in range(3):
                xyz = both[:, 3 * piece + c * n_rows:3 * piece + (c + 1) * n_rows]
                grad_ref[g, c, pl.ds(i, 1), :] = (0.25 / 16) * (
                    total[c:c + 1] + total[8 + c:9 + c] - total[3:4] * xyz)
        return carry

    lax.fori_loop(0, structs // fold, grad_some, 0, unroll=UNROLL)


def split_ens(n_ens, beads, tiles):
    best = None
    for parts in range(1, n_ens + 1):
        if n_ens % parts or beads % parts or beads % (n_ens // parts):
            continue
        cost = 2 * (beads // parts) + tiles * (beads // (n_ens // parts))
        if best is None or cost < best[0]:
            best = (cost, parts)
    return best[1]


def on_device(coords, counts, segments):
    local_n, _, beads = coords.shape
    n_tile = lax.axis_size("tile")
    n_ens = lax.axis_size("ens")
    structs = local_n * n_ens
    n_p = split_ens(n_ens, beads, n_tile)
    n_q = n_ens // n_p
    n_rows, piece = beads // n_p, beads // n_q
    n_cols = piece * n_tile
    tile, ens = lax.axis_index("tile"), lax.axis_index("ens")
    p, q = lax.rem(ens, n_p), lax.div(ens, n_p)
    vmem = pl.BlockSpec(memory_space=pltpu.VMEM)

    send = pl.pallas_call(
        functools.partial(pack_kernel, n_p, n_q),
        out_shape=jax.ShapeDtypeStruct((n_ens, local_n, 3 * (piece + n_rows)), jnp.float32),
        in_specs=[vmem],
        out_specs=vmem,
        name="pack",
    )(jnp.swapaxes(coords, 0, 1))
    both = lax.all_to_all(send, "ens", 0, 0, tiled=True)
    own = both[:, :, :3 * piece]
    pieces = [lax.ppermute(own, "tile", [(t, (t - k) % n_tile) for t in range(n_tile)]) for k in range(1, n_tile)]

    row_base = tile * beads + p * n_rows
    col_bases = [lax.rem(tile + k, n_tile) * beads + q * piece for k in range(n_tile)]
    own_counts = lax.dynamic_slice_in_dim(counts, p * n_rows, n_rows, 0)
    block = jnp.concatenate([lax.dynamic_slice_in_dim(own_counts, b, piece, 1) for b in col_bases], axis=1)
    seg_cols = jnp.concatenate([lax.dynamic_slice_in_dim(segments, b, piece) for b in col_bases])[None, :]
    col_ids = jnp.concatenate([b + jnp.arange(piece, dtype=jnp.int32) for b in col_bases])[None, :]
    seg_rows = lax.dynamic_slice_in_dim(segments, row_base, n_rows)[:, None]

    full = n_cols // LANES * LANES
    end = n_cols - full
    fold = LANES // end if end and LANES % end == 0 and local_n % (LANES // end) == 0 else 1
    deep = up(n_rows, 16)
    row_wide, col_wide = up(n_rows, LANES), up(n_cols, LANES)
    blocks = structs // fold
    lhs, lhs_end = pl.pallas_call(
        functools.partial(row_kernel, n_rows, fold),
        out_shape=[
            jax.ShapeDtypeStruct((structs, deep, 48), jnp.bfloat16),
            jax.ShapeDtypeStruct((blocks, deep, fold * SLOT), jnp.bfloat16),
        ],
        in_specs=[vmem],
        out_specs=[vmem] * 2,
        scratch_shapes=[[pltpu.VMEM((row_wide // LANES, 8 * local_n, LANES), jnp.float32)] * 3],
        compiler_params=pltpu.CompilerParams(vmem_limit_bytes=32 << 20),
        name="rows",
    )(both)
    grad = pl.pallas_call(
        functools.partial(pair_kernel, n_tile, fold),
        out_shape=jax.ShapeDtypeStruct((n_ens, 3, local_n, n_rows), jnp.float32),
        in_specs=[pl.BlockSpec(memory_space=pltpu.SMEM)] + [vmem] * (6 + n_tile),
        out_specs=vmem,
        scratch_shapes=[
            [pltpu.VMEM((col_wide // LANES, 8 * local_n, LANES), jnp.float32)] * 3,
            pltpu.VMEM((structs, 48, full), jnp.bfloat16),
            pltpu.VMEM((blocks, fold * SLOT, LANES), jnp.bfloat16),
            pltpu.VMEM((blocks, fold * 16, LANES), jnp.bfloat16),
            pltpu.VMEM((deep, full), jnp.float32),
            pltpu.VMEM((deep, LANES), jnp.float32),
        ],
        compiler_params=pltpu.CompilerParams(vmem_limit_bytes=40 << 20),
        name="pairs",
    )(row_base[None], seg_rows, seg_cols, col_ids, block, lhs, lhs_end, both, *pieces)

    back = lax.all_to_all(grad, "ens", 0, 0, tiled=True)
    total = pl.pallas_call(
        functools.partial(sum_kernel, n_p, n_q),
        out_shape=jax.ShapeDtypeStruct((3, local_n, beads), jnp.float32),
        in_specs=[vmem],
        out_specs=vmem,
        name="total",
    )(back)
    return jnp.swapaxes(total, 0, 1)


def solution(mesh):
    return jax.shard_map(
        on_device,
        mesh=mesh,
        in_specs=(P("ens", None, "tile"), P("tile", None), P()),
        out_specs=P("ens", None, "tile"),
        check_vma=False,
    )
```

```python
import functools

import jax
import jax.numpy as jnp
from jax import lax
from jax.experimental import pallas as pl
from jax.experimental.pallas import tpu as pltpu
from jax.sharding import PartitionSpec as P

LANES = 128
WIDE = 256
SLOT = 64
UNROLL = 4
NT = (((1,), (1,)), ((), ()))


def up(n, unit):
    return -(-n // unit) * unit


def split3(v):
    hi = v.astype(jnp.bfloat16).astype(jnp.float32)
    rest = v - hi
    mid = rest.astype(jnp.bfloat16).astype(jnp.float32)
    return hi, mid, rest - mid


def pack_kernel(n_p, n_q, xyz_ref, send_ref):
    beads = xyz_ref.shape[2]
    n_rows, piece = beads // n_p, beads // n_q
    for c in range(3):
        for q in range(n_q):
            for p in range(n_p):
                e = q * n_p + p
                send_ref[e, :, pl.ds(c * piece, piece)] = xyz_ref[c, :, pl.ds(q * piece, piece)]
                send_ref[e, :, pl.ds(3 * piece + c * n_rows, n_rows)] = xyz_ref[c, :, pl.ds(p * n_rows, n_rows)]


def sum_kernel(n_p, n_q, back_ref, total_ref):
    n_rows = back_ref.shape[3]
    for c in range(3):
        for p in range(n_p):
            total = back_ref[p, c]
            for q in range(1, n_q):
                total += back_ref[q * n_p + p, c]
            total_ref[c, :, pl.ds(p * n_rows, n_rows)] = total


def put_terms(refs, xyz, norm_row):
    norm = 1.5 - 0.5 * (xyz[0] * xyz[0] + xyz[1] * xyz[1] + xyz[2] * xyz[2])
    n, size = norm.shape
    wide = refs[0].shape[0] * LANES
    for f, v in ((0, xyz[0]), (1, xyz[1]), (2, xyz[2]), (norm_row, norm)):
        if wide > size:
            v = jnp.concatenate([v, jnp.zeros((n, wide - size), jnp.float32)], axis=1)
        for ref, term in zip(refs, split3(v)):
            for k in range(wide // LANES):
                ref[k, pl.ds(f, n, 8), :] = term[:, k * LANES:(k + 1) * LANES]


def get_terms(refs, i):
    return [jnp.concatenate([ref[k, pl.ds(8 * i, 8), :] for k in range(ref.shape[0])], axis=1) for ref in refs]


def init_terms(refs, one_row, per):
    for ref in refs:
        ref[...] = jnp.zeros_like(ref)
    for k in range(refs[0].shape[0]):
        refs[0][k, pl.ds(one_row, per, 8), :] = jnp.ones((per, LANES), jnp.float32)


def row_kernel(n_rows, fold, both_ref, lhs_ref, lhs_end_ref, row_terms):
    groups, per, width = both_ref.shape
    deep = lhs_ref.shape[1]
    first = width - 3 * n_rows
    init_terms(row_terms, 4, per)

    def features(g, carry):
        both = both_ref[g]
        put_terms(row_terms, [both[:, first + c * n_rows:first + (c + 1) * n_rows] for c in range(3)], 3)
        for block in range(per // fold):
            lefts = []
            for inside in range(fold):
                i = block * fold + inside
                hi, mid, lo = get_terms(row_terms, i)
                left = jnp.concatenate([hi, hi, mid, mid, hi, lo], axis=0)
                lhs_ref[g * per + i] = left.T[:deep].astype(jnp.bfloat16)
                lefts += [left, jnp.zeros((SLOT - 48, left.shape[1]), jnp.float32)]
            lhs_end_ref[g * (per // fold) + block] = jnp.concatenate(lefts, axis=0).T[:deep].astype(jnp.bfloat16)
        return carry

    lax.fori_loop(0, groups, features, 0)


def mask_kernel(fold, base_ref, seg_rows_ref, seg_cols_ref, col_ids_ref, counts_ref, mask_ref, goal_ref, mask_end_ref,
                goal_end_ref):
    n_rows, n_cols = counts_ref.shape
    deep, full = mask_ref.shape
    end = n_cols - full
    for ref in (mask_ref, goal_ref, mask_end_ref, goal_end_ref):
        if deep > n_rows:
            ref[pl.ds(n_rows, deep - n_rows), :] = jnp.zeros((deep - n_rows, ref.shape[1]), jnp.float32)

    def mask_and_goal(start, size):
        count = counts_ref[:, pl.ds(start, size)].astype(jnp.float32)
        row_ids = base_ref[0] + lax.broadcasted_iota(jnp.int32, (n_rows, size), 0)
        mask = jnp.where(seg_rows_ref[...] == seg_cols_ref[:, pl.ds(start, size)], 1.0, 0.3)
        mask = jnp.where(row_ids == col_ids_ref[:, pl.ds(start, size)], 0.0, mask)
        return mask, mask * (count / (count + 8.0))

    rows = pl.ds(0, n_rows)
    for start in range(0, full, LANES):
        mask_ref[rows, pl.ds(start, LANES)], goal_ref[rows, pl.ds(start, LANES)] = mask_and_goal(start, LANES)
    if end:
        def spread(v):
            v = jnp.concatenate([v, jnp.zeros((n_rows, LANES - end), jnp.float32)], axis=1)
            return sum((pltpu.roll(v, k * end, 1) for k in range(1, fold)), v)

        mask_end_ref[rows, :], goal_end_ref[rows, :] = [spread(v) for v in mask_and_goal(full, end)]


def pair_kernel(tiles, fold, n_rows, n_cols, mask_ref, goal_ref, mask_end_ref, goal_end_ref, lhs_ref, lhs_end_ref,
                both_ref, *rest):
    piece_refs = rest[:tiles - 1]
    grad_ref, col_terms, rhs_ref, rhs_end_ref, terms_end_ref, weight_ref, weight_end_ref = rest[tiles - 1:]
    groups, per, _ = both_ref.shape
    structs = groups * per
    piece = n_cols // tiles
    deep = weight_ref.shape[0]
    full = rhs_ref.shape[2]
    end = n_cols - full
    chunks = [(a, min(WIDE, full - a)) for a in range(0, full, WIDE)]

    init_terms(col_terms, 3, per)
    if end:
        rhs_end_ref[...] = jnp.zeros_like(rhs_end_ref)

    def features(g, carry):
        both = both_ref[g]
        parts = [both] + [ref[g] for ref in piece_refs]
        cols = [jnp.concatenate([v[:, c * piece:(c + 1) * piece] for v in parts], axis=1) for c in range(3)]
        put_terms(col_terms, cols, 4)
        for block in range(per // fold):
            for inside in range(fold):
                i = block * fold + inside
                s = g * per + i
                hi, mid, lo = get_terms(col_terms, i)
                right = jnp.concatenate([hi, mid, hi, mid, lo, hi], axis=0)
                rhs_ref[s] = right[:, :full].astype(jnp.bfloat16)
                if end:
                    lane = lax.broadcasted_iota(jnp.int32, (48, LANES), 1)
                    last = jnp.where(lane < end, right[:, full:full + LANES], 0.0)
                    if inside:
                        last = pltpu.roll(last, inside * end, 1)
                    last = last.astype(jnp.bfloat16)
                    b = g * (per // fold) + block
                    rhs_end_ref[b, pl.ds(SLOT * inside, 48), :] = last
                    terms_end_ref[b, pl.ds(16 * inside, 16), :] = last[0:16]
        return carry

    lax.fori_loop(0, groups, features, 0)
    weight_ref[...] = jnp.zeros_like(weight_ref)
    if end:
        weight_end_ref[...] = jnp.zeros_like(weight_end_ref)

    def tanh_block(s, start, size):
        return jnp.tanh(jnp.dot(lhs_ref[s], rhs_ref[s, :, pl.ds(start, size)], preferred_element_type=jnp.float32))

    def tanh_end(b):
        return jnp.tanh(jnp.dot(lhs_end_ref[b], rhs_end_ref[b], preferred_element_type=jnp.float32))

    def add_some(b, carry):
        for inside in range(fold):
            for start, size in chunks:
                weight_ref[:, pl.ds(start, size)] += tanh_block(b * fold + inside, start, size)
        if end:
            weight_end_ref[...] += tanh_end(b)
        return carry

    lax.fori_loop(0, structs // fold, add_some, 0, unroll=UNROLL)

    scale = 0.5 / structs
    for start, size in chunks:
        cut = pl.ds(start, size)
        weight_ref[:, cut] = mask_ref[:, cut] * (0.5 + scale * weight_ref[:, cut]) - goal_ref[:, cut]
    if end:
        part = weight_end_ref[...]
        total = sum((pltpu.roll(part, k * end, 1) for k in range(1, fold)), part)
        weight_end_ref[...] = mask_end_ref[...] * (0.5 + scale * total) - goal_end_ref[...]

    def split2(weight, t):
        g = weight * (1.0 - t * t)
        hi = g.astype(jnp.bfloat16)
        return [hi, (g - hi.astype(jnp.float32)).astype(jnp.bfloat16)]

    def sums(terms, parts):
        return lax.dot_general(jnp.concatenate(parts, axis=1), jnp.concatenate(terms, axis=1), NT,
                               preferred_element_type=jnp.float32)

    def grad_some(b, carry):
        if end:
            last = sums([terms_end_ref[b]] * 2, split2(weight_end_ref[...], tanh_end(b))).T
        for inside in range(fold):
            s = b * fold + inside
            terms, parts = [], []
            for start, size in chunks:
                terms += [rhs_ref[s, pl.ds(0, 16), pl.ds(start, size)]] * 2
                parts += split2(weight_ref[:, pl.ds(start, size)], tanh_block(s, start, size))
            total = sums(terms, parts)
            total = total.T
            if end:
                total += last[16 * inside:16 * inside + 16]
            total = total[:, :n_rows]
            g, i = lax.div(s, per), lax.rem(s, per)
            both = both_ref[g, pl.ds(i, 1), :]
            for c in range(3):
                xyz = both[:, 3 * piece + c * n_rows:3 * piece + (c + 1) * n_rows]
                grad_ref[g, c, pl.ds(i, 1), :] = (0.25 / 16) * (
                    total[c:c + 1] + total[8 + c:9 + c] - total[3:4] * xyz)
        return carry

    lax.fori_loop(0, structs // fold, grad_some, 0, unroll=UNROLL)


def split_ens(n_ens, beads, tiles):
    best = None
    for parts in range(1, n_ens + 1):
        if n_ens % parts or beads % parts or beads % (n_ens // parts):
            continue
        cost = 2 * (beads // parts) + tiles * (beads // (n_ens // parts))
        if best is None or cost < best[0]:
            best = (cost, parts)
    return best[1]


def on_device(coords, counts, segments):
    local_n, _, beads = coords.shape
    n_tile = lax.axis_size("tile")
    n_ens = lax.axis_size("ens")
    structs = local_n * n_ens
    n_p = split_ens(n_ens, beads, n_tile)
    n_q = n_ens // n_p
    n_rows, piece = beads // n_p, beads // n_q
    n_cols = piece * n_tile
    tile, ens = lax.axis_index("tile"), lax.axis_index("ens")
    p, q = lax.rem(ens, n_p), lax.div(ens, n_p)
    vmem = pl.BlockSpec(memory_space=pltpu.VMEM)

    send = pl.pallas_call(
        functools.partial(pack_kernel, n_p, n_q),
        out_shape=jax.ShapeDtypeStruct((n_ens, local_n, 3 * (piece + n_rows)), jnp.float32),
        in_specs=[vmem],
        out_specs=vmem,
        name="pack",
    )(jnp.swapaxes(coords, 0, 1))
    both = lax.all_to_all(send, "ens", 0, 0, tiled=True)

    row_base = tile * beads + p * n_rows
    col_bases = [lax.rem(tile + k, n_tile) * beads + q * piece for k in range(n_tile)]
    own_counts = lax.dynamic_slice_in_dim(counts, p * n_rows, n_rows, 0)
    block = jnp.concatenate([lax.dynamic_slice_in_dim(own_counts, b, piece, 1) for b in col_bases], axis=1)
    seg_cols = jnp.concatenate([lax.dynamic_slice_in_dim(segments, b, piece) for b in col_bases])[None, :]
    col_ids = jnp.concatenate([b + jnp.arange(piece, dtype=jnp.int32) for b in col_bases])[None, :]
    seg_rows = lax.dynamic_slice_in_dim(segments, row_base, n_rows)[:, None]

    full = n_cols // LANES * LANES
    end = n_cols - full
    fold = LANES // end if end and LANES % end == 0 and local_n % (LANES // end) == 0 else 1
    deep = up(n_rows, 16)
    row_wide, col_wide = up(n_rows, LANES), up(n_cols, LANES)
    blocks = structs // fold
    masks = pl.pallas_call(
        functools.partial(mask_kernel, fold),
        out_shape=[jax.ShapeDtypeStruct((deep, width), jnp.float32) for width in (full, full, LANES, LANES)],
        in_specs=[pl.BlockSpec(memory_space=pltpu.SMEM)] + [vmem] * 4,
        out_specs=[vmem] * 4,
        compiler_params=pltpu.CompilerParams(vmem_limit_bytes=32 << 20),
        name="masks",
    )(row_base[None], seg_rows, seg_cols, col_ids, block)
    both, masks = lax.optimization_barrier((both, masks))
    own = both[:, :, :3 * piece]
    pieces = [lax.ppermute(own, "tile", [(t, (t - k) % n_tile) for t in range(n_tile)]) for k in range(1, n_tile)]

    lhs, lhs_end = pl.pallas_call(
        functools.partial(row_kernel, n_rows, fold),
        out_shape=[
            jax.ShapeDtypeStruct((structs, deep, 48), jnp.bfloat16),
            jax.ShapeDtypeStruct((blocks, deep, fold * SLOT), jnp.bfloat16),
        ],
        in_specs=[vmem],
        out_specs=[vmem] * 2,
        scratch_shapes=[[pltpu.VMEM((row_wide // LANES, 8 * local_n, LANES), jnp.float32)] * 3],
        compiler_params=pltpu.CompilerParams(vmem_limit_bytes=32 << 20),
        name="rows",
    )(both)
    grad = pl.pallas_call(
        functools.partial(pair_kernel, n_tile, fold, n_rows, n_cols),
        out_shape=jax.ShapeDtypeStruct((n_ens, 3, local_n, n_rows), jnp.float32),
        in_specs=[vmem] * (6 + n_tile),
        out_specs=vmem,
        scratch_shapes=[
            [pltpu.VMEM((col_wide // LANES, 8 * local_n, LANES), jnp.float32)] * 3,
            pltpu.VMEM((structs, 48, full), jnp.bfloat16),
            pltpu.VMEM((blocks, fold * SLOT, LANES), jnp.bfloat16),
            pltpu.VMEM((blocks, fold * 16, LANES), jnp.bfloat16),
            pltpu.VMEM((deep, full), jnp.float32),
            pltpu.VMEM((deep, LANES), jnp.float32),
        ],
        compiler_params=pltpu.CompilerParams(vmem_limit_bytes=40 << 20),
        name="pairs",
    )(*masks, lhs, lhs_end, both, *pieces)

    back = lax.all_to_all(grad, "ens", 0, 0, tiled=True)
    total = pl.pallas_call(
        functools.partial(sum_kernel, n_p, n_q),
        out_shape=jax.ShapeDtypeStruct((3, local_n, beads), jnp.float32),
        in_specs=[vmem],
        out_specs=vmem,
        name="total",
    )(back)
    return jnp.swapaxes(total, 0, 1)


def solution(mesh):
    return jax.shard_map(
        on_device,
        mesh=mesh,
        in_specs=(P("ens", None, "tile"), P("tile", None), P()),
        out_specs=P("ens", None, "tile"),
        check_vma=False,
    )
```

```python
import functools

import jax
import jax.numpy as jnp
from jax import lax
from jax.experimental import pallas as pl
from jax.experimental.pallas import tpu as pltpu
from jax.sharding import PartitionSpec as P

LANES = 128
WIDE = 256
SLOT = 64
UNROLL = 4
NT = (((1,), (1,)), ((), ()))


def up(n, unit):
    return -(-n // unit) * unit


def split3(v):
    hi = v.astype(jnp.bfloat16).astype(jnp.float32)
    rest = v - hi
    mid = rest.astype(jnp.bfloat16).astype(jnp.float32)
    return hi, mid, rest - mid


def pack_kernel(n_p, n_q, xyz_ref, send_ref):
    beads = xyz_ref.shape[2]
    n_rows, piece = beads // n_p, beads // n_q
    for c in range(3):
        for q in range(n_q):
            for p in range(n_p):
                e = q * n_p + p
                send_ref[e, :, pl.ds(c * piece, piece)] = xyz_ref[c, :, pl.ds(q * piece, piece)]
                send_ref[e, :, pl.ds(3 * piece + c * n_rows, n_rows)] = xyz_ref[c, :, pl.ds(p * n_rows, n_rows)]


def sum_kernel(n_p, n_q, back_ref, total_ref):
    n_rows = back_ref.shape[3]
    for c in range(3):
        for p in range(n_p):
            total = back_ref[p, c]
            for q in range(1, n_q):
                total += back_ref[q * n_p + p, c]
            total_ref[c, :, pl.ds(p * n_rows, n_rows)] = total


def put_terms(refs, xyz, norm_row):
    norm = 1.5 - 0.5 * (xyz[0] * xyz[0] + xyz[1] * xyz[1] + xyz[2] * xyz[2])
    n, size = norm.shape
    wide = refs[0].shape[0] * LANES
    for f, v in ((0, xyz[0]), (1, xyz[1]), (2, xyz[2]), (norm_row, norm)):
        if wide > size:
            v = jnp.concatenate([v, jnp.zeros((n, wide - size), jnp.float32)], axis=1)
        for ref, term in zip(refs, split3(v)):
            for k in range(wide // LANES):
                ref[k, pl.ds(f, n, 8), :] = term[:, k * LANES:(k + 1) * LANES]


def get_terms(refs, i):
    return [jnp.concatenate([ref[k, pl.ds(8 * i, 8), :] for k in range(ref.shape[0])], axis=1) for ref in refs]


def init_terms(refs, one_row, per):
    for ref in refs:
        ref[...] = jnp.zeros_like(ref)
    for k in range(refs[0].shape[0]):
        refs[0][k, pl.ds(one_row, per, 8), :] = jnp.ones((per, LANES), jnp.float32)


def row_kernel(n_rows, fold, both_ref, lhs_ref, lhs_end_ref, row_terms):
    groups, per, width = both_ref.shape
    deep = lhs_ref.shape[1]
    first = width - 3 * n_rows
    init_terms(row_terms, 4, per)

    def features(g, carry):
        both = both_ref[g]
        put_terms(row_terms, [both[:, first + c * n_rows:first + (c + 1) * n_rows] for c in range(3)], 3)
        for block in range(per // fold):
            lefts = []
            for inside in range(fold):
                i = block * fold + inside
                hi, mid, lo = get_terms(row_terms, i)
                left = jnp.concatenate([hi, hi, mid, mid, hi, lo], axis=0)
                lhs_ref[g * per + i] = left.T[:deep].astype(jnp.bfloat16)
                lefts += [left, jnp.zeros((SLOT - 48, left.shape[1]), jnp.float32)]
            lhs_end_ref[g * (per // fold) + block] = jnp.concatenate(lefts, axis=0).T[:deep].astype(jnp.bfloat16)
        return carry

    lax.fori_loop(0, groups, features, 0)


def mask_kernel(fold, base_ref, seg_rows_ref, seg_cols_ref, col_ids_ref, counts_ref, mask_ref, goal_ref, mask_end_ref,
                goal_end_ref):
    n_rows, n_cols = counts_ref.shape
    deep, full = mask_ref.shape
    end = n_cols - full
    for ref in (mask_ref, goal_ref, mask_end_ref, goal_end_ref):
        if deep > n_rows:
            ref[pl.ds(n_rows, deep - n_rows), :] = jnp.zeros((deep - n_rows, ref.shape[1]), jnp.float32)

    def mask_and_goal(start, size):
        count = counts_ref[:, pl.ds(start, size)].astype(jnp.float32)
        row_ids = base_ref[0] + lax.broadcasted_iota(jnp.int32, (n_rows, size), 0)
        mask = jnp.where(seg_rows_ref[...] == seg_cols_ref[:, pl.ds(start, size)], 1.0, 0.3)
        mask = jnp.where(row_ids == col_ids_ref[:, pl.ds(start, size)], 0.0, mask)
        return mask, mask * (count / (count + 8.0))

    rows = pl.ds(0, n_rows)
    for start in range(0, full, LANES):
        mask_ref[rows, pl.ds(start, LANES)], goal_ref[rows, pl.ds(start, LANES)] = mask_and_goal(start, LANES)
    if end:
        def spread(v):
            v = jnp.concatenate([v, jnp.zeros((n_rows, LANES - end), jnp.float32)], axis=1)
            return sum((pltpu.roll(v, k * end, 1) for k in range(1, fold)), v)

        mask_end_ref[rows, :], goal_end_ref[rows, :] = [spread(v) for v in mask_and_goal(full, end)]


def pair_kernel(tiles, fold, n_rows, n_cols, mask_ref, goal_ref, mask_end_ref, goal_end_ref, lhs_ref, lhs_end_ref,
                both_ref, *rest):
    piece_refs = rest[:tiles - 1]
    grad_ref, col_terms, rhs_ref, rhs_end_ref, terms_end_ref, weight_ref, weight_end_ref = rest[tiles - 1:]
    groups, per, _ = both_ref.shape
    structs = groups * per
    piece = n_cols // tiles
    deep = weight_ref.shape[0]
    full = rhs_ref.shape[2]
    end = n_cols - full
    chunks = [(a, min(WIDE, full - a)) for a in range(0, full, WIDE)]

    init_terms(col_terms, 3, per)
    if end:
        rhs_end_ref[...] = jnp.zeros_like(rhs_end_ref)

    def features(g, carry):
        both = both_ref[g]
        parts = [both] + [ref[g] for ref in piece_refs]
        cols = [jnp.concatenate([v[:, c * piece:(c + 1) * piece] for v in parts], axis=1) for c in range(3)]
        put_terms(col_terms, cols, 4)
        for block in range(per // fold):
            for inside in range(fold):
                i = block * fold + inside
                s = g * per + i
                hi, mid, lo = get_terms(col_terms, i)
                right = jnp.concatenate([hi, mid, hi, mid, lo, hi], axis=0)
                rhs_ref[s] = right[:, :full].astype(jnp.bfloat16)
                if end:
                    lane = lax.broadcasted_iota(jnp.int32, (48, LANES), 1)
                    last = jnp.where(lane < end, right[:, full:full + LANES], 0.0)
                    if inside:
                        last = pltpu.roll(last, inside * end, 1)
                    last = last.astype(jnp.bfloat16)
                    b = g * (per // fold) + block
                    rhs_end_ref[b, pl.ds(SLOT * inside, 48), :] = last
                    terms_end_ref[b, pl.ds(16 * inside, 16), :] = last[0:16]
        return carry

    lax.fori_loop(0, groups, features, 0)
    weight_ref[...] = jnp.zeros_like(weight_ref)
    if end:
        weight_end_ref[...] = jnp.zeros_like(weight_end_ref)

    def tanh_block(s, start, size):
        return jnp.tanh(jnp.dot(lhs_ref[s], rhs_ref[s, :, pl.ds(start, size)], preferred_element_type=jnp.float32))

    def tanh_end(b):
        return jnp.tanh(jnp.dot(lhs_end_ref[b], rhs_end_ref[b], preferred_element_type=jnp.float32))

    def add_some(b, carry):
        for inside in range(fold):
            for start, size in chunks:
                weight_ref[:, pl.ds(start, size)] += tanh_block(b * fold + inside, start, size)
        if end:
            weight_end_ref[...] += tanh_end(b)
        return carry

    lax.fori_loop(0, structs // fold, add_some, 0, unroll=UNROLL)

    scale = 0.5 / structs
    for start, size in chunks:
        cut = pl.ds(start, size)
        weight_ref[:, cut] = mask_ref[:, cut] * (0.5 + scale * weight_ref[:, cut]) - goal_ref[:, cut]
    if end:
        part = weight_end_ref[...]
        total = sum((pltpu.roll(part, k * end, 1) for k in range(1, fold)), part)
        weight_end_ref[...] = mask_end_ref[...] * (0.5 + scale * total) - goal_end_ref[...]

    def split2(weight, t):
        g = weight * (1.0 - t * t)
        hi = g.astype(jnp.bfloat16)
        return [hi, (g - hi.astype(jnp.float32)).astype(jnp.bfloat16)]

    def sums(terms, parts):
        hi, lo = [jnp.concatenate(v, axis=1) for v in zip(*parts)]
        return (lax.dot_general(hi, terms, NT, preferred_element_type=jnp.float32).T
                + lax.dot_general(terms, lo, NT, preferred_element_type=jnp.float32))

    def grad_some(b, carry):
        if end:
            last = sums(terms_end_ref[b], [split2(weight_end_ref[...], tanh_end(b))])
        for inside in range(fold):
            s = b * fold + inside
            parts = [split2(weight_ref[:, pl.ds(start, size)], tanh_block(s, start, size)) for start, size in chunks]
            total = sums(rhs_ref[s, pl.ds(0, 16), :], parts)
            if end:
                total += last[16 * inside:16 * inside + 16]
            total = total[:, :n_rows]
            g, i = lax.div(s, per), lax.rem(s, per)
            both = both_ref[g, pl.ds(i, 1), :]
            for c in range(3):
                xyz = both[:, 3 * piece + c * n_rows:3 * piece + (c + 1) * n_rows]
                grad_ref[g, c, pl.ds(i, 1), :] = (0.25 / 16) * (
                    total[c:c + 1] + total[8 + c:9 + c] - total[3:4] * xyz)
        return carry

    lax.fori_loop(0, structs // fold, grad_some, 0, unroll=UNROLL)


def split_ens(n_ens, beads, tiles):
    best = None
    for parts in range(1, n_ens + 1):
        if n_ens % parts or beads % parts or beads % (n_ens // parts):
            continue
        cost = 2 * (beads // parts) + tiles * (beads // (n_ens // parts))
        if best is None or cost < best[0]:
            best = (cost, parts)
    return best[1]


def on_device(coords, counts, segments):
    local_n, _, beads = coords.shape
    n_tile = lax.axis_size("tile")
    n_ens = lax.axis_size("ens")
    structs = local_n * n_ens
    n_p = split_ens(n_ens, beads, n_tile)
    n_q = n_ens // n_p
    n_rows, piece = beads // n_p, beads // n_q
    n_cols = piece * n_tile
    tile, ens = lax.axis_index("tile"), lax.axis_index("ens")
    p, q = lax.rem(ens, n_p), lax.div(ens, n_p)
    vmem = pl.BlockSpec(memory_space=pltpu.VMEM)

    send = pl.pallas_call(
        functools.partial(pack_kernel, n_p, n_q),
        out_shape=jax.ShapeDtypeStruct((n_ens, local_n, 3 * (piece + n_rows)), jnp.float32),
        in_specs=[vmem],
        out_specs=vmem,
        name="pack",
    )(jnp.swapaxes(coords, 0, 1))
    both = lax.all_to_all(send, "ens", 0, 0, tiled=True)

    row_base = tile * beads + p * n_rows
    col_bases = [lax.rem(tile + k, n_tile) * beads + q * piece for k in range(n_tile)]
    own_counts = lax.dynamic_slice_in_dim(counts, p * n_rows, n_rows, 0)
    block = jnp.concatenate([lax.dynamic_slice_in_dim(own_counts, b, piece, 1) for b in col_bases], axis=1)
    seg_cols = jnp.concatenate([lax.dynamic_slice_in_dim(segments, b, piece) for b in col_bases])[None, :]
    col_ids = jnp.concatenate([b + jnp.arange(piece, dtype=jnp.int32) for b in col_bases])[None, :]
    seg_rows = lax.dynamic_slice_in_dim(segments, row_base, n_rows)[:, None]

    full = n_cols // LANES * LANES
    end = n_cols - full
    fold = LANES // end if end and LANES % end == 0 and local_n % (LANES // end) == 0 else 1
    deep = up(n_rows, 16)
    row_wide, col_wide = up(n_rows, LANES), up(n_cols, LANES)
    blocks = structs // fold
    masks = pl.pallas_call(
        functools.partial(mask_kernel, fold),
        out_shape=[jax.ShapeDtypeStruct((deep, width), jnp.float32) for width in (full, full, LANES, LANES)],
        in_specs=[pl.BlockSpec(memory_space=pltpu.SMEM)] + [vmem] * 4,
        out_specs=[vmem] * 4,
        compiler_params=pltpu.CompilerParams(vmem_limit_bytes=32 << 20),
        name="masks",
    )(row_base[None], seg_rows, seg_cols, col_ids, block)
    both, masks = lax.optimization_barrier((both, masks))
    own = both[:, :, :3 * piece]
    pieces = [lax.ppermute(own, "tile", [(t, (t - k) % n_tile) for t in range(n_tile)]) for k in range(1, n_tile)]

    lhs, lhs_end = pl.pallas_call(
        functools.partial(row_kernel, n_rows, fold),
        out_shape=[
            jax.ShapeDtypeStruct((structs, deep, 48), jnp.bfloat16),
            jax.ShapeDtypeStruct((blocks, deep, fold * SLOT), jnp.bfloat16),
        ],
        in_specs=[vmem],
        out_specs=[vmem] * 2,
        scratch_shapes=[[pltpu.VMEM((row_wide // LANES, 8 * local_n, LANES), jnp.float32)] * 3],
        compiler_params=pltpu.CompilerParams(vmem_limit_bytes=32 << 20),
        name="rows",
    )(both)
    grad = pl.pallas_call(
        functools.partial(pair_kernel, n_tile, fold, n_rows, n_cols),
        out_shape=jax.ShapeDtypeStruct((n_ens, 3, local_n, n_rows), jnp.float32),
        in_specs=[vmem] * (6 + n_tile),
        out_specs=vmem,
        scratch_shapes=[
            [pltpu.VMEM((col_wide // LANES, 8 * local_n, LANES), jnp.float32)] * 3,
            pltpu.VMEM((structs, 48, full), jnp.bfloat16),
            pltpu.VMEM((blocks, fold * SLOT, LANES), jnp.bfloat16),
            pltpu.VMEM((blocks, fold * 16, LANES), jnp.bfloat16),
            pltpu.VMEM((deep, full), jnp.float32),
            pltpu.VMEM((deep, LANES), jnp.float32),
        ],
        compiler_params=pltpu.CompilerParams(vmem_limit_bytes=40 << 20),
        name="pairs",
    )(*masks, lhs, lhs_end, both, *pieces)

    back = lax.all_to_all(grad, "ens", 0, 0, tiled=True)
    total = pl.pallas_call(
        functools.partial(sum_kernel, n_p, n_q),
        out_shape=jax.ShapeDtypeStruct((3, local_n, beads), jnp.float32),
        in_specs=[vmem],
        out_specs=vmem,
        name="total",
    )(back)
    return jnp.swapaxes(total, 0, 1)


def solution(mesh):
    return jax.shard_map(
        on_device,
        mesh=mesh,
        in_specs=(P("ens", None, "tile"), P("tile", None), P()),
        out_specs=P("ens", None, "tile"),
        check_vma=False,
    )
```

```python
import functools

import jax
import jax.numpy as jnp
from jax import lax
from jax.experimental import pallas as pl
from jax.experimental.pallas import tpu as pltpu
from jax.sharding import PartitionSpec as P

LANES = 128
WIDE = 256
SLOT = 64
UNROLL = 4
NT = (((1,), (1,)), ((), ()))


def up(n, unit):
    return -(-n // unit) * unit


def split3(v):
    hi = v.astype(jnp.bfloat16).astype(jnp.float32)
    rest = v - hi
    mid = rest.astype(jnp.bfloat16).astype(jnp.float32)
    return hi, mid, rest - mid


def pack_kernel(n_p, n_q, xyz_ref, send_ref):
    beads = xyz_ref.shape[2]
    n_rows, piece = beads // n_p, beads // n_q
    for c in range(3):
        for q in range(n_q):
            for p in range(n_p):
                e = q * n_p + p
                send_ref[e, :, pl.ds(c * piece, piece)] = xyz_ref[c, :, pl.ds(q * piece, piece)]
                send_ref[e, :, pl.ds(3 * piece + c * n_rows, n_rows)] = xyz_ref[c, :, pl.ds(p * n_rows, n_rows)]


def sum_kernel(n_p, n_q, back_ref, total_ref):
    n_rows = back_ref.shape[3]
    for c in range(3):
        for p in range(n_p):
            total = back_ref[p, c]
            for q in range(1, n_q):
                total += back_ref[q * n_p + p, c]
            total_ref[c, :, pl.ds(p * n_rows, n_rows)] = total


def put_terms(refs, xyz, norm_row):
    norm = 1.5 - 0.5 * (xyz[0] * xyz[0] + xyz[1] * xyz[1] + xyz[2] * xyz[2])
    n, size = norm.shape
    wide = refs[0].shape[0] * LANES
    for f, v in ((0, xyz[0]), (1, xyz[1]), (2, xyz[2]), (norm_row, norm)):
        if wide > size:
            v = jnp.concatenate([v, jnp.zeros((n, wide - size), jnp.float32)], axis=1)
        for ref, term in zip(refs, split3(v)):
            for k in range(wide // LANES):
                ref[k, pl.ds(f, n, 8), :] = term[:, k * LANES:(k + 1) * LANES]


def get_terms(refs, i):
    return [jnp.concatenate([ref[k, pl.ds(8 * i, 8), :] for k in range(ref.shape[0])], axis=1) for ref in refs]


def init_terms(refs, one_row, per):
    for ref in refs:
        ref[...] = jnp.zeros_like(ref)
    for k in range(refs[0].shape[0]):
        refs[0][k, pl.ds(one_row, per, 8), :] = jnp.ones((per, LANES), jnp.float32)


def row_kernel(n_rows, fold, both_ref, lhs_ref, lhs_end_ref, row_terms):
    groups, per, width = both_ref.shape
    deep = lhs_ref.shape[1]
    first = width - 3 * n_rows
    init_terms(row_terms, 4, per)

    def features(g, carry):
        both = both_ref[g]
        put_terms(row_terms, [both[:, first + c * n_rows:first + (c + 1) * n_rows] for c in range(3)], 3)
        for block in range(per // fold):
            lefts = []
            for inside in range(fold):
                i = block * fold + inside
                hi, mid, lo = get_terms(row_terms, i)
                left = jnp.concatenate([hi, hi, mid, mid, hi, lo], axis=0)
                lhs_ref[g * per + i] = left.T[:deep].astype(jnp.bfloat16)
                lefts += [left, jnp.zeros((SLOT - 48, left.shape[1]), jnp.float32)]
            lhs_end_ref[g * (per // fold) + block] = jnp.concatenate(lefts, axis=0).T[:deep].astype(jnp.bfloat16)
        return carry

    lax.fori_loop(0, groups, features, 0)


def mask_kernel(fold, base_ref, seg_rows_ref, seg_cols_ref, col_ids_ref, counts_ref, mask_ref, goal_ref, mask_end_ref,
                goal_end_ref):
    n_rows, n_cols = counts_ref.shape
    deep, full = mask_ref.shape
    end = n_cols - full
    for ref in (mask_ref, goal_ref, mask_end_ref, goal_end_ref):
        if deep > n_rows:
            ref[pl.ds(n_rows, deep - n_rows), :] = jnp.zeros((deep - n_rows, ref.shape[1]), jnp.float32)

    def mask_and_goal(start, size):
        count = counts_ref[:, pl.ds(start, size)].astype(jnp.float32)
        row_ids = base_ref[0] + lax.broadcasted_iota(jnp.int32, (n_rows, size), 0)
        mask = jnp.where(seg_rows_ref[...] == seg_cols_ref[:, pl.ds(start, size)], 1.0, 0.3)
        mask = jnp.where(row_ids == col_ids_ref[:, pl.ds(start, size)], 0.0, mask)
        return mask, mask * (count / (count + 8.0))

    rows = pl.ds(0, n_rows)
    for start in range(0, full, LANES):
        mask_ref[rows, pl.ds(start, LANES)], goal_ref[rows, pl.ds(start, LANES)] = mask_and_goal(start, LANES)
    if end:
        def spread(v):
            v = jnp.concatenate([v, jnp.zeros((n_rows, LANES - end), jnp.float32)], axis=1)
            return sum((pltpu.roll(v, k * end, 1) for k in range(1, fold)), v)

        mask_end_ref[rows, :], goal_end_ref[rows, :] = [spread(v) for v in mask_and_goal(full, end)]


def pair_kernel(tiles, fold, n_rows, n_cols, mask_ref, goal_ref, mask_end_ref, goal_end_ref, lhs_ref, lhs_end_ref,
                both_ref, *rest):
    piece_refs = rest[:tiles - 1]
    grad_ref, col_terms, rhs_ref, rhs_end_ref, terms_end_ref, weight_ref, weight_end_ref = rest[tiles - 1:]
    groups, per, _ = both_ref.shape
    structs = groups * per
    piece = n_cols // tiles
    deep = weight_ref.shape[0]
    full = rhs_ref.shape[2]
    end = n_cols - full
    chunks = [(a, min(WIDE, full - a)) for a in range(0, full, WIDE)]

    init_terms(col_terms, 3, per)
    if end:
        rhs_end_ref[...] = jnp.zeros_like(rhs_end_ref)

    def features(g):
        both = both_ref[g]
        parts = [both] + [ref[g] for ref in piece_refs]
        cols = [jnp.concatenate([v[:, c * piece:(c + 1) * piece] for v in parts], axis=1) for c in range(3)]
        put_terms(col_terms, cols, 4)
        for block in range(per // fold):
            for inside in range(fold):
                i = block * fold + inside
                s = g * per + i
                hi, mid, lo = get_terms(col_terms, i)
                right = jnp.concatenate([hi, mid, hi, mid, lo, hi], axis=0)
                rhs_ref[s] = right[:, :full].astype(jnp.bfloat16)
                if end:
                    lane = lax.broadcasted_iota(jnp.int32, (48, LANES), 1)
                    last = jnp.where(lane < end, right[:, full:full + LANES], 0.0)
                    if inside:
                        last = pltpu.roll(last, inside * end, 1)
                    last = last.astype(jnp.bfloat16)
                    b = g * (per // fold) + block
                    rhs_end_ref[b, pl.ds(SLOT * inside, 48), :] = last
                    terms_end_ref[b, pl.ds(16 * inside, 16), :] = last[0:16]

    weight_ref[...] = jnp.zeros_like(weight_ref)
    if end:
        weight_end_ref[...] = jnp.zeros_like(weight_end_ref)

    def tanh_block(s, start, size):
        return jnp.tanh(jnp.dot(lhs_ref[s], rhs_ref[s, :, pl.ds(start, size)], preferred_element_type=jnp.float32))

    def tanh_end(b):
        return jnp.tanh(jnp.dot(lhs_end_ref[b], rhs_end_ref[b], preferred_element_type=jnp.float32))

    def add_some(b):
        for inside in range(fold):
            for start, size in chunks:
                weight_ref[:, pl.ds(start, size)] += tanh_block(b * fold + inside, start, size)
        if end:
            weight_end_ref[...] += tanh_end(b)

    together = 2 if groups % 2 == 0 else 1

    def add_groups(step, carry):
        for j in range(together):
            features(step * together + j)
        for j in range(together * (per // fold)):
            add_some(step * (together * (per // fold)) + j)
        return carry

    lax.fori_loop(0, groups // together, add_groups, 0)

    scale = 0.5 / structs
    for start, size in chunks:
        cut = pl.ds(start, size)
        weight_ref[:, cut] = mask_ref[:, cut] * (0.5 + scale * weight_ref[:, cut]) - goal_ref[:, cut]
    if end:
        part = weight_end_ref[...]
        total = sum((pltpu.roll(part, k * end, 1) for k in range(1, fold)), part)
        weight_end_ref[...] = mask_end_ref[...] * (0.5 + scale * total) - goal_end_ref[...]

    def split2(weight, t):
        g = weight * (1.0 - t * t)
        hi = g.astype(jnp.bfloat16)
        return [hi, (g - hi.astype(jnp.float32)).astype(jnp.bfloat16)]

    def sums(terms, parts):
        hi, lo = [jnp.concatenate(v, axis=1) for v in zip(*parts)]
        return (lax.dot_general(hi, terms, NT, preferred_element_type=jnp.float32).T
                + lax.dot_general(terms, lo, NT, preferred_element_type=jnp.float32))

    def grad_some(b, carry):
        if end:
            last = sums(terms_end_ref[b], [split2(weight_end_ref[...], tanh_end(b))])
        for inside in range(fold):
            s = b * fold + inside
            parts = [split2(weight_ref[:, pl.ds(start, size)], tanh_block(s, start, size)) for start, size in chunks]
            total = sums(rhs_ref[s, pl.ds(0, 16), :], parts)
            if end:
                total += last[16 * inside:16 * inside + 16]
            total = total[:, :n_rows]
            g, i = lax.div(s, per), lax.rem(s, per)
            both = both_ref[g, pl.ds(i, 1), :]
            for c in range(3):
                xyz = both[:, 3 * piece + c * n_rows:3 * piece + (c + 1) * n_rows]
                grad_ref[g, c, pl.ds(i, 1), :] = (0.25 / 16) * (
                    total[c:c + 1] + total[8 + c:9 + c] - total[3:4] * xyz)
        return carry

    lax.fori_loop(0, structs // fold, grad_some, 0, unroll=UNROLL)


def split_ens(n_ens, beads, tiles):
    best = None
    for parts in range(1, n_ens + 1):
        if n_ens % parts or beads % parts or beads % (n_ens // parts):
            continue
        cost = 2 * (beads // parts) + tiles * (beads // (n_ens // parts))
        if best is None or cost < best[0]:
            best = (cost, parts)
    return best[1]


def on_device(coords, counts, segments):
    local_n, _, beads = coords.shape
    n_tile = lax.axis_size("tile")
    n_ens = lax.axis_size("ens")
    structs = local_n * n_ens
    n_p = split_ens(n_ens, beads, n_tile)
    n_q = n_ens // n_p
    n_rows, piece = beads // n_p, beads // n_q
    n_cols = piece * n_tile
    tile, ens = lax.axis_index("tile"), lax.axis_index("ens")
    p, q = lax.rem(ens, n_p), lax.div(ens, n_p)
    vmem = pl.BlockSpec(memory_space=pltpu.VMEM)

    send = pl.pallas_call(
        functools.partial(pack_kernel, n_p, n_q),
        out_shape=jax.ShapeDtypeStruct((n_ens, local_n, 3 * (piece + n_rows)), jnp.float32),
        in_specs=[vmem],
        out_specs=vmem,
        name="pack",
    )(jnp.swapaxes(coords, 0, 1))
    both = lax.all_to_all(send, "ens", 0, 0, tiled=True)

    row_base = tile * beads + p * n_rows
    col_bases = [lax.rem(tile + k, n_tile) * beads + q * piece for k in range(n_tile)]
    own_counts = lax.dynamic_slice_in_dim(counts, p * n_rows, n_rows, 0)
    block = jnp.concatenate([lax.dynamic_slice_in_dim(own_counts, b, piece, 1) for b in col_bases], axis=1)
    seg_cols = jnp.concatenate([lax.dynamic_slice_in_dim(segments, b, piece) for b in col_bases])[None, :]
    col_ids = jnp.concatenate([b + jnp.arange(piece, dtype=jnp.int32) for b in col_bases])[None, :]
    seg_rows = lax.dynamic_slice_in_dim(segments, row_base, n_rows)[:, None]

    full = n_cols // LANES * LANES
    end = n_cols - full
    fold = LANES // end if end and LANES % end == 0 and local_n % (LANES // end) == 0 else 1
    deep = up(n_rows, 16)
    row_wide, col_wide = up(n_rows, LANES), up(n_cols, LANES)
    blocks = structs // fold
    masks = pl.pallas_call(
        functools.partial(mask_kernel, fold),
        out_shape=[jax.ShapeDtypeStruct((deep, width), jnp.float32) for width in (full, full, LANES, LANES)],
        in_specs=[pl.BlockSpec(memory_space=pltpu.SMEM)] + [vmem] * 4,
        out_specs=[vmem] * 4,
        compiler_params=pltpu.CompilerParams(vmem_limit_bytes=32 << 20),
        name="masks",
    )(row_base[None], seg_rows, seg_cols, col_ids, block)
    both, masks = lax.optimization_barrier((both, masks))
    own = both[:, :, :3 * piece]
    pieces = [lax.ppermute(own, "tile", [(t, (t - k) % n_tile) for t in range(n_tile)]) for k in range(1, n_tile)]

    lhs, lhs_end = pl.pallas_call(
        functools.partial(row_kernel, n_rows, fold),
        out_shape=[
            jax.ShapeDtypeStruct((structs, deep, 48), jnp.bfloat16),
            jax.ShapeDtypeStruct((blocks, deep, fold * SLOT), jnp.bfloat16),
        ],
        in_specs=[vmem],
        out_specs=[vmem] * 2,
        scratch_shapes=[[pltpu.VMEM((row_wide // LANES, 8 * local_n, LANES), jnp.float32)] * 3],
        compiler_params=pltpu.CompilerParams(vmem_limit_bytes=32 << 20),
        name="rows",
    )(both)
    grad = pl.pallas_call(
        functools.partial(pair_kernel, n_tile, fold, n_rows, n_cols),
        out_shape=jax.ShapeDtypeStruct((n_ens, 3, local_n, n_rows), jnp.float32),
        in_specs=[vmem] * (6 + n_tile),
        out_specs=vmem,
        scratch_shapes=[
            [pltpu.VMEM((col_wide // LANES, 8 * local_n, LANES), jnp.float32)] * 3,
            pltpu.VMEM((structs, 48, full), jnp.bfloat16),
            pltpu.VMEM((blocks, fold * SLOT, LANES), jnp.bfloat16),
            pltpu.VMEM((blocks, fold * 16, LANES), jnp.bfloat16),
            pltpu.VMEM((deep, full), jnp.float32),
            pltpu.VMEM((deep, LANES), jnp.float32),
        ],
        compiler_params=pltpu.CompilerParams(vmem_limit_bytes=40 << 20),
        name="pairs",
    )(*masks, lhs, lhs_end, both, *pieces)

    back = lax.all_to_all(grad, "ens", 0, 0, tiled=True)
    total = pl.pallas_call(
        functools.partial(sum_kernel, n_p, n_q),
        out_shape=jax.ShapeDtypeStruct((3, local_n, beads), jnp.float32),
        in_specs=[vmem],
        out_specs=vmem,
        name="total",
    )(back)
    return jnp.swapaxes(total, 0, 1)


def solution(mesh):
    return jax.shard_map(
        on_device,
        mesh=mesh,
        in_specs=(P("ens", None, "tile"), P("tile", None), P()),
        out_specs=P("ens", None, "tile"),
        check_vma=False,
    )
```

```python
import functools

import jax
import jax.numpy as jnp
from jax import lax
from jax.experimental import pallas as pl
from jax.experimental.pallas import tpu as pltpu
from jax.sharding import PartitionSpec as P

LANES = 128
WIDE = 1024
SLOT = 64
UNROLL = 4
NT = (((1,), (1,)), ((), ()))


def up(n, unit):
    return -(-n // unit) * unit


def split3(v):
    hi = v.astype(jnp.bfloat16).astype(jnp.float32)
    rest = v - hi
    mid = rest.astype(jnp.bfloat16).astype(jnp.float32)
    return hi, mid, rest - mid


def pack_kernel(n_p, n_q, xyz_ref, send_ref):
    beads = xyz_ref.shape[2]
    n_rows, piece = beads // n_p, beads // n_q
    for c in range(3):
        for q in range(n_q):
            for p in range(n_p):
                e = q * n_p + p
                send_ref[e, :, pl.ds(c * piece, piece)] = xyz_ref[c, :, pl.ds(q * piece, piece)]
                send_ref[e, :, pl.ds(3 * piece + c * n_rows, n_rows)] = xyz_ref[c, :, pl.ds(p * n_rows, n_rows)]


def sum_kernel(n_p, n_q, back_ref, total_ref):
    n_rows = back_ref.shape[3]
    for c in range(3):
        for p in range(n_p):
            total = back_ref[p, c]
            for q in range(1, n_q):
                total += back_ref[q * n_p + p, c]
            total_ref[c, :, pl.ds(p * n_rows, n_rows)] = total


def put_terms(refs, xyz, norm_row):
    norm = 1.5 - 0.5 * (xyz[0] * xyz[0] + xyz[1] * xyz[1] + xyz[2] * xyz[2])
    n, size = norm.shape
    wide = refs[0].shape[0] * LANES
    for f, v in ((0, xyz[0]), (1, xyz[1]), (2, xyz[2]), (norm_row, norm)):
        if wide > size:
            v = jnp.concatenate([v, jnp.zeros((n, wide - size), jnp.float32)], axis=1)
        for ref, term in zip(refs, split3(v)):
            for k in range(wide // LANES):
                ref[k, pl.ds(f, n, 8), :] = term[:, k * LANES:(k + 1) * LANES]


def get_terms(refs, i):
    return [jnp.concatenate([ref[k, pl.ds(8 * i, 8), :] for k in range(ref.shape[0])], axis=1) for ref in refs]


def init_terms(refs, one_row, per):
    for ref in refs:
        ref[...] = jnp.zeros_like(ref)
    for k in range(refs[0].shape[0]):
        refs[0][k, pl.ds(one_row, per, 8), :] = jnp.ones((per, LANES), jnp.float32)


def row_kernel(n_rows, fold, both_ref, lhs_ref, lhs_end_ref, row_terms):
    groups, per, width = both_ref.shape
    deep = lhs_ref.shape[1]
    first = width - 3 * n_rows
    init_terms(row_terms, 4, per)

    def features(g, carry):
        both = both_ref[g]
        put_terms(row_terms, [both[:, first + c * n_rows:first + (c + 1) * n_rows] for c in range(3)], 3)
        for block in range(per // fold):
            lefts = []
            for inside in range(fold):
                i = block * fold + inside
                hi, mid, lo = get_terms(row_terms, i)
                left = jnp.concatenate([hi, hi, mid, mid, hi, lo], axis=0)
                lhs_ref[g * per + i] = left.T[:deep].astype(jnp.bfloat16)
                lefts += [left, jnp.zeros((SLOT - 48, left.shape[1]), jnp.float32)]
            lhs_end_ref[g * (per // fold) + block] = jnp.concatenate(lefts, axis=0).T[:deep].astype(jnp.bfloat16)
        return carry

    lax.fori_loop(0, groups, features, 0)


def mask_kernel(fold, base_ref, seg_rows_ref, seg_cols_ref, col_ids_ref, counts_ref, mask_ref, goal_ref, mask_end_ref,
                goal_end_ref):
    n_rows, n_cols = counts_ref.shape
    deep, full = mask_ref.shape
    end = n_cols - full
    for ref in (mask_ref, goal_ref, mask_end_ref, goal_end_ref):
        if deep > n_rows:
            ref[pl.ds(n_rows, deep - n_rows), :] = jnp.zeros((deep - n_rows, ref.shape[1]), jnp.float32)

    def mask_and_goal(start, size):
        count = counts_ref[:, pl.ds(start, size)].astype(jnp.float32)
        row_ids = base_ref[0] + lax.broadcasted_iota(jnp.int32, (n_rows, size), 0)
        mask = jnp.where(seg_rows_ref[...] == seg_cols_ref[:, pl.ds(start, size)], 1.0, 0.3)
        mask = jnp.where(row_ids == col_ids_ref[:, pl.ds(start, size)], 0.0, mask)
        return mask, mask * (count / (count + 8.0))

    rows = pl.ds(0, n_rows)
    for start in range(0, full, LANES):
        mask_ref[rows, pl.ds(start, LANES)], goal_ref[rows, pl.ds(start, LANES)] = mask_and_goal(start, LANES)
    if end:
        def spread(v):
            v = jnp.concatenate([v, jnp.zeros((n_rows, LANES - end), jnp.float32)], axis=1)
            return sum((pltpu.roll(v, k * end, 1) for k in range(1, fold)), v)

        mask_end_ref[rows, :], goal_end_ref[rows, :] = [spread(v) for v in mask_and_goal(full, end)]


def pair_kernel(tiles, fold, n_rows, n_cols, mask_ref, goal_ref, mask_end_ref, goal_end_ref, lhs_ref, lhs_end_ref,
                both_ref, *rest):
    piece_refs = rest[:tiles - 1]
    grad_ref, col_terms, rhs_ref, rhs_end_ref, terms_end_ref, weight_ref, weight_end_ref = rest[tiles - 1:]
    groups, per, _ = both_ref.shape
    structs = groups * per
    piece = n_cols // tiles
    deep = weight_ref.shape[0]
    full = rhs_ref.shape[2]
    end = n_cols - full
    chunks = [(a, min(WIDE, full - a)) for a in range(0, full, WIDE)]

    init_terms(col_terms, 3, per)
    if end:
        rhs_end_ref[...] = jnp.zeros_like(rhs_end_ref)

    def features(g):
        both = both_ref[g]
        parts = [both] + [ref[g] for ref in piece_refs]
        cols = [jnp.concatenate([v[:, c * piece:(c + 1) * piece] for v in parts], axis=1) for c in range(3)]
        put_terms(col_terms, cols, 4)
        for block in range(per // fold):
            for inside in range(fold):
                i = block * fold + inside
                s = g * per + i
                hi, mid, lo = get_terms(col_terms, i)
                right = jnp.concatenate([hi, mid, hi, mid, lo, hi], axis=0)
                rhs_ref[s] = right[:, :full].astype(jnp.bfloat16)
                if end:
                    lane = lax.broadcasted_iota(jnp.int32, (48, LANES), 1)
                    last = jnp.where(lane < end, right[:, full:full + LANES], 0.0)
                    if inside:
                        last = pltpu.roll(last, inside * end, 1)
                    last = last.astype(jnp.bfloat16)
                    b = g * (per // fold) + block
                    rhs_end_ref[b, pl.ds(SLOT * inside, 48), :] = last
                    terms_end_ref[b, pl.ds(16 * inside, 16), :] = last[0:16]

    weight_ref[...] = jnp.zeros_like(weight_ref)
    if end:
        weight_end_ref[...] = jnp.zeros_like(weight_end_ref)

    def tanh_block(s, start, size):
        return jnp.tanh(jnp.dot(lhs_ref[s], rhs_ref[s, :, pl.ds(start, size)], preferred_element_type=jnp.float32))

    def tanh_end(b):
        return jnp.tanh(jnp.dot(lhs_end_ref[b], rhs_end_ref[b], preferred_element_type=jnp.float32))

    def add_some(b):
        for inside in range(fold):
            for start, size in chunks:
                weight_ref[:, pl.ds(start, size)] += tanh_block(b * fold + inside, start, size)
        if end:
            weight_end_ref[...] += tanh_end(b)

    together = 2 if groups % 2 == 0 else 1

    def add_groups(step, carry):
        for j in range(together):
            features(step * together + j)
        for j in range(together * (per // fold)):
            add_some(step * (together * (per // fold)) + j)
        return carry

    lax.fori_loop(0, groups // together, add_groups, 0)

    scale = 0.5 / structs
    for start, size in chunks:
        cut = pl.ds(start, size)
        weight_ref[:, cut] = mask_ref[:, cut] * (0.5 + scale * weight_ref[:, cut]) - goal_ref[:, cut]
    if end:
        part = weight_end_ref[...]
        total = sum((pltpu.roll(part, k * end, 1) for k in range(1, fold)), part)
        weight_end_ref[...] = mask_end_ref[...] * (0.5 + scale * total) - goal_end_ref[...]

    def split2(weight, t):
        g = weight * (1.0 - t * t)
        hi = g.astype(jnp.bfloat16)
        return [hi, (g - hi.astype(jnp.float32)).astype(jnp.bfloat16)]

    def sums(terms, parts):
        hi, lo = [jnp.concatenate(v, axis=1) for v in zip(*parts)]
        return (lax.dot_general(hi, terms, NT, preferred_element_type=jnp.float32).T
                + lax.dot_general(terms, lo, NT, preferred_element_type=jnp.float32))

    def grad_some(b, carry):
        if end:
            last = sums(terms_end_ref[b], [split2(weight_end_ref[...], tanh_end(b))])
        for inside in range(fold):
            s = b * fold + inside
            parts = [split2(weight_ref[:, pl.ds(start, size)], tanh_block(s, start, size)) for start, size in chunks]
            total = sums(rhs_ref[s, pl.ds(0, 16), :], parts)
            if end:
                total += last[16 * inside:16 * inside + 16]
            total = total[:, :n_rows]
            g, i = lax.div(s, per), lax.rem(s, per)
            both = both_ref[g, pl.ds(i, 1), :]
            for c in range(3):
                xyz = both[:, 3 * piece + c * n_rows:3 * piece + (c + 1) * n_rows]
                grad_ref[g, c, pl.ds(i, 1), :] = (0.25 / 16) * (
                    total[c:c + 1] + total[8 + c:9 + c] - total[3:4] * xyz)
        return carry

    lax.fori_loop(0, structs // fold, grad_some, 0, unroll=UNROLL)


def split_ens(n_ens, beads, tiles):
    best = None
    for parts in range(1, n_ens + 1):
        if n_ens % parts or beads % parts or beads % (n_ens // parts):
            continue
        cost = 2 * (beads // parts) + tiles * (beads // (n_ens // parts))
        if best is None or cost < best[0]:
            best = (cost, parts)
    return best[1]


def on_device(coords, counts, segments):
    local_n, _, beads = coords.shape
    n_tile = lax.axis_size("tile")
    n_ens = lax.axis_size("ens")
    structs = local_n * n_ens
    n_p = split_ens(n_ens, beads, n_tile)
    n_q = n_ens // n_p
    n_rows, piece = beads // n_p, beads // n_q
    n_cols = piece * n_tile
    tile, ens = lax.axis_index("tile"), lax.axis_index("ens")
    p, q = lax.rem(ens, n_p), lax.div(ens, n_p)
    vmem = pl.BlockSpec(memory_space=pltpu.VMEM)

    send = pl.pallas_call(
        functools.partial(pack_kernel, n_p, n_q),
        out_shape=jax.ShapeDtypeStruct((n_ens, local_n, 3 * (piece + n_rows)), jnp.float32),
        in_specs=[vmem],
        out_specs=vmem,
        name="pack",
    )(jnp.swapaxes(coords, 0, 1))
    both = lax.all_to_all(send, "ens", 0, 0, tiled=True)

    row_base = tile * beads + p * n_rows
    col_bases = [lax.rem(tile + k, n_tile) * beads + q * piece for k in range(n_tile)]
    own_counts = lax.dynamic_slice_in_dim(counts, p * n_rows, n_rows, 0)
    block = jnp.concatenate([lax.dynamic_slice_in_dim(own_counts, b, piece, 1) for b in col_bases], axis=1)
    seg_cols = jnp.concatenate([lax.dynamic_slice_in_dim(segments, b, piece) for b in col_bases])[None, :]
    col_ids = jnp.concatenate([b + jnp.arange(piece, dtype=jnp.int32) for b in col_bases])[None, :]
    seg_rows = lax.dynamic_slice_in_dim(segments, row_base, n_rows)[:, None]

    full = n_cols // LANES * LANES
    end = n_cols - full
    fold = LANES // end if end and LANES % end == 0 and local_n % (LANES // end) == 0 else 1
    deep = up(n_rows, 16)
    row_wide, col_wide = up(n_rows, LANES), up(n_cols, LANES)
    blocks = structs // fold
    masks = pl.pallas_call(
        functools.partial(mask_kernel, fold),
        out_shape=[jax.ShapeDtypeStruct((deep, width), jnp.float32) for width in (full, full, LANES, LANES)],
        in_specs=[pl.BlockSpec(memory_space=pltpu.SMEM)] + [vmem] * 4,
        out_specs=[vmem] * 4,
        compiler_params=pltpu.CompilerParams(vmem_limit_bytes=32 << 20),
        name="masks",
    )(row_base[None], seg_rows, seg_cols, col_ids, block)
    both, masks = lax.optimization_barrier((both, masks))
    own = both[:, :, :3 * piece]
    pieces = [lax.ppermute(own, "tile", [(t, (t - k) % n_tile) for t in range(n_tile)]) for k in range(1, n_tile)]

    lhs, lhs_end = pl.pallas_call(
        functools.partial(row_kernel, n_rows, fold),
        out_shape=[
            jax.ShapeDtypeStruct((structs, deep, 48), jnp.bfloat16),
            jax.ShapeDtypeStruct((blocks, deep, fold * SLOT), jnp.bfloat16),
        ],
        in_specs=[vmem],
        out_specs=[vmem] * 2,
        scratch_shapes=[[pltpu.VMEM((row_wide // LANES, 8 * local_n, LANES), jnp.float32)] * 3],
        compiler_params=pltpu.CompilerParams(vmem_limit_bytes=32 << 20),
        name="rows",
    )(both)
    grad = pl.pallas_call(
        functools.partial(pair_kernel, n_tile, fold, n_rows, n_cols),
        out_shape=jax.ShapeDtypeStruct((n_ens, 3, local_n, n_rows), jnp.float32),
        in_specs=[vmem] * (6 + n_tile),
        out_specs=vmem,
        scratch_shapes=[
            [pltpu.VMEM((col_wide // LANES, 8 * local_n, LANES), jnp.float32)] * 3,
            pltpu.VMEM((structs, 48, full), jnp.bfloat16),
            pltpu.VMEM((blocks, fold * SLOT, LANES), jnp.bfloat16),
            pltpu.VMEM((blocks, fold * 16, LANES), jnp.bfloat16),
            pltpu.VMEM((deep, full), jnp.float32),
            pltpu.VMEM((deep, LANES), jnp.float32),
        ],
        compiler_params=pltpu.CompilerParams(vmem_limit_bytes=40 << 20),
        name="pairs",
    )(*masks, lhs, lhs_end, both, *pieces)

    back = lax.all_to_all(grad, "ens", 0, 0, tiled=True)
    total = pl.pallas_call(
        functools.partial(sum_kernel, n_p, n_q),
        out_shape=jax.ShapeDtypeStruct((3, local_n, beads), jnp.float32),
        in_specs=[vmem],
        out_specs=vmem,
        name="total",
    )(back)
    return jnp.swapaxes(total, 0, 1)


def solution(mesh):
    return jax.shard_map(
        on_device,
        mesh=mesh,
        in_specs=(P("ens", None, "tile"), P("tile", None), P()),
        out_specs=P("ens", None, "tile"),
        check_vma=False,
    )
```

```python
import functools

import jax
import jax.numpy as jnp
from jax import lax
from jax.experimental import pallas as pl
from jax.experimental.pallas import tpu as pltpu
from jax.sharding import PartitionSpec as P

LANES = 128
WIDE = 256
SLOT = 64
UNROLL = 4
NT = (((1,), (1,)), ((), ()))


def up(n, unit):
    return -(-n // unit) * unit


def split3(v):
    hi = v.astype(jnp.bfloat16).astype(jnp.float32)
    rest = v - hi
    mid = rest.astype(jnp.bfloat16).astype(jnp.float32)
    return hi, mid, rest - mid


def pack_kernel(n_p, n_q, xyz_ref, send_ref):
    beads = xyz_ref.shape[2]
    n_rows, piece = beads // n_p, beads // n_q
    for c in range(3):
        for q in range(n_q):
            for p in range(n_p):
                e = q * n_p + p
                send_ref[e, :, pl.ds(c * piece, piece)] = xyz_ref[c, :, pl.ds(q * piece, piece)]
                send_ref[e, :, pl.ds(3 * piece + c * n_rows, n_rows)] = xyz_ref[c, :, pl.ds(p * n_rows, n_rows)]


def sum_kernel(n_p, n_q, back_ref, total_ref):
    n_rows = back_ref.shape[3]
    for c in range(3):
        for p in range(n_p):
            total = back_ref[p, c]
            for q in range(1, n_q):
                total += back_ref[q * n_p + p, c]
            total_ref[c, :, pl.ds(p * n_rows, n_rows)] = total


def put_terms(refs, xyz, norm_row):
    norm = 1.5 - 0.5 * (xyz[0] * xyz[0] + xyz[1] * xyz[1] + xyz[2] * xyz[2])
    n, size = norm.shape
    wide = refs[0].shape[0] * LANES
    for f, v in ((0, xyz[0]), (1, xyz[1]), (2, xyz[2]), (norm_row, norm)):
        if wide > size:
            v = jnp.concatenate([v, jnp.zeros((n, wide - size), jnp.float32)], axis=1)
        for ref, term in zip(refs, split3(v)):
            for k in range(wide // LANES):
                ref[k, pl.ds(f, n, 8), :] = term[:, k * LANES:(k + 1) * LANES]


def get_terms(refs, i):
    return [jnp.concatenate([ref[k, pl.ds(8 * i, 8), :] for k in range(ref.shape[0])], axis=1) for ref in refs]


def init_terms(refs, one_row, per):
    for ref in refs:
        ref[...] = jnp.zeros_like(ref)
    for k in range(refs[0].shape[0]):
        refs[0][k, pl.ds(one_row, per, 8), :] = jnp.ones((per, LANES), jnp.float32)


def row_kernel(n_rows, fold, both_ref, lhs_ref, lhs_end_ref, row_terms):
    groups, per, width = both_ref.shape
    deep = lhs_ref.shape[1]
    first = width - 3 * n_rows
    init_terms(row_terms, 4, per)

    def features(g, carry):
        both = both_ref[g]
        put_terms(row_terms, [both[:, first + c * n_rows:first + (c + 1) * n_rows] for c in range(3)], 3)
        for block in range(per // fold):
            lefts = []
            for inside in range(fold):
                i = block * fold + inside
                hi, mid, lo = get_terms(row_terms, i)
                left = jnp.concatenate([hi, hi, mid, mid, hi, lo], axis=0)
                lhs_ref[g * per + i] = left.T[:deep].astype(jnp.bfloat16)
                lefts += [left, jnp.zeros((SLOT - 48, left.shape[1]), jnp.float32)]
            lhs_end_ref[g * (per // fold) + block] = jnp.concatenate(lefts, axis=0).T[:deep].astype(jnp.bfloat16)
        return carry

    lax.fori_loop(0, groups, features, 0)


def mask_kernel(fold, base_ref, seg_rows_ref, seg_cols_ref, col_ids_ref, counts_ref, mask_ref, goal_ref):
    n_rows, n_cols = counts_ref.shape
    deep = mask_ref.shape[0]
    full = n_cols // LANES * LANES
    end = n_cols - full
    rows = pl.ds(0, n_rows)
    if deep > n_rows:
        for ref in (mask_ref, goal_ref):
            ref[pl.ds(n_rows, deep - n_rows), :] = jnp.zeros((deep - n_rows, ref.shape[1]), jnp.float32)

    def mask_and_goal(start, size):
        count = counts_ref[:, pl.ds(start, size)].astype(jnp.float32)
        row_ids = base_ref[0] + lax.broadcasted_iota(jnp.int32, (n_rows, size), 0)
        mask = jnp.where(seg_rows_ref[...] == seg_cols_ref[:, pl.ds(start, size)], 1.0, 0.3)
        mask = jnp.where(row_ids == col_ids_ref[:, pl.ds(start, size)], 0.0, mask)
        return mask, mask * (count / (count + 8.0))

    for start in range(0, full, LANES):
        mask_ref[rows, pl.ds(start, LANES)], goal_ref[rows, pl.ds(start, LANES)] = mask_and_goal(start, LANES)
    if end:
        def spread(v):
            v = jnp.concatenate([v, jnp.zeros((n_rows, LANES - end), jnp.float32)], axis=1)
            return sum((pltpu.roll(v, k * end, 1) for k in range(1, fold)), v)

        last = pl.ds(full, LANES)
        mask_ref[rows, last], goal_ref[rows, last] = [spread(v) for v in mask_and_goal(full, end)]


def pair_kernel(tiles, fold, n_rows, n_cols, mask_ref, goal_ref, lhs_ref, lhs_end_ref, both_ref, *rest):
    piece_refs = rest[:tiles - 1]
    grad_ref, col_terms, rhs_ref, rhs_end_ref, terms_end_ref, weight_ref, weight_end_ref = rest[tiles - 1:]
    groups, per, _ = both_ref.shape
    structs = groups * per
    piece = n_cols // tiles
    deep = weight_ref.shape[0]
    full = rhs_ref.shape[2]
    end = n_cols - full
    chunks = [(a, min(WIDE, full - a)) for a in range(0, full, WIDE)]

    init_terms(col_terms, 3, per)
    if end:
        rhs_end_ref[...] = jnp.zeros_like(rhs_end_ref)

    def features(g):
        both = both_ref[g]
        parts = [both] + [ref[g] for ref in piece_refs]
        cols = [jnp.concatenate([v[:, c * piece:(c + 1) * piece] for v in parts], axis=1) for c in range(3)]
        put_terms(col_terms, cols, 4)
        for block in range(per // fold):
            for inside in range(fold):
                i = block * fold + inside
                s = g * per + i
                hi, mid, lo = get_terms(col_terms, i)
                right = jnp.concatenate([hi, mid, hi, mid, lo, hi], axis=0)
                rhs_ref[s] = right[:, :full].astype(jnp.bfloat16)
                if end:
                    lane = lax.broadcasted_iota(jnp.int32, (48, LANES), 1)
                    last = jnp.where(lane < end, right[:, full:full + LANES], 0.0)
                    if inside:
                        last = pltpu.roll(last, inside * end, 1)
                    last = last.astype(jnp.bfloat16)
                    b = g * (per // fold) + block
                    rhs_end_ref[b, pl.ds(SLOT * inside, 48), :] = last
                    terms_end_ref[b, pl.ds(16 * inside, 16), :] = last[0:16]

    weight_ref[...] = jnp.zeros_like(weight_ref)
    if end:
        weight_end_ref[...] = jnp.zeros_like(weight_end_ref)

    def tanh_block(s, start, size):
        return jnp.tanh(jnp.dot(lhs_ref[s], rhs_ref[s, :, pl.ds(start, size)], preferred_element_type=jnp.float32))

    def tanh_end(b):
        return jnp.tanh(jnp.dot(lhs_end_ref[b], rhs_end_ref[b], preferred_element_type=jnp.float32))

    def add_some(b):
        for inside in range(0, fold, 2):
            for start, size in chunks:
                t = [tanh_block(b * fold + i, start, size) for i in range(inside, min(inside + 2, fold))]
                weight_ref[:, pl.ds(start, size)] += functools.reduce(jnp.add, t)
        if end:
            weight_end_ref[...] += tanh_end(b)

    together = 2 if groups % 2 == 0 else 1

    def add_groups(step, carry):
        for j in range(together):
            features(step * together + j)
        for j in range(together * (per // fold)):
            add_some(step * (together * (per // fold)) + j)
        return carry

    lax.fori_loop(0, groups // together, add_groups, 0)

    scale = 0.5 / structs
    for start, size in chunks:
        cut = pl.ds(start, size)
        weight_ref[:, cut] = mask_ref[:, cut] * (0.5 + scale * weight_ref[:, cut]) - goal_ref[:, cut]
    if end:
        part = weight_end_ref[...]
        total = sum((pltpu.roll(part, k * end, 1) for k in range(1, fold)), part)
        last = pl.ds(full, LANES)
        weight_end_ref[...] = mask_ref[:, last] * (0.5 + scale * total) - goal_ref[:, last]

    def split2(weight, t):
        g = weight * (1.0 - t * t)
        hi = g.astype(jnp.bfloat16)
        return [hi, (g - hi.astype(jnp.float32)).astype(jnp.bfloat16)]

    def sums(terms, parts):
        hi, lo = [jnp.concatenate(v, axis=1) for v in zip(*parts)]
        return (lax.dot_general(hi, terms, NT, preferred_element_type=jnp.float32).T
                + lax.dot_general(terms, lo, NT, preferred_element_type=jnp.float32))

    def grad_some(b, carry):
        if end:
            last = sums(terms_end_ref[b], [split2(weight_end_ref[...], tanh_end(b))])
        for inside in range(fold):
            s = b * fold + inside
            parts = [split2(weight_ref[:, pl.ds(start, size)], tanh_block(s, start, size)) for start, size in chunks]
            total = sums(rhs_ref[s, pl.ds(0, 16), :], parts)
            if end:
                total += last[16 * inside:16 * inside + 16]
            total = total[:, :n_rows]
            g, i = lax.div(s, per), lax.rem(s, per)
            both = both_ref[g, pl.ds(i, 1), :]
            for c in range(3):
                xyz = both[:, 3 * piece + c * n_rows:3 * piece + (c + 1) * n_rows]
                grad_ref[g, c, pl.ds(i, 1), :] = (0.25 / 16) * (
                    total[c:c + 1] + total[8 + c:9 + c] - total[3:4] * xyz)
        return carry

    lax.fori_loop(0, structs // fold, grad_some, 0, unroll=UNROLL)


def split_ens(n_ens, beads, tiles):
    best = None
    for parts in range(1, n_ens + 1):
        if n_ens % parts or beads % parts or beads % (n_ens // parts):
            continue
        cost = 2 * (beads // parts) + tiles * (beads // (n_ens // parts))
        if best is None or cost < best[0]:
            best = (cost, parts)
    return best[1]


def on_device(coords, counts, segments):
    local_n, _, beads = coords.shape
    n_tile = lax.axis_size("tile")
    n_ens = lax.axis_size("ens")
    structs = local_n * n_ens
    n_p = split_ens(n_ens, beads, n_tile)
    n_q = n_ens // n_p
    n_rows, piece = beads // n_p, beads // n_q
    n_cols = piece * n_tile
    tile, ens = lax.axis_index("tile"), lax.axis_index("ens")
    p, q = lax.rem(ens, n_p), lax.div(ens, n_p)
    vmem = pl.BlockSpec(memory_space=pltpu.VMEM)

    send = pl.pallas_call(
        functools.partial(pack_kernel, n_p, n_q),
        out_shape=jax.ShapeDtypeStruct((n_ens, local_n, 3 * (piece + n_rows)), jnp.float32),
        in_specs=[vmem],
        out_specs=vmem,
        name="pack",
    )(jnp.swapaxes(coords, 0, 1))
    both = lax.all_to_all(send, "ens", 0, 0, tiled=True)

    row_base = tile * beads + p * n_rows
    col_bases = [lax.rem(tile + k, n_tile) * beads + q * piece for k in range(n_tile)]
    own_counts = lax.dynamic_slice_in_dim(counts, p * n_rows, n_rows, 0)
    block = jnp.concatenate([lax.dynamic_slice_in_dim(own_counts, b, piece, 1) for b in col_bases], axis=1)
    seg_cols = jnp.concatenate([lax.dynamic_slice_in_dim(segments, b, piece) for b in col_bases])[None, :]
    col_ids = jnp.concatenate([b + jnp.arange(piece, dtype=jnp.int32) for b in col_bases])[None, :]
    seg_rows = lax.dynamic_slice_in_dim(segments, row_base, n_rows)[:, None]

    full = n_cols // LANES * LANES
    end = n_cols - full
    fold = LANES // end if end and LANES % end == 0 and local_n % (LANES // end) == 0 else 1
    deep = up(n_rows, 16)
    row_wide, col_wide = up(n_rows, LANES), up(n_cols, LANES)
    blocks = structs // fold
    masks = pl.pallas_call(
        functools.partial(mask_kernel, fold),
        out_shape=[jax.ShapeDtypeStruct((deep, col_wide), jnp.float32)] * 2,
        in_specs=[pl.BlockSpec(memory_space=pltpu.SMEM)] + [vmem] * 4,
        out_specs=[vmem] * 2,
        compiler_params=pltpu.CompilerParams(vmem_limit_bytes=32 << 20),
        name="masks",
    )(row_base[None], seg_rows, seg_cols, col_ids, block)
    both, masks = lax.optimization_barrier((both, masks))
    own = both[:, :, :3 * piece]
    pieces = [lax.ppermute(own, "tile", [(t, (t - k) % n_tile) for t in range(n_tile)]) for k in range(1, n_tile)]

    lhs, lhs_end = pl.pallas_call(
        functools.partial(row_kernel, n_rows, fold),
        out_shape=[
            jax.ShapeDtypeStruct((structs, deep, 48), jnp.bfloat16),
            jax.ShapeDtypeStruct((blocks, deep, fold * SLOT), jnp.bfloat16),
        ],
        in_specs=[vmem],
        out_specs=[vmem] * 2,
        scratch_shapes=[[pltpu.VMEM((row_wide // LANES, 8 * local_n, LANES), jnp.float32)] * 3],
        compiler_params=pltpu.CompilerParams(vmem_limit_bytes=32 << 20),
        name="rows",
    )(both)
    grad = pl.pallas_call(
        functools.partial(pair_kernel, n_tile, fold, n_rows, n_cols),
        out_shape=jax.ShapeDtypeStruct((n_ens, 3, local_n, n_rows), jnp.float32),
        in_specs=[vmem] * (4 + n_tile),
        out_specs=vmem,
        scratch_shapes=[
            [pltpu.VMEM((col_wide // LANES, 8 * local_n, LANES), jnp.float32)] * 3,
            pltpu.VMEM((structs, 48, full), jnp.bfloat16),
            pltpu.VMEM((blocks, fold * SLOT, LANES), jnp.bfloat16),
            pltpu.VMEM((blocks, fold * 16, LANES), jnp.bfloat16),
            pltpu.VMEM((deep, full), jnp.float32),
            pltpu.VMEM((deep, LANES), jnp.float32),
        ],
        compiler_params=pltpu.CompilerParams(vmem_limit_bytes=40 << 20),
        name="pairs",
    )(*masks, lhs, lhs_end, both, *pieces)

    back = lax.all_to_all(grad, "ens", 0, 0, tiled=True)
    total = pl.pallas_call(
        functools.partial(sum_kernel, n_p, n_q),
        out_shape=jax.ShapeDtypeStruct((3, local_n, beads), jnp.float32),
        in_specs=[vmem],
        out_specs=vmem,
        name="total",
    )(back)
    return jnp.swapaxes(total, 0, 1)


def solution(mesh):
    return jax.shard_map(
        on_device,
        mesh=mesh,
        in_specs=(P("ens", None, "tile"), P("tile", None), P()),
        out_specs=P("ens", None, "tile"),
        check_vma=False,
    )
```

```python
import functools

import jax
import jax.numpy as jnp
from jax import lax
from jax.experimental import pallas as pl
from jax.experimental.pallas import tpu as pltpu
from jax.sharding import PartitionSpec as P

LANES = 128
WIDE = 256
SLOT = 64
KEEP_BYTES = 24 << 20
NT = (((1,), (1,)), ((), ()))


def up(n, unit):
    return -(-n // unit) * unit


def split3(v):
    hi = v.astype(jnp.bfloat16).astype(jnp.float32)
    rest = v - hi
    mid = rest.astype(jnp.bfloat16).astype(jnp.float32)
    return hi, mid, rest - mid


def pack_kernel(n_p, n_q, xyz_ref, send_ref):
    beads = xyz_ref.shape[2]
    n_rows, piece = beads // n_p, beads // n_q
    for c in range(3):
        for q in range(n_q):
            for p in range(n_p):
                e = q * n_p + p
                send_ref[e, :, pl.ds(c * piece, piece)] = xyz_ref[c, :, pl.ds(q * piece, piece)]
                send_ref[e, :, pl.ds(3 * piece + c * n_rows, n_rows)] = xyz_ref[c, :, pl.ds(p * n_rows, n_rows)]


def sum_kernel(n_p, n_q, back_ref, total_ref):
    n_rows = back_ref.shape[3]
    for c in range(3):
        for p in range(n_p):
            total = back_ref[p, c]
            for q in range(1, n_q):
                total += back_ref[q * n_p + p, c]
            total_ref[c, :, pl.ds(p * n_rows, n_rows)] = total


def put_terms(refs, xyz, norm_row):
    norm = 1.5 - 0.5 * (xyz[0] * xyz[0] + xyz[1] * xyz[1] + xyz[2] * xyz[2])
    n, size = norm.shape
    wide = refs[0].shape[0] * LANES
    for f, v in ((0, xyz[0]), (1, xyz[1]), (2, xyz[2]), (norm_row, norm)):
        if wide > size:
            v = jnp.concatenate([v, jnp.zeros((n, wide - size), jnp.float32)], axis=1)
        for ref, term in zip(refs, split3(v)):
            for k in range(wide // LANES):
                ref[k, pl.ds(f, n, 8), :] = term[:, k * LANES:(k + 1) * LANES]


def get_terms(refs, i):
    return [jnp.concatenate([ref[k, pl.ds(8 * i, 8), :] for k in range(ref.shape[0])], axis=1) for ref in refs]


def init_terms(refs, one_row, per):
    for ref in refs:
        ref[...] = jnp.zeros_like(ref)
    for k in range(refs[0].shape[0]):
        refs[0][k, pl.ds(one_row, per, 8), :] = jnp.ones((per, LANES), jnp.float32)


def row_kernel(n_rows, fold, both_ref, lhs_ref, lhs_end_ref, row_terms):
    groups, per, width = both_ref.shape
    deep = lhs_ref.shape[1]
    first = width - 3 * n_rows
    init_terms(row_terms, 4, per)

    def features(g, carry):
        both = both_ref[g]
        put_terms(row_terms, [both[:, first + c * n_rows:first + (c + 1) * n_rows] for c in range(3)], 3)
        for block in range(per // fold):
            lefts = []
            for inside in range(fold):
                i = block * fold + inside
                hi, mid, lo = get_terms(row_terms, i)
                left = jnp.concatenate([hi, hi, mid, mid, hi, lo], axis=0)
                lhs_ref[g * per + i] = left.T[:deep].astype(jnp.bfloat16)
                lefts += [left, jnp.zeros((SLOT - 48, left.shape[1]), jnp.float32)]
            lhs_end_ref[g * (per // fold) + block] = jnp.concatenate(lefts, axis=0).T[:deep].astype(jnp.bfloat16)
        return carry

    lax.fori_loop(0, groups, features, 0)


def mask_kernel(fold, base_ref, seg_rows_ref, seg_cols_ref, col_ids_ref, counts_ref, mask_ref, goal_ref):
    n_rows, n_cols = counts_ref.shape
    deep = mask_ref.shape[0]
    full = n_cols // LANES * LANES
    end = n_cols - full
    rows = pl.ds(0, n_rows)
    if deep > n_rows:
        for ref in (mask_ref, goal_ref):
            ref[pl.ds(n_rows, deep - n_rows), :] = jnp.zeros((deep - n_rows, ref.shape[1]), jnp.float32)

    def mask_and_goal(start, size):
        count = counts_ref[:, pl.ds(start, size)].astype(jnp.float32)
        row_ids = base_ref[0] + lax.broadcasted_iota(jnp.int32, (n_rows, size), 0)
        mask = jnp.where(seg_rows_ref[...] == seg_cols_ref[:, pl.ds(start, size)], 1.0, 0.3)
        mask = jnp.where(row_ids == col_ids_ref[:, pl.ds(start, size)], 0.0, mask)
        return mask, mask * (count / (count + 8.0))

    for start in range(0, full, LANES):
        mask_ref[rows, pl.ds(start, LANES)], goal_ref[rows, pl.ds(start, LANES)] = mask_and_goal(start, LANES)
    if end:
        def spread(v):
            v = jnp.concatenate([v, jnp.zeros((n_rows, LANES - end), jnp.float32)], axis=1)
            return sum((pltpu.roll(v, k * end, 1) for k in range(1, fold)), v)

        last = pl.ds(full, LANES)
        mask_ref[rows, last], goal_ref[rows, last] = [spread(v) for v in mask_and_goal(full, end)]


def pair_kernel(tiles, fold, n_rows, n_cols, mask_ref, goal_ref, lhs_ref, lhs_end_ref, both_ref, *rest):
    piece_refs = rest[:tiles - 1]
    (grad_ref, col_terms, rhs_ref, rhs_end_ref, terms_end_ref, weight_ref, weight_end_ref, kept_ref,
     kept_end_ref) = rest[tiles - 1:]
    groups, per, _ = both_ref.shape
    structs = groups * per
    piece = n_cols // tiles
    deep = weight_ref.shape[0]
    full = rhs_ref.shape[2]
    end = n_cols - full
    chunks = [(a, min(WIDE, full - a)) for a in range(0, full, WIDE)]

    init_terms(col_terms, 3, per)
    if end:
        rhs_end_ref[...] = jnp.zeros_like(rhs_end_ref)

    def features(g):
        both = both_ref[g]
        parts = [both] + [ref[g] for ref in piece_refs]
        cols = [jnp.concatenate([v[:, c * piece:(c + 1) * piece] for v in parts], axis=1) for c in range(3)]
        put_terms(col_terms, cols, 4)
        for block in range(per // fold):
            for inside in range(fold):
                i = block * fold + inside
                s = g * per + i
                hi, mid, lo = get_terms(col_terms, i)
                right = jnp.concatenate([hi, mid, hi, mid, lo, hi], axis=0)
                rhs_ref[s] = right[:, :full].astype(jnp.bfloat16)
                if end:
                    lane = lax.broadcasted_iota(jnp.int32, (48, LANES), 1)
                    last = jnp.where(lane < end, right[:, full:full + LANES], 0.0)
                    if inside:
                        last = pltpu.roll(last, inside * end, 1)
                    last = last.astype(jnp.bfloat16)
                    b = g * (per // fold) + block
                    rhs_end_ref[b, pl.ds(SLOT * inside, 48), :] = last
                    terms_end_ref[b, pl.ds(16 * inside, 16), :] = last[0:16]

    weight_ref[...] = jnp.zeros_like(weight_ref)
    if end:
        weight_end_ref[...] = jnp.zeros_like(weight_end_ref)

    def tanh_block(s, start, size):
        return jnp.tanh(jnp.dot(lhs_ref[s], rhs_ref[s, :, pl.ds(start, size)], preferred_element_type=jnp.float32))

    def tanh_end(b):
        return jnp.tanh(jnp.dot(lhs_end_ref[b], rhs_end_ref[b], preferred_element_type=jnp.float32))

    def add_some(b, keep):
        for inside in range(0, fold, 2):
            for start, size in chunks:
                t = []
                for i in range(inside, min(inside + 2, fold)):
                    t.append(tanh_block(b * fold + i, start, size))
                    if keep:
                        kept_ref[b * fold + i, :, pl.ds(start, size)] = t[-1]
                weight_ref[:, pl.ds(start, size)] += functools.reduce(jnp.add, t)
        if end:
            t = tanh_end(b)
            if keep:
                kept_end_ref[b] = t
            weight_end_ref[...] += t

    together = 2 if groups % 2 == 0 else 1
    per_step = together * (per // fold)
    kept = kept_ref.shape[0] // (per_step * fold)

    def add_groups(keep, step, carry):
        for j in range(together):
            features(step * together + j)
        for j in range(per_step):
            add_some(step * per_step + j, keep)
        return carry

    lax.fori_loop(0, kept, functools.partial(add_groups, True), 0)
    lax.fori_loop(kept, groups // together, functools.partial(add_groups, False), 0)

    scale = 0.5 / structs
    for start, size in chunks:
        cut = pl.ds(start, size)
        weight_ref[:, cut] = mask_ref[:, cut] * (0.5 + scale * weight_ref[:, cut]) - goal_ref[:, cut]
    if end:
        part = weight_end_ref[...]
        total = sum((pltpu.roll(part, k * end, 1) for k in range(1, fold)), part)
        last = pl.ds(full, LANES)
        weight_end_ref[...] = mask_ref[:, last] * (0.5 + scale * total) - goal_ref[:, last]

    def split2(weight, t):
        g = weight * (1.0 - t * t)
        hi = g.astype(jnp.bfloat16)
        return [hi, (g - hi.astype(jnp.float32)).astype(jnp.bfloat16)]

    def sums(terms, parts):
        hi, lo = [jnp.concatenate(v, axis=1) for v in zip(*parts)]
        return (lax.dot_general(hi, terms, NT, preferred_element_type=jnp.float32).T
                + lax.dot_general(terms, lo, NT, preferred_element_type=jnp.float32))

    def grad_some(b, keep):
        if end:
            t = kept_end_ref[b] if keep else tanh_end(b)
            last = sums(terms_end_ref[b], [split2(weight_end_ref[...], t)])
        for inside in range(fold):
            s = b * fold + inside
            parts = []
            for start, size in chunks:
                cut = pl.ds(start, size)
                parts.append(split2(weight_ref[:, cut], kept_ref[s, :, cut] if keep else tanh_block(s, start, size)))
            total = sums(rhs_ref[s, pl.ds(0, 16), :], parts)
            if end:
                total += last[16 * inside:16 * inside + 16]
            total = total[:, :n_rows]
            g, i = lax.div(s, per), lax.rem(s, per)
            both = both_ref[g, pl.ds(i, 1), :]
            for c in range(3):
                xyz = both[:, 3 * piece + c * n_rows:3 * piece + (c + 1) * n_rows]
                grad_ref[g, c, pl.ds(i, 1), :] = (0.25 / 16) * (
                    total[c:c + 1] + total[8 + c:9 + c] - total[3:4] * xyz)

    def grad_groups(keep, step, carry):
        for j in range(per_step):
            grad_some(step * per_step + j, keep)
        return carry

    lax.fori_loop(0, kept, functools.partial(grad_groups, True), 0)
    lax.fori_loop(kept, groups // together, functools.partial(grad_groups, False), 0)


def split_ens(n_ens, beads, tiles):
    best = None
    for parts in range(1, n_ens + 1):
        if n_ens % parts or beads % parts or beads % (n_ens // parts):
            continue
        cost = 2 * (beads // parts) + tiles * (beads // (n_ens // parts))
        if best is None or cost < best[0]:
            best = (cost, parts)
    return best[1]


def on_device(coords, counts, segments):
    local_n, _, beads = coords.shape
    n_tile = lax.axis_size("tile")
    n_ens = lax.axis_size("ens")
    structs = local_n * n_ens
    n_p = split_ens(n_ens, beads, n_tile)
    n_q = n_ens // n_p
    n_rows, piece = beads // n_p, beads // n_q
    n_cols = piece * n_tile
    tile, ens = lax.axis_index("tile"), lax.axis_index("ens")
    p, q = lax.rem(ens, n_p), lax.div(ens, n_p)
    vmem = pl.BlockSpec(memory_space=pltpu.VMEM)

    send = pl.pallas_call(
        functools.partial(pack_kernel, n_p, n_q),
        out_shape=jax.ShapeDtypeStruct((n_ens, local_n, 3 * (piece + n_rows)), jnp.float32),
        in_specs=[vmem],
        out_specs=vmem,
        name="pack",
    )(jnp.swapaxes(coords, 0, 1))
    both = lax.all_to_all(send, "ens", 0, 0, tiled=True)

    row_base = tile * beads + p * n_rows
    col_bases = [lax.rem(tile + k, n_tile) * beads + q * piece for k in range(n_tile)]
    own_counts = lax.dynamic_slice_in_dim(counts, p * n_rows, n_rows, 0)
    block = jnp.concatenate([lax.dynamic_slice_in_dim(own_counts, b, piece, 1) for b in col_bases], axis=1)
    seg_cols = jnp.concatenate([lax.dynamic_slice_in_dim(segments, b, piece) for b in col_bases])[None, :]
    col_ids = jnp.concatenate([b + jnp.arange(piece, dtype=jnp.int32) for b in col_bases])[None, :]
    seg_rows = lax.dynamic_slice_in_dim(segments, row_base, n_rows)[:, None]

    full = n_cols // LANES * LANES
    end = n_cols - full
    fold = LANES // end if end and LANES % end == 0 and local_n % (LANES // end) == 0 else 1
    deep = up(n_rows, 16)
    row_wide, col_wide = up(n_rows, LANES), up(n_cols, LANES)
    blocks = structs // fold
    kept = min(structs, local_n * (2 if n_ens % 2 == 0 else 1))
    if 4 * kept * deep * (full + LANES) > KEEP_BYTES:
        kept = 0
    masks = pl.pallas_call(
        functools.partial(mask_kernel, fold),
        out_shape=[jax.ShapeDtypeStruct((deep, col_wide), jnp.float32)] * 2,
        in_specs=[pl.BlockSpec(memory_space=pltpu.SMEM)] + [vmem] * 4,
        out_specs=[vmem] * 2,
        compiler_params=pltpu.CompilerParams(vmem_limit_bytes=32 << 20),
        name="masks",
    )(row_base[None], seg_rows, seg_cols, col_ids, block)
    both, masks = lax.optimization_barrier((both, masks))
    own = both[:, :, :3 * piece]
    pieces = [lax.ppermute(own, "tile", [(t, (t - k) % n_tile) for t in range(n_tile)]) for k in range(1, n_tile)]

    lhs, lhs_end = pl.pallas_call(
        functools.partial(row_kernel, n_rows, fold),
        out_shape=[
            jax.ShapeDtypeStruct((structs, deep, 48), jnp.bfloat16),
            jax.ShapeDtypeStruct((blocks, deep, fold * SLOT), jnp.bfloat16),
        ],
        in_specs=[vmem],
        out_specs=[vmem] * 2,
        scratch_shapes=[[pltpu.VMEM((row_wide // LANES, 8 * local_n, LANES), jnp.float32)] * 3],
        compiler_params=pltpu.CompilerParams(vmem_limit_bytes=32 << 20),
        name="rows",
    )(both)
    grad = pl.pallas_call(
        functools.partial(pair_kernel, n_tile, fold, n_rows, n_cols),
        out_shape=jax.ShapeDtypeStruct((n_ens, 3, local_n, n_rows), jnp.float32),
        in_specs=[vmem] * (4 + n_tile),
        out_specs=vmem,
        scratch_shapes=[
            [pltpu.VMEM((col_wide // LANES, 8 * local_n, LANES), jnp.float32)] * 3,
            pltpu.VMEM((structs, 48, full), jnp.bfloat16),
            pltpu.VMEM((blocks, fold * SLOT, LANES), jnp.bfloat16),
            pltpu.VMEM((blocks, fold * 16, LANES), jnp.bfloat16),
            pltpu.VMEM((deep, full), jnp.float32),
            pltpu.VMEM((deep, LANES), jnp.float32),
            pltpu.VMEM((max(kept, 1), deep, full), jnp.float32),
            pltpu.VMEM((max(kept // fold, 1), deep, LANES), jnp.float32),
        ],
        compiler_params=pltpu.CompilerParams(vmem_limit_bytes=44 << 20),
        name="pairs",
    )(*masks, lhs, lhs_end, both, *pieces)

    back = lax.all_to_all(grad, "ens", 0, 0, tiled=True)
    total = pl.pallas_call(
        functools.partial(sum_kernel, n_p, n_q),
        out_shape=jax.ShapeDtypeStruct((3, local_n, beads), jnp.float32),
        in_specs=[vmem],
        out_specs=vmem,
        name="total",
    )(back)
    return jnp.swapaxes(total, 0, 1)


def solution(mesh):
    return jax.shard_map(
        on_device,
        mesh=mesh,
        in_specs=(P("ens", None, "tile"), P("tile", None), P()),
        out_specs=P("ens", None, "tile"),
        check_vma=False,
    )
```

```python
import functools

import jax
import jax.numpy as jnp
from jax import lax
from jax.experimental import pallas as pl
from jax.experimental.pallas import tpu as pltpu
from jax.sharding import PartitionSpec as P

LANES = 128
WIDE = 256
SLOT = 64
TOGETHER = 4
NT = (((1,), (1,)), ((), ()))


def up(n, unit):
    return -(-n // unit) * unit


def split3(v):
    hi = v.astype(jnp.bfloat16).astype(jnp.float32)
    rest = v - hi
    mid = rest.astype(jnp.bfloat16).astype(jnp.float32)
    return hi, mid, rest - mid


def pack_kernel(n_p, n_q, xyz_ref, send_ref):
    beads = xyz_ref.shape[2]
    n_rows, piece = beads // n_p, beads // n_q
    for c in range(3):
        for q in range(n_q):
            for p in range(n_p):
                e = q * n_p + p
                send_ref[e, :, pl.ds(c * piece, piece)] = xyz_ref[c, :, pl.ds(q * piece, piece)]
                send_ref[e, :, pl.ds(3 * piece + c * n_rows, n_rows)] = xyz_ref[c, :, pl.ds(p * n_rows, n_rows)]


def sum_kernel(n_p, n_q, back_ref, total_ref):
    n_rows = back_ref.shape[3]
    for c in range(3):
        for p in range(n_p):
            total = back_ref[p, c]
            for q in range(1, n_q):
                total += back_ref[q * n_p + p, c]
            total_ref[c, :, pl.ds(p * n_rows, n_rows)] = total


def put_terms(refs, xyz, norm_row):
    norm = 1.5 - 0.5 * (xyz[0] * xyz[0] + xyz[1] * xyz[1] + xyz[2] * xyz[2])
    n, size = norm.shape
    wide = refs[0].shape[0] * LANES
    for f, v in ((0, xyz[0]), (1, xyz[1]), (2, xyz[2]), (norm_row, norm)):
        if wide > size:
            v = jnp.concatenate([v, jnp.zeros((n, wide - size), jnp.float32)], axis=1)
        for ref, term in zip(refs, split3(v)):
            for k in range(wide // LANES):
                ref[k, pl.ds(f, n, 8), :] = term[:, k * LANES:(k + 1) * LANES]


def get_terms(refs, i):
    return [jnp.concatenate([ref[k, pl.ds(8 * i, 8), :] for k in range(ref.shape[0])], axis=1) for ref in refs]


def init_terms(refs, one_row, per):
    for ref in refs:
        ref[...] = jnp.zeros_like(ref)
    for k in range(refs[0].shape[0]):
        refs[0][k, pl.ds(one_row, per, 8), :] = jnp.ones((per, LANES), jnp.float32)


def row_kernel(n_rows, fold, both_ref, lhs_ref, lhs_end_ref, row_terms):
    groups, per, width = both_ref.shape
    deep = lhs_ref.shape[1]
    first = width - 3 * n_rows
    init_terms(row_terms, 4, per)

    def features(g, carry):
        both = both_ref[g]
        put_terms(row_terms, [both[:, first + c * n_rows:first + (c + 1) * n_rows] for c in range(3)], 3)
        for block in range(per // fold):
            lefts = []
            for inside in range(fold):
                i = block * fold + inside
                hi, mid, lo = get_terms(row_terms, i)
                left = jnp.concatenate([hi, hi, mid, mid, hi, lo], axis=0)
                lhs_ref[g * per + i] = left.T[:deep].astype(jnp.bfloat16)
                lefts += [left, jnp.zeros((SLOT - 48, left.shape[1]), jnp.float32)]
            lhs_end_ref[g * (per // fold) + block] = jnp.concatenate(lefts, axis=0).T[:deep].astype(jnp.bfloat16)
        return carry

    lax.fori_loop(0, groups, features, 0)


def mask_kernel(fold, base_ref, seg_rows_ref, seg_cols_ref, col_ids_ref, counts_ref, mask_ref, goal_ref):
    n_rows, n_cols = counts_ref.shape
    deep = mask_ref.shape[0]
    full = n_cols // LANES * LANES
    end = n_cols - full
    rows = pl.ds(0, n_rows)
    if deep > n_rows:
        for ref in (mask_ref, goal_ref):
            ref[pl.ds(n_rows, deep - n_rows), :] = jnp.zeros((deep - n_rows, ref.shape[1]), jnp.float32)

    def mask_and_goal(start, size):
        count = counts_ref[:, pl.ds(start, size)].astype(jnp.float32)
        row_ids = base_ref[0] + lax.broadcasted_iota(jnp.int32, (n_rows, size), 0)
        mask = jnp.where(seg_rows_ref[...] == seg_cols_ref[:, pl.ds(start, size)], 1.0, 0.3)
        mask = jnp.where(row_ids == col_ids_ref[:, pl.ds(start, size)], 0.0, mask)
        return mask, mask * (count / (count + 8.0))

    for start in range(0, full, LANES):
        mask_ref[rows, pl.ds(start, LANES)], goal_ref[rows, pl.ds(start, LANES)] = mask_and_goal(start, LANES)
    if end:
        def spread(v):
            v = jnp.concatenate([v, jnp.zeros((n_rows, LANES - end), jnp.float32)], axis=1)
            return sum((pltpu.roll(v, k * end, 1) for k in range(1, fold)), v)

        last = pl.ds(full, LANES)
        mask_ref[rows, last], goal_ref[rows, last] = [spread(v) for v in mask_and_goal(full, end)]


def pair_kernel(tiles, fold, n_rows, n_cols, mask_ref, goal_ref, lhs_ref, lhs_end_ref, both_ref, *rest):
    piece_refs = rest[:tiles - 1]
    grad_ref, col_terms, rhs_ref, rhs_end_ref, terms_end_ref, weight_ref, weight_end_ref, sums_ref = rest[tiles - 1:]
    groups, per, _ = both_ref.shape
    structs = groups * per
    piece = n_cols // tiles
    deep = weight_ref.shape[0]
    full = rhs_ref.shape[2]
    end = n_cols - full
    chunks = [(a, min(WIDE, full - a)) for a in range(0, full, WIDE)]

    init_terms(col_terms, 3, per)
    if end:
        rhs_end_ref[...] = jnp.zeros_like(rhs_end_ref)

    def features(g):
        both = both_ref[g]
        parts = [both] + [ref[g] for ref in piece_refs]
        cols = [jnp.concatenate([v[:, c * piece:(c + 1) * piece] for v in parts], axis=1) for c in range(3)]
        put_terms(col_terms, cols, 4)
        for block in range(per // fold):
            for inside in range(fold):
                i = block * fold + inside
                s = g * per + i
                hi, mid, lo = get_terms(col_terms, i)
                right = jnp.concatenate([hi, mid, hi, mid, lo, hi], axis=0)
                rhs_ref[s] = right[:, :full].astype(jnp.bfloat16)
                if end:
                    lane = lax.broadcasted_iota(jnp.int32, (48, LANES), 1)
                    last = jnp.where(lane < end, right[:, full:full + LANES], 0.0)
                    if inside:
                        last = pltpu.roll(last, inside * end, 1)
                    last = last.astype(jnp.bfloat16)
                    b = g * (per // fold) + block
                    rhs_end_ref[b, pl.ds(SLOT * inside, 48), :] = last
                    terms_end_ref[b, pl.ds(16 * inside, 16), :] = last[0:16]

    weight_ref[...] = jnp.zeros_like(weight_ref)
    if end:
        weight_end_ref[...] = jnp.zeros_like(weight_end_ref)

    def tanh_block(s, start, size):
        return jnp.tanh(jnp.dot(lhs_ref[s], rhs_ref[s, :, pl.ds(start, size)], preferred_element_type=jnp.float32))

    def tanh_end(b):
        return jnp.tanh(jnp.dot(lhs_end_ref[b], rhs_end_ref[b], preferred_element_type=jnp.float32))

    def add_some(b):
        for inside in range(0, fold, 2):
            for start, size in chunks:
                t = [tanh_block(b * fold + i, start, size) for i in range(inside, min(inside + 2, fold))]
                weight_ref[:, pl.ds(start, size)] += functools.reduce(jnp.add, t)
        if end:
            weight_end_ref[...] += tanh_end(b)

    together = TOGETHER if groups % TOGETHER == 0 else 1

    def add_groups(step, carry):
        for j in range(together):
            features(step * together + j)
        for j in range(together * (per // fold)):
            add_some(step * (together * (per // fold)) + j)
        return carry

    lax.fori_loop(0, groups // together, add_groups, 0)

    scale = 0.5 / structs
    for start, size in chunks:
        cut = pl.ds(start, size)
        weight_ref[:, cut] = mask_ref[:, cut] * (0.5 + scale * weight_ref[:, cut]) - goal_ref[:, cut]
    if end:
        part = weight_end_ref[...]
        total = sum((pltpu.roll(part, k * end, 1) for k in range(1, fold)), part)
        last = pl.ds(full, LANES)
        weight_end_ref[...] = mask_ref[:, last] * (0.5 + scale * total) - goal_ref[:, last]

    def split2(weight, t):
        g = weight * (1.0 - t * t)
        hi = g.astype(jnp.bfloat16)
        return [hi, (g - hi.astype(jnp.float32)).astype(jnp.bfloat16)]

    def sums(terms, parts):
        hi, lo = [jnp.concatenate(v, axis=1) for v in zip(*parts)]
        return (lax.dot_general(hi, terms, NT, preferred_element_type=jnp.float32).T
                + lax.dot_general(terms, lo, NT, preferred_element_type=jnp.float32))

    def grad_group(g):
        for block in range(per // fold):
            b = g * (per // fold) + block
            if end:
                last = sums(terms_end_ref[b], [split2(weight_end_ref[...], tanh_end(b))])
            for inside in range(fold):
                s = b * fold + inside
                parts = [split2(weight_ref[:, pl.ds(start, size)], tanh_block(s, start, size)) for start, size in chunks]
                total = sums(rhs_ref[s, pl.ds(0, 16), :], parts)
                if end:
                    total += last[16 * inside:16 * inside + 16]
                total = total[:, :n_rows]
                mixed = total[0:3] + total[8:11]
                i = block * fold + inside
                for c in range(3):
                    sums_ref[c, pl.ds(i, 1), :] = mixed[c:c + 1]
                sums_ref[3, pl.ds(i, 1), :] = total[3:4]
        both = both_ref[g]
        for c in range(3):
            xyz = both[:, 3 * piece + c * n_rows:3 * piece + (c + 1) * n_rows]
            grad_ref[g, c] = (0.25 / 16) * (sums_ref[c] - sums_ref[3] * xyz)

    def grad_groups(step, carry):
        for j in range(together):
            grad_group(step * together + j)
        return carry

    lax.fori_loop(0, groups // together, grad_groups, 0)


def split_ens(n_ens, beads, tiles):
    best = None
    for parts in range(1, n_ens + 1):
        if n_ens % parts or beads % parts or beads % (n_ens // parts):
            continue
        cost = 2 * (beads // parts) + tiles * (beads // (n_ens // parts))
        if best is None or cost < best[0]:
            best = (cost, parts)
    return best[1]


def on_device(coords, counts, segments):
    local_n, _, beads = coords.shape
    n_tile = lax.axis_size("tile")
    n_ens = lax.axis_size("ens")
    structs = local_n * n_ens
    n_p = split_ens(n_ens, beads, n_tile)
    n_q = n_ens // n_p
    n_rows, piece = beads // n_p, beads // n_q
    n_cols = piece * n_tile
    tile, ens = lax.axis_index("tile"), lax.axis_index("ens")
    p, q = lax.rem(ens, n_p), lax.div(ens, n_p)
    vmem = pl.BlockSpec(memory_space=pltpu.VMEM)

    send = pl.pallas_call(
        functools.partial(pack_kernel, n_p, n_q),
        out_shape=jax.ShapeDtypeStruct((n_ens, local_n, 3 * (piece + n_rows)), jnp.float32),
        in_specs=[vmem],
        out_specs=vmem,
        name="pack",
    )(jnp.swapaxes(coords, 0, 1))
    both = lax.all_to_all(send, "ens", 0, 0, tiled=True)

    row_base = tile * beads + p * n_rows
    col_bases = [lax.rem(tile + k, n_tile) * beads + q * piece for k in range(n_tile)]
    own_counts = lax.dynamic_slice_in_dim(counts, p * n_rows, n_rows, 0)
    block = jnp.concatenate([lax.dynamic_slice_in_dim(own_counts, b, piece, 1) for b in col_bases], axis=1)
    seg_cols = jnp.concatenate([lax.dynamic_slice_in_dim(segments, b, piece) for b in col_bases])[None, :]
    col_ids = jnp.concatenate([b + jnp.arange(piece, dtype=jnp.int32) for b in col_bases])[None, :]
    seg_rows = lax.dynamic_slice_in_dim(segments, row_base, n_rows)[:, None]

    full = n_cols // LANES * LANES
    end = n_cols - full
    fold = LANES // end if end and LANES % end == 0 and local_n % (LANES // end) == 0 else 1
    deep = up(n_rows, 16)
    row_wide, col_wide = up(n_rows, LANES), up(n_cols, LANES)
    blocks = structs // fold
    masks = pl.pallas_call(
        functools.partial(mask_kernel, fold),
        out_shape=[jax.ShapeDtypeStruct((deep, col_wide), jnp.float32)] * 2,
        in_specs=[pl.BlockSpec(memory_space=pltpu.SMEM)] + [vmem] * 4,
        out_specs=[vmem] * 2,
        compiler_params=pltpu.CompilerParams(vmem_limit_bytes=32 << 20),
        name="masks",
    )(row_base[None], seg_rows, seg_cols, col_ids, block)
    both, masks = lax.optimization_barrier((both, masks))
    own = both[:, :, :3 * piece]
    pieces = [lax.ppermute(own, "tile", [(t, (t - k) % n_tile) for t in range(n_tile)]) for k in range(1, n_tile)]

    lhs, lhs_end = pl.pallas_call(
        functools.partial(row_kernel, n_rows, fold),
        out_shape=[
            jax.ShapeDtypeStruct((structs, deep, 48), jnp.bfloat16),
            jax.ShapeDtypeStruct((blocks, deep, fold * SLOT), jnp.bfloat16),
        ],
        in_specs=[vmem],
        out_specs=[vmem] * 2,
        scratch_shapes=[[pltpu.VMEM((row_wide // LANES, 8 * local_n, LANES), jnp.float32)] * 3],
        compiler_params=pltpu.CompilerParams(vmem_limit_bytes=32 << 20),
        name="rows",
    )(both)
    grad = pl.pallas_call(
        functools.partial(pair_kernel, n_tile, fold, n_rows, n_cols),
        out_shape=jax.ShapeDtypeStruct((n_ens, 3, local_n, n_rows), jnp.float32),
        in_specs=[vmem] * (4 + n_tile),
        out_specs=vmem,
        scratch_shapes=[
            [pltpu.VMEM((col_wide // LANES, 8 * local_n, LANES), jnp.float32)] * 3,
            pltpu.VMEM((structs, 48, full), jnp.bfloat16),
            pltpu.VMEM((blocks, fold * SLOT, LANES), jnp.bfloat16),
            pltpu.VMEM((blocks, fold * 16, LANES), jnp.bfloat16),
            pltpu.VMEM((deep, full), jnp.float32),
            pltpu.VMEM((deep, LANES), jnp.float32),
            pltpu.VMEM((4, local_n, n_rows), jnp.float32),
        ],
        compiler_params=pltpu.CompilerParams(vmem_limit_bytes=40 << 20),
        name="pairs",
    )(*masks, lhs, lhs_end, both, *pieces)

    back = lax.all_to_all(grad, "ens", 0, 0, tiled=True)
    total = pl.pallas_call(
        functools.partial(sum_kernel, n_p, n_q),
        out_shape=jax.ShapeDtypeStruct((3, local_n, beads), jnp.float32),
        in_specs=[vmem],
        out_specs=vmem,
        name="total",
    )(back)
    return jnp.swapaxes(total, 0, 1)


def solution(mesh):
    return jax.shard_map(
        on_device,
        mesh=mesh,
        in_specs=(P("ens", None, "tile"), P("tile", None), P()),
        out_specs=P("ens", None, "tile"),
        check_vma=False,
    )
```

```python
import functools

import jax
import jax.numpy as jnp
from jax import lax
from jax.experimental import pallas as pl
from jax.experimental.pallas import tpu as pltpu
from jax.sharding import PartitionSpec as P

LANES = 128
WIDE = 256
SLOT = 64
TOGETHER = 2
KEEP_BYTES = 24 << 20
NT = (((1,), (1,)), ((), ()))


def up(n, unit):
    return -(-n // unit) * unit


def split3(v):
    hi = v.astype(jnp.bfloat16).astype(jnp.float32)
    rest = v - hi
    mid = rest.astype(jnp.bfloat16).astype(jnp.float32)
    return hi, mid, rest - mid


def pack_kernel(n_p, n_q, xyz_ref, send_ref):
    beads = xyz_ref.shape[2]
    n_rows, piece = beads // n_p, beads // n_q
    for c in range(3):
        for q in range(n_q):
            for p in range(n_p):
                e = q * n_p + p
                send_ref[e, :, pl.ds(c * piece, piece)] = xyz_ref[c, :, pl.ds(q * piece, piece)]
                send_ref[e, :, pl.ds(3 * piece + c * n_rows, n_rows)] = xyz_ref[c, :, pl.ds(p * n_rows, n_rows)]


def sum_kernel(n_p, n_q, back_ref, total_ref):
    n_rows = back_ref.shape[3]
    for c in range(3):
        for p in range(n_p):
            total = back_ref[p, c]
            for q in range(1, n_q):
                total += back_ref[q * n_p + p, c]
            total_ref[c, :, pl.ds(p * n_rows, n_rows)] = total


def put_terms(refs, xyz, norm_row):
    norm = 1.5 - 0.5 * (xyz[0] * xyz[0] + xyz[1] * xyz[1] + xyz[2] * xyz[2])
    n, size = norm.shape
    wide = refs[0].shape[0] * LANES
    for f, v in ((0, xyz[0]), (1, xyz[1]), (2, xyz[2]), (norm_row, norm)):
        if wide > size:
            v = jnp.concatenate([v, jnp.zeros((n, wide - size), jnp.float32)], axis=1)
        for ref, term in zip(refs, split3(v)):
            for k in range(wide // LANES):
                ref[k, pl.ds(f, n, 8), :] = term[:, k * LANES:(k + 1) * LANES]


def get_terms(refs, i):
    return [jnp.concatenate([ref[k, pl.ds(8 * i, 8), :] for k in range(ref.shape[0])], axis=1) for ref in refs]


def init_terms(refs, one_row, per):
    for ref in refs:
        ref[...] = jnp.zeros_like(ref)
    for k in range(refs[0].shape[0]):
        refs[0][k, pl.ds(one_row, per, 8), :] = jnp.ones((per, LANES), jnp.float32)


def row_kernel(n_rows, fold, both_ref, lhs_ref, lhs_end_ref, row_terms):
    groups, per, width = both_ref.shape
    deep = lhs_ref.shape[1]
    first = width - 3 * n_rows
    init_terms(row_terms, 4, per)

    def features(g, carry):
        both = both_ref[g]
        put_terms(row_terms, [both[:, first + c * n_rows:first + (c + 1) * n_rows] for c in range(3)], 3)
        for block in range(per // fold):
            lefts = []
            for inside in range(fold):
                i = block * fold + inside
                hi, mid, lo = get_terms(row_terms, i)
                left = jnp.concatenate([hi, hi, mid, mid, hi, lo], axis=0)
                lhs_ref[g * per + i] = left.T[:deep].astype(jnp.bfloat16)
                lefts += [left, jnp.zeros((SLOT - 48, left.shape[1]), jnp.float32)]
            lhs_end_ref[g * (per // fold) + block] = jnp.concatenate(lefts, axis=0).T[:deep].astype(jnp.bfloat16)
        return carry

    lax.fori_loop(0, groups, features, 0)


def mask_kernel(fold, base_ref, seg_rows_ref, seg_cols_ref, col_ids_ref, counts_ref, mask_ref, goal_ref):
    n_rows, n_cols = counts_ref.shape
    deep = mask_ref.shape[0]
    full = n_cols // LANES * LANES
    end = n_cols - full
    rows = pl.ds(0, n_rows)
    if deep > n_rows:
        for ref in (mask_ref, goal_ref):
            ref[pl.ds(n_rows, deep - n_rows), :] = jnp.zeros((deep - n_rows, ref.shape[1]), jnp.float32)

    def mask_and_goal(start, size):
        count = counts_ref[:, pl.ds(start, size)].astype(jnp.float32)
        row_ids = base_ref[0] + lax.broadcasted_iota(jnp.int32, (n_rows, size), 0)
        mask = jnp.where(seg_rows_ref[...] == seg_cols_ref[:, pl.ds(start, size)], 1.0, 0.3)
        mask = jnp.where(row_ids == col_ids_ref[:, pl.ds(start, size)], 0.0, mask)
        return mask, mask * (count / (count + 8.0))

    for start in range(0, full, LANES):
        mask_ref[rows, pl.ds(start, LANES)], goal_ref[rows, pl.ds(start, LANES)] = mask_and_goal(start, LANES)
    if end:
        def spread(v):
            v = jnp.concatenate([v, jnp.zeros((n_rows, LANES - end), jnp.float32)], axis=1)
            return sum((pltpu.roll(v, k * end, 1) for k in range(1, fold)), v)

        last = pl.ds(full, LANES)
        mask_ref[rows, last], goal_ref[rows, last] = [spread(v) for v in mask_and_goal(full, end)]


def pair_kernel(tiles, fold, n_rows, n_cols, mask_ref, goal_ref, lhs_ref, lhs_end_ref, both_ref, *rest):
    piece_refs = rest[:tiles - 1]
    (grad_ref, col_terms, rhs_ref, rhs_end_ref, terms_end_ref, weight_ref, weight_end_ref, sums_ref,
     kept_ref, kept_end_ref) = rest[tiles - 1:]
    groups, per, _ = both_ref.shape
    structs = groups * per
    piece = n_cols // tiles
    deep = weight_ref.shape[0]
    full = rhs_ref.shape[2]
    end = n_cols - full
    chunks = [(a, min(WIDE, full - a)) for a in range(0, full, WIDE)]

    init_terms(col_terms, 3, per)
    if end:
        rhs_end_ref[...] = jnp.zeros_like(rhs_end_ref)

    def features(g):
        both = both_ref[g]
        parts = [both] + [ref[g] for ref in piece_refs]
        cols = [jnp.concatenate([v[:, c * piece:(c + 1) * piece] for v in parts], axis=1) for c in range(3)]
        put_terms(col_terms, cols, 4)
        for block in range(per // fold):
            for inside in range(fold):
                i = block * fold + inside
                s = g * per + i
                hi, mid, lo = get_terms(col_terms, i)
                right = jnp.concatenate([hi, mid, hi, mid, lo, hi], axis=0)
                rhs_ref[s] = right[:, :full].astype(jnp.bfloat16)
                if end:
                    lane = lax.broadcasted_iota(jnp.int32, (48, LANES), 1)
                    last = jnp.where(lane < end, right[:, full:full + LANES], 0.0)
                    if inside:
                        last = pltpu.roll(last, inside * end, 1)
                    last = last.astype(jnp.bfloat16)
                    b = g * (per // fold) + block
                    rhs_end_ref[b, pl.ds(SLOT * inside, 48), :] = last
                    terms_end_ref[b, pl.ds(16 * inside, 16), :] = last[0:16]

    weight_ref[...] = jnp.zeros_like(weight_ref)
    if end:
        weight_end_ref[...] = jnp.zeros_like(weight_end_ref)

    def tanh_block(s, start, size):
        return jnp.tanh(jnp.dot(lhs_ref[s], rhs_ref[s, :, pl.ds(start, size)], preferred_element_type=jnp.float32))

    def tanh_end(b):
        return jnp.tanh(jnp.dot(lhs_end_ref[b], rhs_end_ref[b], preferred_element_type=jnp.float32))

    def add_some(b, keep):
        for inside in range(0, fold, 2):
            for start, size in chunks:
                t = []
                for i in range(inside, min(inside + 2, fold)):
                    t.append(tanh_block(b * fold + i, start, size))
                    if keep:
                        kept_ref[b * fold + i, :, pl.ds(start, size)] = 1.0 - t[-1] * t[-1]
                weight_ref[:, pl.ds(start, size)] += functools.reduce(jnp.add, t)
        if end:
            t = tanh_end(b)
            if keep:
                kept_end_ref[b] = 1.0 - t * t
            weight_end_ref[...] += t

    together = TOGETHER if groups % TOGETHER == 0 else 1
    per_step = together * (per // fold)
    kept = kept_ref.shape[0] // (per_step * fold)

    def add_groups(keep, step, carry):
        for j in range(together):
            features(step * together + j)
        for j in range(per_step):
            add_some(step * per_step + j, keep)
        return carry

    lax.fori_loop(0, kept, functools.partial(add_groups, True), 0)
    lax.fori_loop(kept, groups // together, functools.partial(add_groups, False), 0)

    scale = 0.5 / structs
    for start, size in chunks:
        cut = pl.ds(start, size)
        weight_ref[:, cut] = mask_ref[:, cut] * (0.5 + scale * weight_ref[:, cut]) - goal_ref[:, cut]
    if end:
        part = weight_end_ref[...]
        total = sum((pltpu.roll(part, k * end, 1) for k in range(1, fold)), part)
        last = pl.ds(full, LANES)
        weight_end_ref[...] = mask_ref[:, last] * (0.5 + scale * total) - goal_ref[:, last]

    def slope(t):
        return 1.0 - t * t

    def split2(weight, slopes):
        g = weight * slopes
        hi = g.astype(jnp.bfloat16)
        return [hi, (g - hi.astype(jnp.float32)).astype(jnp.bfloat16)]

    def sums(terms, parts):
        hi, lo = [jnp.concatenate(v, axis=1) for v in zip(*parts)]
        return (lax.dot_general(hi, terms, NT, preferred_element_type=jnp.float32).T
                + lax.dot_general(terms, lo, NT, preferred_element_type=jnp.float32))

    def grad_group(g, keep):
        for block in range(per // fold):
            b = g * (per // fold) + block
            if end:
                slopes = kept_end_ref[b] if keep else slope(tanh_end(b))
                last = sums(terms_end_ref[b], [split2(weight_end_ref[...], slopes)])
            for inside in range(fold):
                s = b * fold + inside
                parts = []
                for start, size in chunks:
                    cut = pl.ds(start, size)
                    slopes = kept_ref[s, :, cut] if keep else slope(tanh_block(s, start, size))
                    parts.append(split2(weight_ref[:, cut], slopes))
                total = sums(rhs_ref[s, pl.ds(0, 16), :], parts)
                if end:
                    total += last[16 * inside:16 * inside + 16]
                total = total[:, :n_rows]
                mixed = total[0:3] + total[8:11]
                i = block * fold + inside
                for c in range(3):
                    sums_ref[c, pl.ds(i, 1), :] = mixed[c:c + 1]
                sums_ref[3, pl.ds(i, 1), :] = total[3:4]
        both = both_ref[g]
        for c in range(3):
            xyz = both[:, 3 * piece + c * n_rows:3 * piece + (c + 1) * n_rows]
            grad_ref[g, c] = (0.25 / 16) * (sums_ref[c] - sums_ref[3] * xyz)

    def grad_groups(keep, step, carry):
        for j in range(together):
            grad_group(step * together + j, keep)
        return carry

    lax.fori_loop(0, kept, functools.partial(grad_groups, True), 0)
    lax.fori_loop(kept, groups // together, functools.partial(grad_groups, False), 0)


def split_ens(n_ens, beads, tiles):
    best = None
    for parts in range(1, n_ens + 1):
        if n_ens % parts or beads % parts or beads % (n_ens // parts):
            continue
        cost = 2 * (beads // parts) + tiles * (beads // (n_ens // parts))
        if best is None or cost < best[0]:
            best = (cost, parts)
    return best[1]


def on_device(coords, counts, segments):
    local_n, _, beads = coords.shape
    n_tile = lax.axis_size("tile")
    n_ens = lax.axis_size("ens")
    structs = local_n * n_ens
    n_p = split_ens(n_ens, beads, n_tile)
    n_q = n_ens // n_p
    n_rows, piece = beads // n_p, beads // n_q
    n_cols = piece * n_tile
    tile, ens = lax.axis_index("tile"), lax.axis_index("ens")
    p, q = lax.rem(ens, n_p), lax.div(ens, n_p)
    vmem = pl.BlockSpec(memory_space=pltpu.VMEM)

    send = pl.pallas_call(
        functools.partial(pack_kernel, n_p, n_q),
        out_shape=jax.ShapeDtypeStruct((n_ens, local_n, 3 * (piece + n_rows)), jnp.float32),
        in_specs=[vmem],
        out_specs=vmem,
        name="pack",
    )(jnp.swapaxes(coords, 0, 1))
    both = lax.all_to_all(send, "ens", 0, 0, tiled=True)

    row_base = tile * beads + p * n_rows
    col_bases = [lax.rem(tile + k, n_tile) * beads + q * piece for k in range(n_tile)]
    own_counts = lax.dynamic_slice_in_dim(counts, p * n_rows, n_rows, 0)
    block = jnp.concatenate([lax.dynamic_slice_in_dim(own_counts, b, piece, 1) for b in col_bases], axis=1)
    seg_cols = jnp.concatenate([lax.dynamic_slice_in_dim(segments, b, piece) for b in col_bases])[None, :]
    col_ids = jnp.concatenate([b + jnp.arange(piece, dtype=jnp.int32) for b in col_bases])[None, :]
    seg_rows = lax.dynamic_slice_in_dim(segments, row_base, n_rows)[:, None]

    full = n_cols // LANES * LANES
    end = n_cols - full
    fold = LANES // end if end and LANES % end == 0 and local_n % (LANES // end) == 0 else 1
    deep = up(n_rows, 16)
    row_wide, col_wide = up(n_rows, LANES), up(n_cols, LANES)
    blocks = structs // fold
    kept = local_n * (TOGETHER if n_ens % TOGETHER == 0 else 1)
    if 4 * kept * deep * (full + LANES) > KEEP_BYTES:
        kept = 0
    masks = pl.pallas_call(
        functools.partial(mask_kernel, fold),
        out_shape=[jax.ShapeDtypeStruct((deep, col_wide), jnp.float32)] * 2,
        in_specs=[pl.BlockSpec(memory_space=pltpu.SMEM)] + [vmem] * 4,
        out_specs=[vmem] * 2,
        compiler_params=pltpu.CompilerParams(vmem_limit_bytes=32 << 20),
        name="masks",
    )(row_base[None], seg_rows, seg_cols, col_ids, block)
    both, masks = lax.optimization_barrier((both, masks))
    own = both[:, :, :3 * piece]
    pieces = [lax.ppermute(own, "tile", [(t, (t - k) % n_tile) for t in range(n_tile)]) for k in range(1, n_tile)]

    lhs, lhs_end = pl.pallas_call(
        functools.partial(row_kernel, n_rows, fold),
        out_shape=[
            jax.ShapeDtypeStruct((structs, deep, 48), jnp.bfloat16),
            jax.ShapeDtypeStruct((blocks, deep, fold * SLOT), jnp.bfloat16),
        ],
        in_specs=[vmem],
        out_specs=[vmem] * 2,
        scratch_shapes=[[pltpu.VMEM((row_wide // LANES, 8 * local_n, LANES), jnp.float32)] * 3],
        compiler_params=pltpu.CompilerParams(vmem_limit_bytes=32 << 20),
        name="rows",
    )(both)
    grad = pl.pallas_call(
        functools.partial(pair_kernel, n_tile, fold, n_rows, n_cols),
        out_shape=jax.ShapeDtypeStruct((n_ens, 3, local_n, n_rows), jnp.float32),
        in_specs=[vmem] * (4 + n_tile),
        out_specs=vmem,
        scratch_shapes=[
            [pltpu.VMEM((col_wide // LANES, 8 * local_n, LANES), jnp.float32)] * 3,
            pltpu.VMEM((structs, 48, full), jnp.bfloat16),
            pltpu.VMEM((blocks, fold * SLOT, LANES), jnp.bfloat16),
            pltpu.VMEM((blocks, fold * 16, LANES), jnp.bfloat16),
            pltpu.VMEM((deep, full), jnp.float32),
            pltpu.VMEM((deep, LANES), jnp.float32),
            pltpu.VMEM((4, local_n, n_rows), jnp.float32),
            pltpu.VMEM((max(kept, 1), deep, full), jnp.float32),
            pltpu.VMEM((max(kept // fold, 1), deep, LANES), jnp.float32),
        ],
        compiler_params=pltpu.CompilerParams(vmem_limit_bytes=40 << 20),
        name="pairs",
    )(*masks, lhs, lhs_end, both, *pieces)

    back = lax.all_to_all(grad, "ens", 0, 0, tiled=True)
    total = pl.pallas_call(
        functools.partial(sum_kernel, n_p, n_q),
        out_shape=jax.ShapeDtypeStruct((3, local_n, beads), jnp.float32),
        in_specs=[vmem],
        out_specs=vmem,
        name="total",
    )(back)
    return jnp.swapaxes(total, 0, 1)


def solution(mesh):
    return jax.shard_map(
        on_device,
        mesh=mesh,
        in_specs=(P("ens", None, "tile"), P("tile", None), P()),
        out_specs=P("ens", None, "tile"),
        check_vma=False,
    )
```

```python
import functools

import jax
import jax.numpy as jnp
from jax import lax
from jax.experimental import pallas as pl
from jax.experimental.pallas import tpu as pltpu
from jax.sharding import PartitionSpec as P

LANES = 128
WIDE = 256
SLOT = 64
TOGETHER = 2
WIDE_STEP = 3
KEEP_BYTES = 24 << 20
NT = (((1,), (1,)), ((), ()))


def up(n, unit):
    return -(-n // unit) * unit


def split3(v):
    hi = v.astype(jnp.bfloat16).astype(jnp.float32)
    rest = v - hi
    mid = rest.astype(jnp.bfloat16).astype(jnp.float32)
    return hi, mid, rest - mid


def pack_kernel(n_p, n_q, xyz_ref, send_ref):
    beads = xyz_ref.shape[2]
    n_rows, piece = beads // n_p, beads // n_q
    for c in range(3):
        for q in range(n_q):
            for p in range(n_p):
                e = q * n_p + p
                send_ref[e, :, pl.ds(c * piece, piece)] = xyz_ref[c, :, pl.ds(q * piece, piece)]
                send_ref[e, :, pl.ds(3 * piece + c * n_rows, n_rows)] = xyz_ref[c, :, pl.ds(p * n_rows, n_rows)]


def sum_kernel(n_p, n_q, back_ref, total_ref):
    n_rows = back_ref.shape[3]
    for c in range(3):
        for p in range(n_p):
            total = back_ref[p, c]
            for q in range(1, n_q):
                total += back_ref[q * n_p + p, c]
            total_ref[c, :, pl.ds(p * n_rows, n_rows)] = total


def put_terms(refs, xyz, norm_row):
    norm = 1.5 - 0.5 * (xyz[0] * xyz[0] + xyz[1] * xyz[1] + xyz[2] * xyz[2])
    n, size = norm.shape
    wide = refs[0].shape[0] * LANES
    for f, v in ((0, xyz[0]), (1, xyz[1]), (2, xyz[2]), (norm_row, norm)):
        if wide > size:
            v = jnp.concatenate([v, jnp.zeros((n, wide - size), jnp.float32)], axis=1)
        for ref, term in zip(refs, split3(v)):
            for k in range(wide // LANES):
                ref[k, pl.ds(f, n, 8), :] = term[:, k * LANES:(k + 1) * LANES]


def get_terms(refs, i):
    return [jnp.concatenate([ref[k, pl.ds(8 * i, 8), :] for k in range(ref.shape[0])], axis=1) for ref in refs]


def init_terms(refs, one_row, per):
    for ref in refs:
        ref[...] = jnp.zeros_like(ref)
    for k in range(refs[0].shape[0]):
        refs[0][k, pl.ds(one_row, per, 8), :] = jnp.ones((per, LANES), jnp.float32)


def row_kernel(n_rows, fold, both_ref, lhs_ref, lhs_end_ref, row_terms):
    groups, per, width = both_ref.shape
    deep = lhs_ref.shape[1]
    first = width - 3 * n_rows
    init_terms(row_terms, 4, per)

    def features(g, carry):
        both = both_ref[g]
        put_terms(row_terms, [both[:, first + c * n_rows:first + (c + 1) * n_rows] for c in range(3)], 3)
        for block in range(per // fold):
            lefts = []
            for inside in range(fold):
                i = block * fold + inside
                hi, mid, lo = get_terms(row_terms, i)
                left = jnp.concatenate([hi, hi, mid, mid, hi, lo], axis=0)
                lhs_ref[g * per + i] = left.T[:deep].astype(jnp.bfloat16)
                lefts += [left, jnp.zeros((SLOT - 48, left.shape[1]), jnp.float32)]
            lhs_end_ref[g * (per // fold) + block] = jnp.concatenate(lefts, axis=0).T[:deep].astype(jnp.bfloat16)
        return carry

    lax.fori_loop(0, groups, features, 0)


def mask_kernel(fold, base_ref, seg_rows_ref, seg_cols_ref, col_ids_ref, counts_ref, mask_ref, goal_ref):
    n_rows, n_cols = counts_ref.shape
    deep = mask_ref.shape[0]
    full = n_cols // LANES * LANES
    end = n_cols - full
    rows = pl.ds(0, n_rows)
    if deep > n_rows:
        for ref in (mask_ref, goal_ref):
            ref[pl.ds(n_rows, deep - n_rows), :] = jnp.zeros((deep - n_rows, ref.shape[1]), jnp.float32)

    def mask_and_goal(start, size):
        count = counts_ref[:, pl.ds(start, size)].astype(jnp.float32)
        row_ids = base_ref[0] + lax.broadcasted_iota(jnp.int32, (n_rows, size), 0)
        mask = jnp.where(seg_rows_ref[...] == seg_cols_ref[:, pl.ds(start, size)], 1.0, 0.3)
        mask = jnp.where(row_ids == col_ids_ref[:, pl.ds(start, size)], 0.0, mask)
        return mask, mask * (count / (count + 8.0))

    for start in range(0, full, LANES):
        mask_ref[rows, pl.ds(start, LANES)], goal_ref[rows, pl.ds(start, LANES)] = mask_and_goal(start, LANES)
    if end:
        def spread(v):
            v = jnp.concatenate([v, jnp.zeros((n_rows, LANES - end), jnp.float32)], axis=1)
            return sum((pltpu.roll(v, k * end, 1) for k in range(1, fold)), v)

        last = pl.ds(full, LANES)
        mask_ref[rows, last], goal_ref[rows, last] = [spread(v) for v in mask_and_goal(full, end)]


def pair_kernel(tiles, fold, n_rows, n_cols, mask_ref, goal_ref, lhs_ref, lhs_end_ref, both_ref, *rest):
    piece_refs = rest[:tiles - 1]
    (grad_ref, col_terms, rhs_ref, rhs_end_ref, terms_end_ref, weight_ref, weight_end_ref, sums_ref,
     kept_ref, kept_end_ref) = rest[tiles - 1:]
    groups, per, _ = both_ref.shape
    structs = groups * per
    piece = n_cols // tiles
    deep = weight_ref.shape[0]
    full = rhs_ref.shape[2]
    end = n_cols - full
    chunks = [(a, min(WIDE, full - a)) for a in range(0, full, WIDE)]

    init_terms(col_terms, 3, per)
    if end:
        rhs_end_ref[...] = jnp.zeros_like(rhs_end_ref)

    def features(g):
        both = both_ref[g]
        parts = [both] + [ref[g] for ref in piece_refs]
        cols = [jnp.concatenate([v[:, c * piece:(c + 1) * piece] for v in parts], axis=1) for c in range(3)]
        put_terms(col_terms, cols, 4)
        for block in range(per // fold):
            for inside in range(fold):
                i = block * fold + inside
                s = g * per + i
                hi, mid, lo = get_terms(col_terms, i)
                right = jnp.concatenate([hi, mid, hi, mid, lo, hi], axis=0)
                rhs_ref[s] = right[:, :full].astype(jnp.bfloat16)
                if end:
                    lane = lax.broadcasted_iota(jnp.int32, (48, LANES), 1)
                    last = jnp.where(lane < end, right[:, full:full + LANES], 0.0)
                    if inside:
                        last = pltpu.roll(last, inside * end, 1)
                    last = last.astype(jnp.bfloat16)
                    b = g * (per // fold) + block
                    rhs_end_ref[b, pl.ds(SLOT * inside, 48), :] = last
                    terms_end_ref[b, pl.ds(16 * inside, 16), :] = last[0:16]

    weight_ref[...] = jnp.zeros_like(weight_ref)
    if end:
        weight_end_ref[...] = jnp.zeros_like(weight_end_ref)

    def tanh_block(s, start, size):
        return jnp.tanh(jnp.dot(lhs_ref[s], rhs_ref[s, :, pl.ds(start, size)], preferred_element_type=jnp.float32))

    def tanh_end(b):
        return jnp.tanh(jnp.dot(lhs_end_ref[b], rhs_end_ref[b], preferred_element_type=jnp.float32))

    def add_some(b, keep):
        for inside in range(0, fold, 2):
            for start, size in chunks:
                t = []
                for i in range(inside, min(inside + 2, fold)):
                    t.append(tanh_block(b * fold + i, start, size))
                    if keep:
                        kept_ref[b * fold + i, :, pl.ds(start, size)] = 1.0 - t[-1] * t[-1]
                weight_ref[:, pl.ds(start, size)] += functools.reduce(jnp.add, t)
        if end:
            t = tanh_end(b)
            if keep:
                kept_end_ref[b] = 1.0 - t * t
            weight_end_ref[...] += t

    together = TOGETHER if groups % TOGETHER == 0 else 1
    per_step = together * (per // fold)
    kept = kept_ref.shape[0] // (per_step * fold)

    first = kept * together
    wide_step = WIDE_STEP if (groups - first) % WIDE_STEP == 0 else together

    def add_groups(keep, start, n, step, carry):
        for j in range(n):
            features(start + step * n + j)
        for j in range(n * (per // fold)):
            add_some((start + step * n) * (per // fold) + j, keep)
        return carry

    lax.fori_loop(0, kept, functools.partial(add_groups, True, 0, together), 0)
    lax.fori_loop(0, (groups - first) // wide_step, functools.partial(add_groups, False, first, wide_step), 0)

    scale = 0.5 / structs
    for start, size in chunks:
        cut = pl.ds(start, size)
        weight_ref[:, cut] = mask_ref[:, cut] * (0.5 + scale * weight_ref[:, cut]) - goal_ref[:, cut]
    if end:
        part = weight_end_ref[...]
        total = sum((pltpu.roll(part, k * end, 1) for k in range(1, fold)), part)
        last = pl.ds(full, LANES)
        weight_end_ref[...] = mask_ref[:, last] * (0.5 + scale * total) - goal_ref[:, last]

    def slope(t):
        return 1.0 - t * t

    def split2(weight, slopes):
        g = weight * slopes
        hi = g.astype(jnp.bfloat16)
        return [hi, (g - hi.astype(jnp.float32)).astype(jnp.bfloat16)]

    def sums(terms, parts):
        hi, lo = [jnp.concatenate(v, axis=1) for v in zip(*parts)]
        return (lax.dot_general(hi, terms, NT, preferred_element_type=jnp.float32).T
                + lax.dot_general(terms, lo, NT, preferred_element_type=jnp.float32))

    def grad_group(g, keep):
        for block in range(per // fold):
            b = g * (per // fold) + block
            if end:
                slopes = kept_end_ref[b] if keep else slope(tanh_end(b))
                last = sums(terms_end_ref[b], [split2(weight_end_ref[...], slopes)])
            for inside in range(fold):
                s = b * fold + inside
                parts = []
                for start, size in chunks:
                    cut = pl.ds(start, size)
                    slopes = kept_ref[s, :, cut] if keep else slope(tanh_block(s, start, size))
                    parts.append(split2(weight_ref[:, cut], slopes))
                total = sums(rhs_ref[s, pl.ds(0, 16), :], parts)
                if end:
                    total += last[16 * inside:16 * inside + 16]
                total = total[:, :n_rows]
                mixed = total[0:3] + total[8:11]
                i = block * fold + inside
                for c in range(3):
                    sums_ref[c, pl.ds(i, 1), :] = mixed[c:c + 1]
                sums_ref[3, pl.ds(i, 1), :] = total[3:4]
        both = both_ref[g]
        for c in range(3):
            xyz = both[:, 3 * piece + c * n_rows:3 * piece + (c + 1) * n_rows]
            grad_ref[g, c] = (0.25 / 16) * (sums_ref[c] - sums_ref[3] * xyz)

    def grad_groups(keep, start, n, step, carry):
        for j in range(n):
            grad_group(start + step * n + j, keep)
        return carry

    lax.fori_loop(0, kept, functools.partial(grad_groups, True, 0, together), 0)
    lax.fori_loop(0, (groups - first) // wide_step, functools.partial(grad_groups, False, first, wide_step), 0)


def split_ens(n_ens, beads, tiles):
    best = None
    for parts in range(1, n_ens + 1):
        if n_ens % parts or beads % parts or beads % (n_ens // parts):
            continue
        cost = 2 * (beads // parts) + tiles * (beads // (n_ens // parts))
        if best is None or cost < best[0]:
            best = (cost, parts)
    return best[1]


def on_device(coords, counts, segments):
    local_n, _, beads = coords.shape
    n_tile = lax.axis_size("tile")
    n_ens = lax.axis_size("ens")
    structs = local_n * n_ens
    n_p = split_ens(n_ens, beads, n_tile)
    n_q = n_ens // n_p
    n_rows, piece = beads // n_p, beads // n_q
    n_cols = piece * n_tile
    tile, ens = lax.axis_index("tile"), lax.axis_index("ens")
    p, q = lax.rem(ens, n_p), lax.div(ens, n_p)
    vmem = pl.BlockSpec(memory_space=pltpu.VMEM)

    send = pl.pallas_call(
        functools.partial(pack_kernel, n_p, n_q),
        out_shape=jax.ShapeDtypeStruct((n_ens, local_n, 3 * (piece + n_rows)), jnp.float32),
        in_specs=[vmem],
        out_specs=vmem,
        name="pack",
    )(jnp.swapaxes(coords, 0, 1))
    both = lax.all_to_all(send, "ens", 0, 0, tiled=True)

    row_base = tile * beads + p * n_rows
    col_bases = [lax.rem(tile + k, n_tile) * beads + q * piece for k in range(n_tile)]
    own_counts = lax.dynamic_slice_in_dim(counts, p * n_rows, n_rows, 0)
    block = jnp.concatenate([lax.dynamic_slice_in_dim(own_counts, b, piece, 1) for b in col_bases], axis=1)
    seg_cols = jnp.concatenate([lax.dynamic_slice_in_dim(segments, b, piece) for b in col_bases])[None, :]
    col_ids = jnp.concatenate([b + jnp.arange(piece, dtype=jnp.int32) for b in col_bases])[None, :]
    seg_rows = lax.dynamic_slice_in_dim(segments, row_base, n_rows)[:, None]

    full = n_cols // LANES * LANES
    end = n_cols - full
    fold = LANES // end if end and LANES % end == 0 and local_n % (LANES // end) == 0 else 1
    deep = up(n_rows, 16)
    row_wide, col_wide = up(n_rows, LANES), up(n_cols, LANES)
    blocks = structs // fold
    kept = local_n * (TOGETHER if n_ens % TOGETHER == 0 else 1)
    if 4 * kept * deep * (full + LANES) > KEEP_BYTES:
        kept = 0
    masks = pl.pallas_call(
        functools.partial(mask_kernel, fold),
        out_shape=[jax.ShapeDtypeStruct((deep, col_wide), jnp.float32)] * 2,
        in_specs=[pl.BlockSpec(memory_space=pltpu.SMEM)] + [vmem] * 4,
        out_specs=[vmem] * 2,
        compiler_params=pltpu.CompilerParams(vmem_limit_bytes=32 << 20),
        name="masks",
    )(row_base[None], seg_rows, seg_cols, col_ids, block)
    both, masks = lax.optimization_barrier((both, masks))
    own = both[:, :, :3 * piece]
    pieces = [lax.ppermute(own, "tile", [(t, (t - k) % n_tile) for t in range(n_tile)]) for k in range(1, n_tile)]

    lhs, lhs_end = pl.pallas_call(
        functools.partial(row_kernel, n_rows, fold),
        out_shape=[
            jax.ShapeDtypeStruct((structs, deep, 48), jnp.bfloat16),
            jax.ShapeDtypeStruct((blocks, deep, fold * SLOT), jnp.bfloat16),
        ],
        in_specs=[vmem],
        out_specs=[vmem] * 2,
        scratch_shapes=[[pltpu.VMEM((row_wide // LANES, 8 * local_n, LANES), jnp.float32)] * 3],
        compiler_params=pltpu.CompilerParams(vmem_limit_bytes=32 << 20),
        name="rows",
    )(both)
    grad = pl.pallas_call(
        functools.partial(pair_kernel, n_tile, fold, n_rows, n_cols),
        out_shape=jax.ShapeDtypeStruct((n_ens, 3, local_n, n_rows), jnp.float32),
        in_specs=[vmem] * (4 + n_tile),
        out_specs=vmem,
        scratch_shapes=[
            [pltpu.VMEM((col_wide // LANES, 8 * local_n, LANES), jnp.float32)] * 3,
            pltpu.VMEM((structs, 48, full), jnp.bfloat16),
            pltpu.VMEM((blocks, fold * SLOT, LANES), jnp.bfloat16),
            pltpu.VMEM((blocks, fold * 16, LANES), jnp.bfloat16),
            pltpu.VMEM((deep, full), jnp.float32),
            pltpu.VMEM((deep, LANES), jnp.float32),
            pltpu.VMEM((4, local_n, n_rows), jnp.float32),
            pltpu.VMEM((max(kept, 1), deep, full), jnp.float32),
            pltpu.VMEM((max(kept // fold, 1), deep, LANES), jnp.float32),
        ],
        compiler_params=pltpu.CompilerParams(vmem_limit_bytes=40 << 20),
        name="pairs",
    )(*masks, lhs, lhs_end, both, *pieces)

    back = lax.all_to_all(grad, "ens", 0, 0, tiled=True)
    total = pl.pallas_call(
        functools.partial(sum_kernel, n_p, n_q),
        out_shape=jax.ShapeDtypeStruct((3, local_n, beads), jnp.float32),
        in_specs=[vmem],
        out_specs=vmem,
        name="total",
    )(back)
    return jnp.swapaxes(total, 0, 1)


def solution(mesh):
    return jax.shard_map(
        on_device,
        mesh=mesh,
        in_specs=(P("ens", None, "tile"), P("tile", None), P()),
        out_specs=P("ens", None, "tile"),
        check_vma=False,
    )
```
